32 devices in a mesh: fsdp: 2 (over core), ctx: 4 (over z), tp: 4 (over y, x).
Axes of the slice: x: 2, y: 2, z: 4, core: 2. Of those that a mesh axis runs over, the one named last changes fastest.
Arguments:
- tokens: bfloat16 [4096, 2048], P(('fsdp', 'ctx')), may hold values from -6 to 6
- seq_bounds: int32 [2, 3], P('fsdp'), may hold values from 0 to 2048, as said below
- w_query: bfloat16 [2048, 2048], P('fsdp', 'tp'), may hold values from -0.125 to 0.125
- w_key: bfloat16 [2048, 2048], P('fsdp', 'tp'), may hold values from -0.125 to 0.125
- w_value: bfloat16 [2048, 2048], P('fsdp', 'tp'), may hold values from -0.125 to 0.125
- w_beta: bfloat16 [2048, 16], P('fsdp', 'tp'), may hold values from -0.125 to 0.125
- conv_taps: float32 [3, 4, 2048], P(None, None, 'tp'), may hold values from -3 to 3
- out_gain: float32 [128], replicated, may hold values from 0.1 to 1.9
- w_out: bfloat16 [2048, 2048], P('fsdp', 'tp'), may hold values from -0.125 to 0.125
- attn_gain: float32 [2048], replicated, may hold values from 0.1 to 1.9
- ffn_gain: float32 [2048], replicated, may hold values from 0.1 to 1.9
- w_gate: bfloat16 [2048, 5632], P('fsdp', 'tp'), may hold values from -0.125 to 0.125
- w_up: bfloat16 [2048, 5632], P('fsdp', 'tp'), may hold values from -0.125 to 0.125
- w_down: bfloat16 [2048, 5632], P('fsdp', 'tp'), may hold values from -0.078125 to 0.078125
- cotangent: bfloat16 [4096, 2048], P(('fsdp', 'ctx')), may hold values from -6 to 6
Outputs:
- out: bfloat16 [4096, 2048], P(('fsdp', 'ctx'))
- d_tokens: bfloat16 [4096, 2048], P(('fsdp', 'ctx'))
- d_w_query: float32 [2048, 2048], P(('fsdp', 'ctx'), 'tp')
- d_w_key: float32 [2048, 2048], P(('fsdp', 'ctx'), 'tp')
- d_w_value: float32 [2048, 2048], P(('fsdp', 'ctx'), 'tp')
- d_w_beta: float32 [2048, 16], P(('fsdp', 'ctx'), 'tp')
- d_conv_taps: float32 [3, 4, 2048], P(None, None, 'tp')
- d_out_gain: float32 [128], replicated
- d_w_out: float32 [2048, 2048], P(('fsdp', 'ctx'), 'tp')
- d_attn_gain: float32 [2048], replicated
- d_ffn_gain: float32 [2048], replicated
- d_w_gate: float32 [2048, 5632], P(('fsdp', 'ctx'), 'tp')
- d_w_up: float32 [2048, 5632], P(('fsdp', 'ctx'), 'tp')
- d_w_down: float32 [2048, 5632], P(('fsdp', 'ctx'), 'tp')
The draws below stay inside these ranges and needn't reach their ends.
Inputs may be any that keep to these rules, and one draw needn't show every extreme that they name: `seq_bounds`: row t holds e0 <= e1 < e2 for stream t, with e0 < 256 and 1664 <= e1 <= 1920; in every draw some stream has e2 = 2048 and some stream has e0 = 0.
All inputs are finite; a program needn't handle non-finite values.
Results may differ from the reference program's by a relative error of at most 0.023.
Values may be sent and summed in bfloat16 or wider, within the bound.
No kernel may reach another device: no remote copies, remote signals or barrier semaphores. Data moves between devices by JAX's collectives and lax.ppermute only.
A program may use at most 192 MiB of HBM per device.

```python
import math
import jax
import jax.numpy as jnp
from jax import lax

D = 2048
H = 16
DH = 128
FF = 5632
TAPS = 4
GROUP = 64
TOK_DEV = 512
HD = 2048
SEQ = 2048
TOKENS = 4096
N_FSDP = 2


def draw_seq_bounds(key, part):
    key = jax.random.fold_in(key, 7)
    keys = jax.random.split(key, 5)
    lead_end = jax.random.randint(keys[0], (N_FSDP,), 0, TOK_DEV // 2)
    span_end = jax.random.randint(keys[1], (N_FSDP,), SEQ - 3 * TOK_DEV // 4, SEQ - TOK_DEV // 4 + 1)
    trail_end = span_end + jax.random.randint(keys[2], (N_FSDP,), 1, TOK_DEV // 4 + 1)
    full_stream = jax.random.randint(keys[3], (), 0, N_FSDP)
    open_stream = jax.random.randint(keys[4], (), 0, N_FSDP)
    streams = jnp.arange(N_FSDP)
    trail_end = jnp.where(streams == full_stream, SEQ, trail_end)
    lead_end = jnp.where(streams == open_stream, 0, lead_end)
    return jnp.stack([lead_end, span_end, trail_end], axis=1).astype(jnp.int32)


def spiked(values, key, source, target, blocks, factor):
    def block_of(position):
        return (jnp.arange(values.shape[position]) // (values.shape[position] // blocks)).reshape((-1,) + (1,) * (values.ndim - 1 - position))

    first = jax.random.permutation(key, blocks)[block_of(target)]
    other_side = (block_of(target) + blocks // 2) % blocks
    return jnp.where((block_of(source) == first) | (block_of(source) == other_side), factor * values, values)


def shard_levels(stream_key, shape, cuts, low, top_value):
    loudness, own = 1.0, jax.random.fold_in(stream_key, 6)
    for axis_at, parts in cuts:
        heights = jnp.exp(jax.random.uniform(jax.random.fold_in(own, axis_at), (parts,), jnp.float32, low / len(cuts), top_value / len(cuts)))
        loudness = loudness * jnp.repeat(heights, shape[axis_at] // parts).reshape([-1 if axis == axis_at else 1 for axis in range(len(shape))])
    return loudness


def normal_values(stream_key, extent, scale, reach, shards=(), kind=jnp.bfloat16):
    factor_of = shard_levels(stream_key, extent, shards, -0.22, 0.18) if shards else 1.0
    entries = jax.random.normal(stream_key, extent, jnp.float32) * scale * factor_of
    return jnp.minimum(jnp.maximum(entries, -reach), reach).astype(kind)


def bell_draw_with(key, extent, width, most, shards, heavy, kind=jnp.bfloat16):
    array = width * jax.random.normal(key, extent, jnp.float32)
    if shards:
        array = array * shard_levels(key, extent, shards, -0.22, 0.18)
    return jnp.clip(spiked(array, jax.random.fold_in(key, 3), *heavy), -most, most).astype(kind)


def setup_inputs(seed: int = 0) -> dict:
    key_list = jax.random.split(jax.random.key(seed), 16)
    return {
        "tokens": normal_values(key_list[0], (TOKENS, D), 1.0, 6.0, ((0, 8),)),
        "seq_bounds": draw_seq_bounds(jax.random.fold_in(key_list[15], 71), 0),
        "w_query": normal_values(key_list[2], (D, HD), D ** -0.5, 0.125, ((0, 2), (1, 4))),
        "w_key": normal_values(key_list[3], (D, HD), D ** -0.5, 0.125, ((0, 2), (1, 4))),
        "w_value": normal_values(key_list[4], (D, HD), D ** -0.5, 0.125, ((0, 2), (1, 4))),
        "w_beta": normal_values(key_list[5], (D, H), D ** -0.5, 0.125, ((0, 2), (1, 4))),
        "conv_taps": normal_values(key_list[6], (3, TAPS, HD), 0.5, 3.0, ((2, 4),), jnp.float32),
        "out_gain": jnp.clip(1.0 + 0.18 * jax.random.normal(key_list[7], (DH,), jnp.float32), 0.1, 1.9),
        "w_out": normal_values(key_list[8], (D, HD), HD ** -0.5, 0.125, ((0, 2), (1, 4))),
        "attn_gain": jnp.clip(1.0 + 0.18 * jax.random.normal(key_list[9], (D,), jnp.float32), 0.1, 1.9),
        "ffn_gain": jnp.clip(1.0 + 0.18 * jax.random.normal(key_list[10], (D,), jnp.float32), 0.1, 1.9),
        "w_gate": normal_values(key_list[11], (D, FF), D ** -0.5, 0.125, ((0, 2), (1, 4))),
        "w_up": normal_values(key_list[12], (D, FF), D ** -0.5, 0.125, ((0, 2), (1, 4))),
        "w_down": normal_values(key_list[13], (D, FF), FF ** -0.5, 0.078125, ((0, 2), (1, 4))),
        "cotangent": bell_draw_with(key_list[14], (TOKENS, D), 1.0, 6.0, ((0, 8),), (0, 1, 8, 2.0)),
    }


EPS = 1e-06
HIGH = lax.Precision.HIGHEST

@jax.custom_vjp
def low(v):
    return lax.optimization_barrier(v.astype(jnp.bfloat16)).astype(jnp.float32)

@jax.custom_vjp
def low_back(v):
    return v

def low_keep(v):
    return (low(v), None)

def low_pass(kept, grad):
    return (grad,)

def back_keep(v):
    return (v, None)

def back_low(kept, grad):
    return (low(grad),)
low.defvjp(low_keep, low_pass)
low_back.defvjp(back_keep, back_low)

def matmul(left_side, right_side):
    return jnp.dot(left_side.astype(jnp.float32), right_side.astype(jnp.float32), precision=HIGH, preferred_element_type=jnp.float32)

def rms_norm(values, gain):
    return values * lax.rsqrt(lax.optimization_barrier(jnp.mean(values * values, axis=-1, keepdims=True)) + EPS) * gain

def unit_rows(values):
    return values * lax.rsqrt(lax.optimization_barrier(jnp.sum(values * values, axis=-1, keepdims=True)) + EPS)

def segment_ids(places, bounds):
    ids = jnp.zeros(places.shape, jnp.int32)
    for index in range(3):
        ids = ids + (places >= bounds[..., index:index + 1]).astype(jnp.int32)
    return jnp.where(places < 0, jnp.int32(-1), ids)

def group_step(state, block):
    queries, keys_unit, values, strength, seg_block, prev_id = block
    same = (seg_block[:, None] == seg_block[None, :]).astype(jnp.float32)
    carry_in = (seg_block == prev_id).astype(jnp.float32)
    tail = (seg_block == seg_block[-1]).astype(jnp.float32)
    whole = (seg_block[-1] == prev_id).astype(jnp.float32)
    scaled = keys_unit * strength[:, None]
    gram = matmul(scaled, keys_unit.T) * same
    system = jnp.eye(GROUP, dtype=jnp.float32) + jnp.tril(gram, -1)
    right_hand = jnp.concatenate([scaled, values * strength[:, None]], axis=1)
    solved = jax.scipy.linalg.solve_triangular(system, right_hand, lower=True, unit_diagonal=True)
    erase = solved[:, :DH]
    write = solved[:, DH:]
    fresh = write - carry_in[:, None] * matmul(erase, state)
    scores = jnp.tril(matmul(queries, keys_unit.T) * same)
    output = carry_in[:, None] * matmul(queries, state) + matmul(scores, fresh)
    return (whole * state + matmul(keys_unit.T, tail[:, None] * fresh), output)

def delta_head(queries, keys_unit, values, strength, seg_row, prev_row):
    blocks = (queries.reshape(-1, GROUP, DH), keys_unit.reshape(-1, GROUP, DH), values.reshape(-1, GROUP, DH), strength.reshape(-1, GROUP), seg_row.reshape(-1, GROUP), prev_row)
    start_state = jnp.zeros((DH, DH), jnp.float32)
    final_state, outputs = lax.scan(jax.checkpoint(group_step), start_state, blocks)
    return outputs.reshape(-1, DH)

def make_layer(mask, seg, prev):

    def layer(hidden_in, query_weight, key_weight, value_weight, beta_weight, taps_all, head_gain, out_weight, first_gain, second_gain, gate_weight, up_weight, down_weight):
        normed = low(rms_norm(hidden_in, first_gain))
        projected = low_back(matmul(normed, jnp.concatenate([query_weight, key_weight, value_weight], axis=1)))
        strength = jax.nn.sigmoid(low_back(matmul(normed, beta_weight))) * mask[:, None]
        streams = jnp.pad(projected.reshape(N_FSDP, SEQ, 3 * HD), ((0, 0), (TAPS - 1, 0), (0, 0)))
        seg_pad = jnp.concatenate([jnp.full((N_FSDP, TAPS - 1), -1, jnp.int32), seg], axis=1)
        kernel = jnp.concatenate([taps_all[0], taps_all[1], taps_all[2]], axis=1)
        mixed = jnp.zeros((N_FSDP, SEQ, 3 * HD), jnp.float32)
        for tap_index in range(TAPS):
            offset = TAPS - 1 - tap_index
            same_tap = (seg_pad[:, offset:offset + SEQ] == seg).astype(jnp.float32)[..., None]
            mixed = mixed + kernel[tap_index] * streams[:, offset:offset + SEQ] * same_tap
        mixed = jax.nn.silu(mixed)
        queries = unit_rows(mixed[..., :HD].reshape(N_FSDP, SEQ, H, DH)) * (1.0 / math.sqrt(DH))
        keys_unit = unit_rows(mixed[..., HD:2 * HD].reshape(N_FSDP, SEQ, H, DH))
        values = mixed[..., 2 * HD:].reshape(N_FSDP, SEQ, H, DH)
        gates = strength.reshape(N_FSDP, SEQ, H).transpose(0, 2, 1)
        per_head = jax.vmap(delta_head, in_axes=(0, 0, 0, 0, None, None))
        heads_out = jax.vmap(per_head)(queries.transpose(0, 2, 1, 3), keys_unit.transpose(0, 2, 1, 3), values.transpose(0, 2, 1, 3), gates, seg, prev)
        heads_out = heads_out.transpose(0, 2, 1, 3)
        normed_heads = low(rms_norm(heads_out, head_gain)).reshape(TOKENS, HD)
        attended = low_back(matmul(normed_heads, out_weight.T))
        hidden = hidden_in + attended
        normed_two = low(rms_norm(hidden, second_gain))
        gate = low_back(matmul(normed_two, gate_weight))
        up_proj = low_back(matmul(normed_two, up_weight))
        act = low(jax.nn.silu(gate) * up_proj)
        return hidden + low_back(matmul(act, down_weight.T))
    return layer

def reference(tokens, seq_bounds, w_query, w_key, w_value, w_beta, conv_taps, out_gain, w_out, attn_gain, ffn_gain, w_gate, w_up, w_down, cotangent):
    bounds = seq_bounds.astype(jnp.int32)
    positions = jnp.broadcast_to(jnp.arange(SEQ, dtype=jnp.int32)[None, :], (N_FSDP, SEQ))
    seg = segment_ids(positions, bounds)
    before = jnp.broadcast_to((jnp.arange(SEQ // GROUP, dtype=jnp.int32) * GROUP - 1)[None, :], (N_FSDP, SEQ // GROUP))
    prev = segment_ids(before, bounds)
    mask = (positions < bounds[:, 2:3]).astype(jnp.float32).reshape(TOKENS)
    params = (tokens.astype(jnp.float32), w_query.astype(jnp.float32), w_key.astype(jnp.float32), w_value.astype(jnp.float32), w_beta.astype(jnp.float32), conv_taps.astype(jnp.float32), out_gain.astype(jnp.float32), w_out.astype(jnp.float32), attn_gain.astype(jnp.float32), ffn_gain.astype(jnp.float32), w_gate.astype(jnp.float32), w_up.astype(jnp.float32), w_down.astype(jnp.float32))
    result, pullback = jax.vjp(make_layer(mask, seg, prev), *params)
    grads = pullback(cotangent.astype(jnp.float32) * mask[:, None])
    return (result.astype(jnp.bfloat16), grads[0].astype(jnp.bfloat16), grads[1], grads[2], grads[3], grads[4], grads[5], grads[6], grads[7], grads[8], grads[9], grads[10], grads[11], grads[12])
```

```python
import functools
import math

import jax
import jax.numpy as jnp
from jax import lax
from jax.experimental import pallas as pl
from jax.experimental.pallas import tpu as pltpu
from jax.sharding import PartitionSpec as P

EPS = 1e-06
HIGH = lax.Precision.HIGHEST
F32 = jnp.float32
BF16 = jnp.bfloat16
CHUNK = 128
RIM = 16
TAPS = 4
VMEM = pltpu.VMEM
WHOLE = pl.BlockSpec(memory_space=pltpu.VMEM)
SCALARS = pl.BlockSpec(memory_space=pltpu.SMEM)


def dot_nn(left, right, precision=None):
    return lax.dot_general(
        left, right, (((1,), (0,)), ((), ())), precision=precision, preferred_element_type=F32
    )


def dot_nt(left, right, precision=None):
    return lax.dot_general(
        left, right, (((1,), (1,)), ((), ())), precision=precision, preferred_element_type=F32
    )


def dot_tn(left, right, precision=None):
    return lax.dot_general(
        left, right, (((0,), (0,)), ((), ())), precision=precision, preferred_element_type=F32
    )


def call(kernel, out_shape, operands, flops=0, scratch=(), grid=None, in_specs=None, out_specs=None):
    size = sum(math.prod(x.shape) * x.dtype.itemsize for x in operands)
    outs = out_shape if isinstance(out_shape, (list, tuple)) else [out_shape]
    size += sum(math.prod(x.shape) * x.dtype.itemsize for x in outs)
    extra = {} if grid is None else {"grid": grid}
    return pl.pallas_call(
        kernel,
        out_shape=out_shape,
        in_specs=in_specs or [SCALARS] + [WHOLE] * (len(operands) - 1),
        out_specs=out_specs or (type(out_shape)([WHOLE] * len(outs)) if isinstance(out_shape, (list, tuple)) else WHOLE),
        scratch_shapes=list(scratch),
        cost_estimate=pl.CostEstimate(flops=flops, bytes_accessed=size, transcendentals=0),
        compiler_params=pltpu.CompilerParams(vmem_limit_bytes=58 << 20),
        **extra,
    )(*operands)


def shape(*dims, dtype=F32):
    return jax.ShapeDtypeStruct(dims, dtype)


def seg_of(places, meta):
    ids = (
        (places >= meta[0]).astype(jnp.int32)
        + (places >= meta[1]).astype(jnp.int32)
        + (places >= meta[2]).astype(jnp.int32)
    )
    return jnp.where(places < 0, -1, ids)


def row_of(meta, slot, rows):
    return pl.ds(pl.multiple_of(meta[6 + slot], rows), rows)


def halves(meta, half):
    return (
        pl.ds(pl.multiple_of(meta[4], half), half),
        pl.ds(pl.multiple_of(meta[5], half), half),
    )


def project_kernel(meta, tok, rim, gain, wq, wk, wv, wb, xq, xk, xv, xb, normed, proj, logits, ext):
    rows, width = tok.shape
    for source, at, count in ((rim, 0, RIM), (tok, RIM, rows)):
        values = source[...].astype(F32)
        scale = lax.rsqrt(jnp.mean(values * values, axis=-1, keepdims=True) + EPS)
        ext[pl.ds(at, count), :] = (values * scale * gain[...]).astype(BF16)
    normed[...] = ext[pl.ds(RIM, rows), :]
    own, oth = halves(meta, width // 2)
    left, right = ext[:, own], ext[:, oth]
    chan = wq.shape[1]
    for at, (a, b) in enumerate(((wq, xq), (wk, xk), (wv, xv))):
        proj[:, at * chan : (at + 1) * chan] = dot_nn(left, a[...]) + dot_nn(right, b[...])
    logits[...] = dot_nn(left[RIM:], wb[...]) + dot_nn(right[RIM:], xb[...])


def conv_rows(ext, taps, rows, sames):
    mixed = None
    for j in range(TAPS):
        term = taps[j : j + 1, :] * ext[RIM - j : RIM - j + rows, :] * sames[j]
        mixed = term if mixed is None else mixed + term
    return mixed


def tap_masks(meta, rows):
    places = meta[3] + lax.broadcasted_iota(jnp.int32, (rows, 1), 0)
    seg = seg_of(places, meta)
    return places, [(seg_of(places - j, meta) == seg).astype(F32) for j in range(TAPS)]


def pick_column(values, head):
    lane = lax.broadcasted_iota(jnp.int32, values.shape, 1)
    return jnp.sum(jnp.where(lane == head, values, 0.0), axis=1, keepdims=True)


def chunk_masks(meta, at):
    first = meta[3] + at * CHUNK
    row = lax.broadcasted_iota(jnp.int32, (CHUNK, CHUNK), 0)
    col = lax.broadcasted_iota(jnp.int32, (CHUNK, CHUNK), 1)
    seg_col = seg_of(first + lax.broadcasted_iota(jnp.int32, (CHUNK, 1), 0), meta)
    seg_row = seg_of(first + lax.broadcasted_iota(jnp.int32, (1, CHUNK), 1), meta)
    before = seg_of(first - 1, meta)
    last = seg_of(first + CHUNK - 1, meta)
    same = (seg_col == seg_row).astype(F32)
    strict = jnp.where(row > col, same, 0.0)
    lower = jnp.where(row >= col, same, 0.0)
    carry_in = (seg_col == before).astype(F32)
    tail = (seg_col == last).astype(F32)
    whole = (last == before).astype(F32)
    return strict, lower, carry_in, tail, whole


def unit_inverse(gram):
    row = lax.broadcasted_iota(jnp.int32, (CHUNK, CHUNK), 0)
    col = lax.broadcasted_iota(jnp.int32, (CHUNK, CHUNK), 1)
    eye = (row == col).astype(F32)
    size = 8
    near = jnp.where(row // size == col // size, gram, 0.0)
    inverse = eye - near
    power = dot_nn(near, near, HIGH)
    inverse = inverse + dot_nn(inverse, power, HIGH)
    power = dot_nn(power, power, HIGH)
    inverse = inverse + dot_nn(inverse, power, HIGH)
    while size < CHUNK:
        off = (row // (2 * size) == col // (2 * size)) & (row // size != col // size)
        inverse = inverse - dot_nn(inverse, dot_nn(jnp.where(off, gram, 0.0), inverse, HIGH), HIGH)
        size *= 2
    return inverse


def silu_parts(mixed):
    sig = jax.nn.sigmoid(mixed)
    return sig, mixed * sig


def unit_parts(values):
    scale = lax.rsqrt(jnp.sum(values * values, axis=-1, keepdims=True) + EPS)
    return scale, values * scale


def delta_kernel(
    meta, eq, ek, ev, tq, tk, tv, logits,
    w_out, u_out, p_out, t_out, qe_out, m_out, mp_out, bp_out, qh_out, oh_out, mtot, btot,
):
    rows, width = w_out.shape[1:]
    head = pl.program_id(0)
    places, sames = tap_masks(meta, rows)
    q = silu_parts(conv_rows(eq, tq[0], rows, sames))[1]
    k = silu_parts(conv_rows(ek, tk[0], rows, sames))[1]
    v = silu_parts(conv_rows(ev, tv[0], rows, sames))[1]
    q = unit_parts(q)[1] * (1.0 / math.sqrt(width))
    k = unit_parts(k)[1]
    strength = jax.nn.sigmoid(pick_column(logits[...], head)) * (places < meta[2]).astype(F32)
    eye = (
        lax.broadcasted_iota(jnp.int32, (width, width), 0)
        == lax.broadcasted_iota(jnp.int32, (width, width), 1)
    ).astype(F32)
    parts = []
    for at in range(rows // CHUNK):
        here = slice(at * CHUNK, (at + 1) * CHUNK)
        strict, lower, carry_in, tail, whole = chunk_masks(meta, at)
        qc, kc, vc, bc = q[here], k[here], v[here], strength[here]
        scaled = bc * kc
        gram = dot_nt(scaled, kc, HIGH) * strict
        scores = dot_nt(qc, kc, HIGH) * lower
        inverse = unit_inverse(gram)
        both = dot_nn(inverse, jnp.concatenate([scaled, bc * vc], axis=1), HIGH)
        erase, write = both[:, :width], both[:, width:]
        carried = carry_in * erase
        state = dot_tn(kc, tail * jnp.concatenate([carried, write], axis=1), HIGH)
        step = whole * eye - state[:, :width]
        reach = dot_nn(scores, jnp.concatenate([carried, write], axis=1), HIGH)
        query = carry_in * qc - reach[:, :width]
        w_out[0, here, :] = erase
        u_out[0, here, :] = write
        p_out[0, here, :] = scores
        t_out[0, here, :] = inverse
        qe_out[0, here, :] = query
        m_out[0, here, :] = step
        parts.append((query, step, reach[:, width:], state[:, width:]))
    prefix, added = eye, jnp.zeros((width, width), F32)
    for at, (query, step, local, extra) in enumerate(parts):
        here = slice(at * CHUNK, (at + 1) * CHUNK)
        mp_out[0, here, :] = prefix
        bp_out[0, here, :] = added
        both = dot_nn(
            jnp.concatenate([query, step], axis=0), jnp.concatenate([prefix, added], axis=1), HIGH
        )
        qh_out[0, here, :] = both[:CHUNK, :width]
        oh_out[0, here, :] = both[:CHUNK, width:] + local
        prefix, added = both[CHUNK:, :width], both[CHUNK:, width:] + extra
    mtot[0] = prefix
    btot[0] = added


def hop_kernel(step, extra, state, out, *, flip):
    for head in range(step.shape[0]):
        value = state[head].astype(F32)
        product = dot_tn(step[head], value, HIGH) if flip else dot_nn(step[head], value, HIGH)
        out[head] = (product + extra[head]).astype(BF16)


def attend_kernel(meta, qh, oh, state, gain, w_own, w_oth, heads_slot, o_out, *rest):
    pieces, low = rest[:-1], rest[-1]
    heads, rows, width = qh.shape
    for head in range(heads):
        out = dot_nn(qh[head], state[head].astype(F32), HIGH) + oh[head]
        o_out[head] = out
        scale = lax.rsqrt(jnp.mean(out * out, axis=-1, keepdims=True) + EPS)
        low[:, head * width : (head + 1) * width] = (out * scale * gain[...]).astype(BF16)
    count = rows // len(pieces)
    own, oth = halves(meta, w_own.shape[0])
    for slot, piece in enumerate(pieces):
        part = low[row_of(meta, slot, count), :]
        heads_slot[pl.ds(slot * count, count), :] = part
        piece[:, own] = dot_nt(part, w_own[...]).astype(BF16)
        piece[:, oth] = dot_nt(part, w_oth[...]).astype(BF16)


def norm_two_kernel(a, b, c, d, tok, gain, hidden_out, normed_out):
    total = a[...].astype(F32) + b[...].astype(F32) + c[...].astype(F32) + d[...].astype(F32)
    hidden = tok[...].astype(F32) + total
    scale = lax.rsqrt(jnp.mean(hidden * hidden, axis=-1, keepdims=True) + EPS)
    hidden_out[...] = hidden
    normed_out[...] = (hidden * scale * gain[...]).astype(BF16)


def norm_back(grad, values, gain):
    scale = lax.rsqrt(jnp.mean(values * values, axis=-1, keepdims=True) + EPS)
    normal = values * scale
    hat = grad * gain
    back = scale * (hat - normal * jnp.mean(hat * normal, axis=-1, keepdims=True))
    return back, jnp.sum(grad * normal, axis=0, keepdims=True)


def norm_two_back_kernel(meta, a, b, c, d, hidden, cot, gain, grad_hidden, grad_att, d_gain):
    total = a[...].astype(F32) + b[...].astype(F32) + c[...].astype(F32) + d[...].astype(F32)
    back, d_gain[...] = norm_back(total, hidden[...], gain[...])
    places = meta[3] + meta[6] + lax.broadcasted_iota(jnp.int32, (hidden.shape[0], 1), 0)
    grad = cot[...].astype(F32) * (places < meta[2]).astype(F32) + back
    grad_hidden[...] = grad
    grad_att[...] = grad.astype(BF16)


def norm_one_back_kernel(a, b, c, d, tok, gain, grad_hidden, d_tok, d_gain):
    total = a[...].astype(F32) + b[...].astype(F32) + c[...].astype(F32) + d[...].astype(F32)
    back, d_gain[...] = norm_back(total, tok[...].astype(F32), gain[...])
    d_tok[...] = (grad_hidden[...] + back).astype(BF16)


def place_kernel(meta, a, b, c, d, out):
    rows = a.shape[0]
    for slot, piece in enumerate((a, b, c, d)):
        out[row_of(meta, slot, rows), :] = piece[...]


def grad_act_kernel(meta, cot, w_own, w_oth, low_out, act_out):
    rows, width = cot.shape
    slots = 4
    count = rows // slots
    for slot in range(slots):
        at = row_of(meta, slot, count)
        places = meta[3] + meta[6 + slot] + lax.broadcasted_iota(jnp.int32, (count, 1), 0)
        keep = (places < meta[2]).astype(F32)
        low_out[pl.ds(slot * count, count), :] = (cot[at, :].astype(F32) * keep).astype(BF16)
    own, oth = halves(meta, width // 2)

    @pl.loop(0, 2)
    def _(step):
        at = pl.ds(pl.multiple_of(step * (rows // 2), rows // 2), rows // 2)
        act_out[at, :] = dot_nn(low_out[at, own], w_own[...]) + dot_nn(low_out[at, oth], w_oth[...])


def ffn_kernel(meta, n0, n1, n2, n3, g_own, g_oth, u_own, u_oth, grad_act, n_out, act_out, gu_out, *pieces):
    count, width = n0.shape
    units = g_own.shape[1]
    for slot, source in enumerate((n0, n1, n2, n3)):
        n_out[pl.ds(slot * count, count), :] = source[...]
    own, oth = halves(meta, width // 2)
    for step in range(2):
        at = pl.ds(step * 2 * count, 2 * count)
        left, right = n_out[at, own], n_out[at, oth]
        gate = dot_nn(left, g_own[...]) + dot_nn(right, g_oth[...])
        up = dot_nn(left, u_own[...]) + dot_nn(right, u_oth[...])
        sig = jax.nn.sigmoid(gate)
        act_out[at, :] = (gate * sig * up).astype(BF16)
        grad = grad_act[at, :]
        grad_gate = (grad * up * sig * (1.0 + gate * (1.0 - sig))).astype(BF16)
        grad_up = (grad * gate * sig).astype(BF16)
        gu_out[at, :units] = grad_gate
        gu_out[at, units:] = grad_up
        first = (dot_nt(grad_gate, g_own[...]) + dot_nt(grad_up, u_own[...])).astype(BF16)
        pieces[2 * step][:, own] = first[:count]
        pieces[2 * step + 1][:, own] = first[count:]
        second = (dot_nt(grad_gate, g_oth[...]) + dot_nt(grad_up, u_oth[...])).astype(BF16)
        pieces[2 * step][:, oth] = second[:count]
        pieces[2 * step + 1][:, oth] = second[count:]


def down_kernel(meta, act, w_own, w_oth, *pieces):
    count = pieces[0].shape[0]
    own, oth = halves(meta, w_own.shape[0])
    first = dot_nt(act[...], w_own[...]).astype(BF16)
    for slot, piece in enumerate(pieces):
        piece[:, own] = first[slot * count : (slot + 1) * count]
    second = dot_nt(act[...], w_oth[...]).astype(BF16)
    for slot, piece in enumerate(pieces):
        piece[:, oth] = second[slot * count : (slot + 1) * count]


def heads_back_kernel(
    meta, g0, g1, g2, g3, w_own, w_oth, o_in, gain, qe, qh, grad_o, d_chunk, d_total, d_gain, cat_out, grad
):
    heads, rows, width = o_in.shape
    count = g0.shape[0]
    own, oth = halves(meta, w_own.shape[0])
    for slot, source in enumerate((g0, g1, g2, g3)):
        cat_out[pl.ds(slot * count, count), :] = source[...]
    whole = dot_nn(cat_out[:, own], w_own[...]) + dot_nn(cat_out[:, oth], w_oth[...])
    for slot in range(4):
        grad[row_of(meta, slot, count), :] = whole[slot * count : (slot + 1) * count]
    total_gain = jnp.zeros((1, width), F32)
    for head in range(heads):
        out = o_in[head]
        back, part = norm_back(grad[:, head * width : (head + 1) * width], out, gain[...])
        total_gain = total_gain + part
        grad_o[head] = back
        d_total[head] = dot_tn(qh[head], back, HIGH)
        for at in range(rows // CHUNK):
            here = slice(at * CHUNK, (at + 1) * CHUNK)
            d_chunk[head, here, :] = dot_tn(qe[head, here, :], back[here], HIGH)
    d_gain[...] = total_gain


def delta_back_kernel(
    meta, eq, ek, ev, tq, tk, tv, logits,
    w_in, u_in, p_in, t_in, m_in, mp_in, bp_in, s_in, ds_in, do_in, dc_in,
    grad_main, grad_rim, grad_tail, d_taps, d_logits, pad,
):
    rows, width = w_in.shape[1:]
    head = pl.program_id(0)
    places, sames = tap_masks(meta, rows)
    mixed = [conv_rows(e, t[0], rows, sames) for e, t in ((eq, tq), (ek, tk), (ev, tv))]
    sigs, values = zip(*[silu_parts(m) for m in mixed], strict=True)
    scale_q, unit_q = unit_parts(values[0])
    scale_k, unit_k = unit_parts(values[1])
    root = 1.0 / math.sqrt(width)
    q = unit_q * root
    k = unit_k
    v = values[2]
    keep = (places < meta[2]).astype(F32)
    sig_b = jax.nn.sigmoid(pick_column(logits[...], head))
    strength = sig_b * keep
    chunks = rows // CHUNK
    state_in = s_in[0].astype(F32)
    grads_after = [None] * chunks
    grads_after[chunks - 1] = ds_in[0].astype(F32)
    for at in range(chunks - 1, 0, -1):
        here = slice(at * CHUNK, (at + 1) * CHUNK)
        grads_after[at - 1] = dot_tn(m_in[0, here, :], grads_after[at], HIGH) + dc_in[0, here, :]
    grads_q, grads_k, grads_v, grads_b = [], [], [], []
    for at in range(chunks):
        here = slice(at * CHUNK, (at + 1) * CHUNK)
        strict, lower, carry_in, tail, whole = chunk_masks(meta, at)
        qc, kc, vc, bc = q[here], k[here], v[here], strength[here]
        erase, write, scores, inverse = w_in[0, here, :], u_in[0, here, :], p_in[0, here, :], t_in[0, here, :]
        state = dot_nn(mp_in[0, here, :], state_in, HIGH) + bp_in[0, here, :]
        grad_state = grads_after[at]
        grad_o = do_in[0, here, :]
        fresh = write - carry_in * dot_nn(erase, state, HIGH)
        d_fresh = dot_tn(scores, grad_o, HIGH) + tail * dot_nn(kc, grad_state, HIGH)
        d_scores = dot_nt(grad_o, fresh, HIGH) * lower
        back = dot_nt(jnp.concatenate([carry_in * grad_o, carry_in * d_fresh], axis=0), state, HIGH)
        d_q = back[:CHUNK] + dot_nn(d_scores, kc, HIGH)
        d_k = dot_tn(d_scores, qc, HIGH) + dot_nt(tail * fresh, grad_state, HIGH)
        d_erase = -back[CHUNK:]
        right = dot_tn(inverse, jnp.concatenate([d_erase, d_fresh], axis=1), HIGH)
        d_gram = -strict * dot_nt(right, jnp.concatenate([erase, write], axis=1), HIGH)
        d_scaled = right[:, :width] + dot_nn(d_gram, kc, HIGH)
        d_k = d_k + dot_tn(d_gram, bc * kc, HIGH) + bc * d_scaled
        d_b = jnp.sum(d_scaled * kc + right[:, width:] * vc, axis=1, keepdims=True)
        grads_q.append(d_q)
        grads_k.append(d_k)
        grads_v.append(bc * right[:, width:])
        grads_b.append(d_b)
    d_q, d_k, d_v, d_b = (jnp.concatenate(g, axis=0) for g in (grads_q, grads_k, grads_v, grads_b))
    d_logit = d_b * keep * sig_b * (1.0 - sig_b)
    lane = lax.broadcasted_iota(jnp.int32, d_logits.shape, 1)
    d_logits[...] = jnp.where(lane == head, d_logit, d_logits[...])
    d_q = root * scale_q * (d_q - unit_q * jnp.sum(d_q * unit_q, axis=-1, keepdims=True))
    d_k = scale_k * (d_k - unit_k * jnp.sum(d_k * unit_k, axis=-1, keepdims=True))
    zeros = jnp.zeros((RIM, width), F32)
    pad[pl.ds(0, RIM), :] = zeros
    pad[pl.ds(RIM + rows, RIM), :] = zeros
    heads_width = grad_main.shape[1] // 3
    for block, (ext, taps, grad) in enumerate(((eq, tq, d_q), (ek, tk, d_k), (ev, tv, d_v))):
        d_mixed = grad * sigs[block] * (1.0 + mixed[block] * (1.0 - sigs[block]))
        total = jnp.zeros((rows + RIM, width), F32)
        for j in range(TAPS):
            masked = d_mixed * sames[j]
            pad[pl.ds(RIM, rows), :] = masked
            total = total + taps[0, j : j + 1, :] * pad[pl.ds(j, rows + RIM), :]
            d_taps[block, j : j + 1, :] = jnp.sum(
                masked * ext[RIM - j : RIM - j + rows, :], axis=0, keepdims=True
            )
        lanes = pl.ds(pl.multiple_of(block * heads_width + head * width, width), width)
        grad_main[:, lanes] = total[RIM:].astype(BF16)
        grad_rim[:, lanes] = total[:RIM]
        grad_tail[:, lanes] = total[rows:]


def back_project_kernel(meta, grad, logit, wq, wk, wv, wb, xq, xk, xv, xb, *pieces):
    count = pieces[0].shape[0]
    chan = wq.shape[1]
    own, oth = halves(meta, wq.shape[0])
    for side, weights in ((own, (wq, wk, wv, wb)), (oth, (xq, xk, xv, xb))):
        total = dot_nt(logit[...], weights[3][...])
        for block in range(3):
            total = total + dot_nt(grad[:, block * chan : (block + 1) * chan], weights[block][...])
        total = total.astype(BF16)
        for slot, piece in enumerate(pieces):
            piece[:, side] = total[slot * count : (slot + 1) * count]


def flipped(value, axis, bit):
    return lax.ppermute(value, axis, [(i, i ^ bit) for i in range(lax.axis_size(axis))])


def shifted(value, axis, by, reach=None):
    length = lax.axis_size(axis)
    pairs = [(i, i + by) for i in range(length) if 0 <= i + by < length]
    if reach is not None:
        pairs = [pair for pair in pairs if reach(pair[0])]
    return lax.ppermute(value, axis, pairs)


def exchanged(pieces):
    return [pieces[0]] + [flipped(piece, "tp", slot) for slot, piece in enumerate(pieces) if slot]


def gathered(piece):
    return [piece] + [flipped(piece, "tp", slot) for slot in range(1, lax.axis_size("tp"))]


def summed(value, axis):
    bit = 1
    while bit < lax.axis_size(axis):
        value = value + flipped(value, axis, bit)
        bit *= 2
    return value


def contract_rows(left_side, right_side):
    return lax.dot_general(
        left_side, right_side, (((0,), (0,)), ((), ())), preferred_element_type=F32
    )


def pair_gradient(left, right, half):
    mine = lax.axis_index("fsdp")
    other = lax.dynamic_slice_in_dim(left, (1 - mine) * half, half, 1)
    same = lax.dynamic_slice_in_dim(left, mine * half, half, 1)
    sent = flipped(contract_rows(other, right).astype(BF16), "fsdp", 1)
    return (contract_rows(same, right) + sent.astype(F32)).astype(BF16)


def line_scatter(value):
    length = lax.axis_size("ctx")
    place = lax.axis_index("ctx")
    rows = value.shape[0] // length

    def part(index):
        return lax.dynamic_slice_in_dim(value, jnp.clip(index, 0, length - 1) * rows, rows, 0)

    right = left = None
    for step in range(length - 1):
        send = part(length - 1 - step + place)
        if right is not None:
            send = (send.astype(F32) + right.astype(F32)).astype(BF16)
        right = shifted(send, "ctx", 1, lambda i: i <= step)
        send = part(place - (length - 1) + step)
        if left is not None:
            send = (send.astype(F32) + left.astype(F32)).astype(BF16)
        left = shifted(send, "ctx", -1, lambda i: i >= length - 1 - step)
    total = part(place).astype(F32)
    if length > 1:
        total = total + right.astype(F32) + left.astype(F32)
    return total


def shards(
    tokens, seq_bounds, w_query, w_key, w_value, w_beta, conv_taps, out_gain, w_out,
    attn_gain, ffn_gain, w_gate, w_up, w_down, cotangent,
):
    rows, width = tokens.shape
    half = w_query.shape[0]
    chan = w_query.shape[1]
    heads = w_beta.shape[1]
    dim = out_gain.shape[0]
    units = w_gate.shape[1]
    slots = lax.axis_size("tp")
    count = rows // slots
    core, place, member = lax.axis_index("fsdp"), lax.axis_index("ctx"), lax.axis_index("tp")
    meta = jnp.concatenate(
        [
            seq_bounds[0],
            jnp.stack(
                [place * rows, core * half, (1 - core) * half]
                + [(member ^ slot) * count for slot in range(slots)]
            ).astype(jnp.int32),
        ]
    )
    attn_row, ffn_row, out_row = attn_gain[None, :], ffn_gain[None, :], out_gain[None, :]

    rim = shifted(tokens[rows - RIM :], "ctx", 1)
    x_query, x_key, x_value, x_beta = (flipped(w, "fsdp", 1) for w in (w_query, w_key, w_value, w_beta))
    tok_own = lax.dynamic_slice_in_dim(tokens, member * count, count, 0)
    cot_own = lax.dynamic_slice_in_dim(cotangent, member * count, count, 0)

    normed, proj, logits = call(
        project_kernel,
        [shape(rows, width, dtype=BF16), shape(rows + RIM, 3 * chan), shape(rows, heads)],
        (meta, tokens, rim, attn_row, w_query, w_key, w_value, w_beta, x_query, x_key, x_value, x_beta),
        flops=2 * rows * width * 3 * chan,
        scratch=[VMEM((rows + RIM, width), BF16)],
    )
    ext_specs = [
        pl.BlockSpec((rows + RIM, dim), functools.partial(lambda b, h: (0, b * heads + h), b))
        for b in range(3)
    ]
    tap_specs = [
        pl.BlockSpec((1, TAPS, dim), functools.partial(lambda b, h: (b, 0, h), b)) for b in range(3)
    ]
    per_head = pl.BlockSpec((1, rows, dim), lambda h: (h, 0, 0))
    per_state = pl.BlockSpec((1, dim, dim), lambda h: (h, 0, 0))
    logit_spec = pl.BlockSpec((rows, heads), lambda h: (0, 0))
    tall, square = shape(heads, rows, dim), shape(heads, dim, dim)
    erase, write, scores, inverse, query_eff, step, prefix, added, query_hat, out_hat, m_total, b_total = call(
        delta_kernel,
        [tall] * 10 + [square] * 2,
        (meta, proj, proj, proj, conv_taps, conv_taps, conv_taps, logits),
        flops=heads * 60 * rows * dim * dim,
        grid=(heads,),
        in_specs=[SCALARS] + ext_specs + tap_specs + [logit_spec],
        out_specs=[per_head] * 10 + [per_state] * 2,
    )

    def hop(matrix, extra, state, flip):
        return call(
            functools.partial(hop_kernel, flip=flip),
            shape(heads, dim, dim, dtype=BF16),
            (matrix, extra, state),
            flops=2 * heads * dim**3,
            in_specs=[WHOLE] * 3,
        )

    state = jnp.zeros((heads, dim, dim), BF16)
    for index in range(lax.axis_size("ctx") - 1):
        sent = b_total.astype(BF16) if index == 0 else hop(m_total, b_total, state, False)
        state = shifted(sent, "ctx", 1)

    x_out = flipped(w_out, "fsdp", 1)
    piece_shape = shape(count, width, dtype=BF16)
    heads_slot, heads_out, *pieces = call(
        attend_kernel,
        [shape(rows, chan, dtype=BF16), tall] + [piece_shape] * slots,
        (meta, query_hat, out_hat, state, out_row, w_out, x_out),
        flops=2 * rows * width * chan,
        scratch=[VMEM((rows, chan), BF16)],
    )
    x_down, x_gate, x_up = (flipped(w, "fsdp", 1) for w in (w_down, w_gate, w_up))
    grad_low, grad_act = call(
        grad_act_kernel,
        [shape(rows, width, dtype=BF16), shape(rows, units)],
        (meta, cotangent, w_down, x_down),
        flops=2 * rows * width * units,
    )
    hidden, normed_two = call(
        norm_two_kernel,
        [shape(count, width), piece_shape],
        (*exchanged(pieces), tok_own, ffn_row),
        in_specs=[WHOLE] * 6,
    )
    normed_slot, act, grad_gu, *pieces = call(
        ffn_kernel,
        [
            shape(rows, width, dtype=BF16),
            shape(rows, units, dtype=BF16),
            shape(rows, 2 * units, dtype=BF16),
        ]
        + [piece_shape] * slots,
        (meta, *gathered(normed_two), w_gate, x_gate, w_up, x_up, grad_act),
        flops=8 * rows * width * units,
    )
    received = exchanged(pieces)
    down_pair = pair_gradient(grad_low, act, half)
    gu_pair = pair_gradient(normed_slot, grad_gu, half)
    grad_hidden, grad_att, d_ffn_part = call(
        norm_two_back_kernel,
        [shape(count, width), piece_shape, shape(1, width)],
        (meta, *received, hidden, cot_own, ffn_row),
    )
    down_pieces = call(
        down_kernel,
        [piece_shape] * slots,
        (meta, act, w_down, x_down),
        flops=2 * rows * width * units,
    )
    grad_o, d_chunk, d_total, d_head_part, grad_att_slot = call(
        heads_back_kernel,
        [tall, tall, square, shape(1, dim), shape(rows, width, dtype=BF16)],
        (meta, *gathered(grad_att), w_out, x_out, heads_out, out_row, query_eff, query_hat),
        flops=2 * rows * width * chan,
        scratch=[VMEM((rows, chan), F32)],
    )
    grad_state = jnp.zeros((heads, dim, dim), BF16)
    for index in range(lax.axis_size("ctx") - 1):
        sent = d_total.astype(BF16) if index == 0 else hop(m_total, d_total, grad_state, True)
        grad_state = shifted(sent, "ctx", -1)
    out_pair = pair_gradient(grad_att_slot, heads_slot, half)

    grad_main, grad_rim, grad_tail, d_conv_part, d_logits = call(
        delta_back_kernel,
        [
            shape(rows, 3 * chan, dtype=BF16),
            shape(RIM, 3 * chan),
            shape(RIM, 3 * chan),
            shape(3, TAPS, chan),
            shape(rows, heads),
        ],
        (
            meta, proj, proj, proj, conv_taps, conv_taps, conv_taps, logits,
            erase, write, scores, inverse, step, prefix, added, state, grad_state, grad_o, d_chunk,
        ),
        flops=heads * 60 * rows * dim * dim,
        grid=(heads,),
        in_specs=[SCALARS] + ext_specs + tap_specs + [logit_spec] + [per_head] * 7 + [per_state] * 2 + [per_head] * 2,
        out_specs=[
            pl.BlockSpec((rows, 3 * chan), lambda h: (0, 0)),
            pl.BlockSpec((RIM, 3 * chan), lambda h: (0, 0)),
            pl.BlockSpec((RIM, 3 * chan), lambda h: (0, 0)),
            pl.BlockSpec((3, TAPS, dim), lambda h: (0, 0, h)),
            pl.BlockSpec((rows, heads), lambda h: (0, 0)),
        ],
        scratch=[VMEM((rows + 2 * RIM, dim), F32)],
    )
    tail = (grad_tail + shifted(grad_rim, "ctx", -1)).astype(BF16)
    grad_proj = lax.dynamic_update_slice(grad_main, tail, (rows - RIM, 0))
    grad_logit = d_logits.astype(BF16)
    ordered = jnp.concatenate(
        [
            lax.dynamic_slice_in_dim(grad_proj, (member ^ slot) * count, count, 0)
            for slot in range(slots)
        ],
        axis=0,
    )
    ordered_logit = jnp.concatenate(
        [
            lax.dynamic_slice_in_dim(grad_logit, (member ^ slot) * count, count, 0)
            for slot in range(slots)
        ],
        axis=0,
    )
    pieces = call(
        back_project_kernel,
        [piece_shape] * slots,
        (meta, ordered, ordered_logit, w_query, w_key, w_value, w_beta, x_query, x_key, x_value, x_beta),
        flops=2 * rows * width * 3 * chan,
    )
    d_tok_own, d_attn_part = call(
        norm_one_back_kernel,
        [piece_shape, shape(1, width)],
        (*exchanged(pieces), tok_own, attn_row, grad_hidden),
        in_specs=[WHOLE] * 7,
    )
    d_tokens = call(place_kernel, shape(rows, width, dtype=BF16), (meta, *gathered(d_tok_own)))
    proj_pair = pair_gradient(normed, grad_proj, half)

    down_sum = hidden
    for piece in exchanged(down_pieces):
        down_sum = down_sum + piece.astype(F32)
    out = call(place_kernel, shape(rows, width, dtype=BF16), (meta, *gathered(down_sum.astype(BF16))))

    d_w_down = line_scatter(down_pair)
    d_w_gu = line_scatter(gu_pair)
    d_w_out = line_scatter(out_pair)
    d_w_proj = line_scatter(proj_pair)

    d_beta_part = contract_rows(grad_logit, normed)
    conv_rows_count = 3 * TAPS * chan // width
    early = summed(
        jnp.concatenate([d_ffn_part, jnp.pad(d_head_part, ((0, 0), (0, width - dim)))], axis=0), "tp"
    )
    bundle = jnp.concatenate([early, d_beta_part, d_conv_part.reshape(conv_rows_count, width)], axis=0)
    bundle = summed(summed(bundle, "fsdp"), "ctx")
    d_attn = summed(summed(summed(d_attn_part, "tp"), "fsdp"), "ctx")
    share = width // (lax.axis_size("fsdp") * lax.axis_size("ctx"))
    d_beta = lax.dynamic_slice_in_dim(
        bundle[2 : 2 + heads], core * half + place * share, share, 1
    ).T
    return (
        out,
        d_tokens,
        d_w_proj[:, :chan],
        d_w_proj[:, chan : 2 * chan],
        d_w_proj[:, 2 * chan :],
        d_beta,
        bundle[2 + heads :].reshape(3, TAPS, chan),
        bundle[1, :dim],
        d_w_out,
        d_attn[0],
        bundle[0],
        d_w_gu[:, :units],
        d_w_gu[:, units:],
        d_w_down,
    )


def solution(mesh):
    both = P(("fsdp", "ctx"), None)
    weight = P("fsdp", "tp")
    grad = P(("fsdp", "ctx"), "tp")
    in_specs = (
        both, P("fsdp", None), weight, weight, weight, weight, P(None, None, "tp"), P(), weight,
        P(), P(), weight, weight, weight, both,
    )
    out_specs = (
        both, both, grad, grad, grad, grad, P(None, None, "tp"), P(), grad, P(), P(), grad, grad, grad,
    )
    return jax.shard_map(shards, mesh=mesh, in_specs=in_specs, out_specs=out_specs, check_vma=False)
```

```python
import functools
import math

import jax
import jax.numpy as jnp
from jax import lax
from jax.experimental import pallas as pl
from jax.experimental.pallas import tpu as pltpu
from jax.sharding import PartitionSpec as P

EPS = 1e-06
HIGH = True
F32 = jnp.float32
BF16 = jnp.bfloat16
CHUNK = 128
RIM = 16
TAPS = 4
VMEM = pltpu.VMEM
WHOLE = pl.BlockSpec(memory_space=pltpu.VMEM)
SCALARS = pl.BlockSpec(memory_space=pltpu.SMEM)


def split(value):
    high = value.astype(BF16)
    return high, (value - high.astype(F32)).astype(BF16)


def product(dims, left, right, exact):
    def one(a, b):
        return lax.dot_general(a, b, (dims, ((), ())), preferred_element_type=F32)

    if not exact:
        return one(left.astype(BF16), right.astype(BF16))
    (left_hi, left_lo), (right_hi, right_lo) = split(left), split(right)
    return one(left_hi, right_hi) + (one(left_hi, right_lo) + one(left_lo, right_hi))


def dot_nn(left, right, exact=False):
    return product(((1,), (0,)), left, right, exact)


def dot_nt(left, right, exact=False):
    return product(((1,), (1,)), left, right, exact)


def dot_tn(left, right, exact=False):
    return product(((0,), (0,)), left, right, exact)


def call(kernel, out_shape, operands, flops=0, scratch=(), scalars=True, after=(), filler=False):
    outs = out_shape if isinstance(out_shape, list) else [out_shape]
    size = sum(math.prod(x.shape) * x.dtype.itemsize for x in (*operands, *outs))
    given = len(operands)

    def body(*refs):
        kernel(*refs[:given], *refs[given + len(after) :])

    return pl.pallas_call(
        body,
        out_shape=out_shape,
        in_specs=[SCALARS] * scalars
        + [WHOLE] * (given - scalars)
        + [pl.BlockSpec(memory_space=pl.ANY)] * len(after),
        out_specs=[WHOLE] * len(outs) if isinstance(out_shape, list) else WHOLE,
        scratch_shapes=list(scratch),
        cost_estimate=pl.CostEstimate(
            flops=1 if filler else flops, bytes_accessed=1 if filler else size, transcendentals=0
        ),
        compiler_params=pltpu.CompilerParams(vmem_limit_bytes=58 << 20),
    )(*operands, *after)


def shape(*dims, dtype=F32):
    return jax.ShapeDtypeStruct(dims, dtype)


def seg_of(places, meta):
    ids = (
        (places >= meta[0]).astype(jnp.int32)
        + (places >= meta[1]).astype(jnp.int32)
        + (places >= meta[2]).astype(jnp.int32)
    )
    return jnp.where(places < 0, -1, ids)


def row_of(meta, slot, rows):
    return pl.ds(pl.multiple_of(meta[6 + slot], rows), rows)


def halves(meta, half):
    return (
        pl.ds(pl.multiple_of(meta[4], half), half),
        pl.ds(pl.multiple_of(meta[5], half), half),
    )


def project_kernel(meta, tok, rim, gain, wq, wk, wv, wb, xq, xk, xv, xb, ext, proj, logits):
    rows, width = tok.shape
    for source, at, count in ((rim, 0, RIM), (tok, RIM, rows)):
        values = source[...].astype(F32)
        scale = lax.rsqrt(jnp.mean(values * values, axis=-1, keepdims=True) + EPS)
        ext[pl.ds(at, count), :] = (values * scale * gain[...]).astype(BF16)
    own, oth = halves(meta, width // 2)
    left, right = ext[:, own], ext[:, oth]
    chan = wq.shape[1]
    for at, (a, b) in enumerate(((wq, xq), (wk, xk), (wv, xv))):
        proj[:, at * chan : (at + 1) * chan] = dot_nn(left, a[...]) + dot_nn(right, b[...])
    logits[...] = dot_nn(left[RIM:], wb[...]) + dot_nn(right[RIM:], xb[...])


def conv_rows(ext, taps, block, lanes, rows, sames):
    start = block * taps.shape[2]
    columns = slice(start + lanes.start, start + lanes.stop)
    mixed = None
    for j in range(TAPS):
        term = taps[block, j : j + 1, lanes] * ext[RIM - j : RIM - j + rows, columns] * sames[j]
        mixed = term if mixed is None else mixed + term
    return mixed


def tap_masks(meta, rows):
    places = meta[3] + lax.broadcasted_iota(jnp.int32, (rows, 1), 0)
    seg = seg_of(places, meta)
    return places, [(seg_of(places - j, meta) == seg).astype(F32) for j in range(TAPS)]


def pick_column(values, head):
    lane = lax.broadcasted_iota(jnp.int32, values.shape, 1)
    return jnp.sum(jnp.where(lane == head, values, 0.0), axis=1, keepdims=True)


def chunk_masks(meta, at):
    first = meta[3] + at * CHUNK
    row = lax.broadcasted_iota(jnp.int32, (CHUNK, CHUNK), 0)
    col = lax.broadcasted_iota(jnp.int32, (CHUNK, CHUNK), 1)
    seg_col = seg_of(first + lax.broadcasted_iota(jnp.int32, (CHUNK, 1), 0), meta)
    seg_row = seg_of(first + lax.broadcasted_iota(jnp.int32, (1, CHUNK), 1), meta)
    before = seg_of(first - 1, meta)
    last = seg_of(first + CHUNK - 1, meta)
    same = (seg_col == seg_row).astype(F32)
    strict = jnp.where(row > col, same, 0.0)
    lower = jnp.where(row >= col, same, 0.0)
    carry_in = (seg_col == before).astype(F32)
    tail = (seg_col == last).astype(F32)
    whole = (last == before).astype(F32)
    return strict, lower, carry_in, tail, whole


def unit_inverses(grams):
    row = lax.broadcasted_iota(jnp.int32, (CHUNK, CHUNK), 0)
    col = lax.broadcasted_iota(jnp.int32, (CHUNK, CHUNK), 1)
    eye = (row == col).astype(F32)
    size = 8
    near = [jnp.where(row // size == col // size, g, 0.0) for g in grams]
    power = [dot_nn(n, n) for n in near]
    inverse = [eye - n for n in near]
    inverse = [x + dot_nn(x, p) for x, p in zip(inverse, power)]
    power = [dot_nn(p, p) for p in power]
    inverse = [x + dot_nn(x, p) for x, p in zip(inverse, power)]
    while size < CHUNK:
        off = (row // (2 * size) == col // (2 * size)) & (row // size != col // size)
        inner = [dot_nn(jnp.where(off, g, 0.0), x) for g, x in zip(grams, inverse)]
        inverse = [x - dot_nn(x, y) for x, y in zip(inverse, inner)]
        size *= 2
    resid = [(eye - x) - dot_nn(g, x, HIGH) for g, x in zip(grams, inverse)]
    return [x + dot_nn(x, r) for x, r in zip(inverse, resid)]

def silu_parts(mixed):
    sig = jax.nn.sigmoid(mixed)
    return sig, mixed * sig


def unit_parts(values):
    scale = lax.rsqrt(jnp.sum(values * values, axis=-1, keepdims=True) + EPS)
    return scale, values * scale


def delta_kernel(
    meta, ext, taps, logits,
    w_out, u_out, p_out, t_out, qe_out, m_out, mp_out, bp_out, qh_out, oh_out, mtot, btot,
):
    group, rows, width = w_out.shape
    places, sames = tap_masks(meta, rows)
    keep = (places < meta[2]).astype(F32)
    row = lax.broadcasted_iota(jnp.int32, (width, width), 0)
    col = lax.broadcasted_iota(jnp.int32, (width, width), 1)
    eye = (row == col).astype(F32)
    q, k, v, b = [], [], [], []
    for head in range(group):
        lanes = slice(head * width, (head + 1) * width)
        x = silu_parts(conv_rows(ext, taps, 0, lanes, rows, sames))[1]
        q.append(unit_parts(x)[1] * (1.0 / math.sqrt(width)))
        x = silu_parts(conv_rows(ext, taps, 1, lanes, rows, sames))[1]
        k.append(unit_parts(x)[1])
        v.append(silu_parts(conv_rows(ext, taps, 2, lanes, rows, sames))[1])
        b.append(jax.nn.sigmoid(pick_column(logits[...], head)) * keep)
    chunks = rows // CHUNK
    spots = [slice(at * CHUNK, (at + 1) * CHUNK) for at in range(chunks)]
    masks = [chunk_masks(meta, at) for at in range(chunks)]
    chains = [(head, at) for head in range(group) for at in range(chunks)]
    kc = [k[h][spots[a]] for h, a in chains]
    qc = [q[h][spots[a]] for h, a in chains]
    scaled = [b[h][spots[a]] * k[h][spots[a]] for h, a in chains]
    scaled_v = [b[h][spots[a]] * v[h][spots[a]] for h, a in chains]
    grams = [dot_nt(s, x, HIGH) * masks[a][0] for (h, a), s, x in zip(chains, scaled, kc)]
    scores = [dot_nt(y, x, HIGH) * masks[a][1] for (h, a), y, x in zip(chains, qc, kc)]
    inverse = unit_inverses(grams)
    both = [dot_nn(t, jnp.concatenate([s, u], axis=1), HIGH) for t, s, u in zip(inverse, scaled, scaled_v)]
    inner = [
        jnp.concatenate([masks[a][2] * x[:, :width], x[:, width:]], axis=1) for (h, a), x in zip(chains, both)
    ]
    states = [dot_tn(x, masks[a][3] * y, HIGH) for (h, a), x, y in zip(chains, kc, inner)]
    reach = [dot_nn(s, y, HIGH) for s, y in zip(scores, inner)]
    steps = [masks[a][4] * eye - s[:, :width] for (h, a), s in zip(chains, states)]
    query = [masks[a][2] * x - y[:, :width] for (h, a), x, y in zip(chains, qc, reach)]
    for i, (h, a) in enumerate(chains):
        w_out[h, spots[a], :] = both[i][:, :width]
        u_out[h, spots[a], :] = both[i][:, width:]
        p_out[h, spots[a], :] = scores[i]
        t_out[h, spots[a], :] = inverse[i]
        qe_out[h, spots[a], :] = query[i]
        m_out[h, spots[a], :] = steps[i]
    prefix = [eye] * group
    added = [jnp.zeros((width, width), F32)] * group
    for a in range(chunks):
        for h in range(group):
            i = h * chunks + a
            mp_out[h, spots[a], :] = prefix[h]
            bp_out[h, spots[a], :] = added[h]
            if a == 0:
                qh_out[h, spots[a], :] = query[i]
                oh_out[h, spots[a], :] = reach[i][:, width:]
                prefix[h], added[h] = steps[i], states[i][:, width:]
                continue
            out = dot_nn(
                jnp.concatenate([query[i], steps[i]], axis=0),
                jnp.concatenate([prefix[h], added[h]], axis=1),
                HIGH,
            )
            qh_out[h, spots[a], :] = out[:CHUNK, :width]
            oh_out[h, spots[a], :] = out[:CHUNK, width:] + reach[i][:, width:]
            prefix[h], added[h] = out[CHUNK:, :width], out[CHUNK:, width:] + states[i][:, width:]
    for h in range(group):
        mtot[h] = prefix[h]
        btot[h] = added[h]


def hop_kernel(step, extra, state, out, *, flip):
    for head in range(step.shape[0]):
        value = state[head].astype(F32)
        product = dot_tn(step[head], value, HIGH) if flip else dot_nn(step[head], value, HIGH)
        out[head] = (product + extra[head]).astype(BF16)


def attend_kernel(meta, qh, oh, state, gain, w_own, w_oth, heads_slot, o_out, *rest):
    pieces, low = rest[:-1], rest[-1]
    heads, rows, width = qh.shape
    for head in range(heads):
        out = dot_nn(qh[head], state[head].astype(F32), HIGH) + oh[head]
        o_out[head] = out
        scale = lax.rsqrt(jnp.mean(out * out, axis=-1, keepdims=True) + EPS)
        low[:, head * width : (head + 1) * width] = (out * scale * gain[...]).astype(BF16)
    count = rows // len(pieces)
    own, oth = halves(meta, w_own.shape[0])
    for slot, piece in enumerate(pieces):
        part = low[row_of(meta, slot, count), :]
        heads_slot[pl.ds(slot * count, count), :] = part
        piece[:, own] = dot_nt(part, w_own[...]).astype(BF16)
        piece[:, oth] = dot_nt(part, w_oth[...]).astype(BF16)


def norm_two_kernel(a, b, c, d, tok, gain, hidden_out, normed_out):
    total = a[...].astype(F32) + b[...].astype(F32) + c[...].astype(F32) + d[...].astype(F32)
    hidden = tok[...].astype(F32) + total
    scale = lax.rsqrt(jnp.mean(hidden * hidden, axis=-1, keepdims=True) + EPS)
    hidden_out[...] = hidden
    normed_out[...] = (hidden * scale * gain[...]).astype(BF16)


def norm_back(grad, values, gain):
    scale = lax.rsqrt(jnp.mean(values * values, axis=-1, keepdims=True) + EPS)
    normal = values * scale
    hat = grad * gain
    back = scale * (hat - normal * jnp.mean(hat * normal, axis=-1, keepdims=True))
    return back, jnp.sum(grad * normal, axis=0, keepdims=True)


def norm_two_back_kernel(meta, a, b, c, d, hidden, cot, gain, grad_hidden, grad_att, d_gain):
    total = a[...].astype(F32) + b[...].astype(F32) + c[...].astype(F32) + d[...].astype(F32)
    back, d_gain[...] = norm_back(total, hidden[...], gain[...])
    places = meta[3] + meta[6] + lax.broadcasted_iota(jnp.int32, (hidden.shape[0], 1), 0)
    grad = cot[...].astype(F32) * (places < meta[2]).astype(F32) + back
    grad_hidden[...] = grad
    grad_att[...] = grad.astype(BF16)


def norm_one_back_kernel(a, b, c, d, tok, gain, grad_hidden, d_tok, d_gain):
    total = a[...].astype(F32) + b[...].astype(F32) + c[...].astype(F32) + d[...].astype(F32)
    back, d_gain[...] = norm_back(total, tok[...].astype(F32), gain[...])
    d_tok[...] = (grad_hidden[...] + back).astype(BF16)


def place_kernel(meta, a, b, c, d, out):
    rows = a.shape[0]
    for slot, piece in enumerate((a, b, c, d)):
        out[row_of(meta, slot, rows), :] = piece[...]


def grad_act_kernel(meta, cot, w_own, w_oth, low_out, act_out):
    rows, width = cot.shape
    slots = 4
    count = rows // slots
    for slot in range(slots):
        at = row_of(meta, slot, count)
        places = meta[3] + meta[6 + slot] + lax.broadcasted_iota(jnp.int32, (count, 1), 0)
        keep = (places < meta[2]).astype(F32)
        low_out[pl.ds(slot * count, count), :] = (cot[at, :].astype(F32) * keep).astype(BF16)
    own, oth = halves(meta, width // 2)

    @pl.loop(0, 2)
    def _(step):
        at = pl.ds(pl.multiple_of(step * (rows // 2), rows // 2), rows // 2)
        act_out[at, :] = dot_nn(low_out[at, own], w_own[...]) + dot_nn(low_out[at, oth], w_oth[...])


def ffn_kernel(meta, n0, n1, n2, n3, g_own, g_oth, u_own, u_oth, grad_act, n_out, act_out, gg_out, gu_out, *pieces):
    count, width = n0.shape
    for slot, source in enumerate((n0, n1, n2, n3)):
        n_out[pl.ds(slot * count, count), :] = source[...]
    own, oth = halves(meta, width // 2)
    for step in range(2):
        at = pl.ds(step * 2 * count, 2 * count)
        left, right = n_out[at, own], n_out[at, oth]
        gate = dot_nn(left, g_own[...]) + dot_nn(right, g_oth[...])
        up = dot_nn(left, u_own[...]) + dot_nn(right, u_oth[...])
        sig = jax.nn.sigmoid(gate)
        act_out[at, :] = (gate * sig * up).astype(BF16)
        grad = grad_act[at, :]
        grad_gate = (grad * up * sig * (1.0 + gate * (1.0 - sig))).astype(BF16)
        grad_up = (grad * gate * sig).astype(BF16)
        gg_out[at, :] = grad_gate
        gu_out[at, :] = grad_up
        first = (dot_nt(grad_gate, g_own[...]) + dot_nt(grad_up, u_own[...])).astype(BF16)
        pieces[2 * step][:, own] = first[:count]
        pieces[2 * step + 1][:, own] = first[count:]
        second = (dot_nt(grad_gate, g_oth[...]) + dot_nt(grad_up, u_oth[...])).astype(BF16)
        pieces[2 * step][:, oth] = second[:count]
        pieces[2 * step + 1][:, oth] = second[count:]


def down_kernel(meta, act, w_own, w_oth, *pieces):
    count = pieces[0].shape[0]
    own, oth = halves(meta, w_own.shape[0])
    first = dot_nt(act[...], w_own[...]).astype(BF16)
    for slot, piece in enumerate(pieces):
        piece[:, own] = first[slot * count : (slot + 1) * count]
    second = dot_nt(act[...], w_oth[...]).astype(BF16)
    for slot, piece in enumerate(pieces):
        piece[:, oth] = second[slot * count : (slot + 1) * count]


def heads_back_kernel(
    meta, g0, g1, g2, g3, w_own, w_oth, o_in, gain, qe, qh, grad_o, d_chunk, d_total, d_gain, cat_out, grad
):
    heads, rows, width = o_in.shape
    count = g0.shape[0]
    own, oth = halves(meta, w_own.shape[0])
    for slot, source in enumerate((g0, g1, g2, g3)):
        cat_out[pl.ds(slot * count, count), :] = source[...]
    whole = dot_nn(cat_out[:, own], w_own[...]) + dot_nn(cat_out[:, oth], w_oth[...])
    for slot in range(4):
        grad[row_of(meta, slot, count), :] = whole[slot * count : (slot + 1) * count]
    total_gain = jnp.zeros((1, width), F32)
    for head in range(heads):
        out = o_in[head]
        back, part = norm_back(grad[:, head * width : (head + 1) * width], out, gain[...])
        total_gain = total_gain + part
        grad_o[head] = back
        d_total[head] = dot_tn(qh[head], back, HIGH)
        for at in range(rows // CHUNK):
            here = slice(at * CHUNK, (at + 1) * CHUNK)
            d_chunk[head, here, :] = dot_tn(qe[head, here, :], back[here], HIGH)
    d_gain[...] = total_gain


def delta_back_kernel(
    meta, ext, taps, logits,
    w_in, u_in, p_in, t_in, m_in, mp_in, bp_in, s_in, ds_in, do_in, dc_in,
    grad_ext, grad_rim, grad_tail, d_taps, d_logits, pad,
):
    group, rows, width = w_in.shape
    places, sames = tap_masks(meta, rows)
    keep = (places < meta[2]).astype(F32)
    root = 1.0 / math.sqrt(width)
    chunks = rows // CHUNK
    spots = [slice(at * CHUNK, (at + 1) * CHUNK) for at in range(chunks)]
    masks = [chunk_masks(meta, at) for at in range(chunks)]
    chains = [(head, at) for head in range(group) for at in range(chunks)]
    q, k, v, b, sig_b, scale_q, scale_k = [], [], [], [], [], [], []
    for head in range(group):
        lanes = slice(head * width, (head + 1) * width)
        scale, unit = unit_parts(silu_parts(conv_rows(ext, taps, 0, lanes, rows, sames))[1])
        scale_q.append(scale)
        q.append(unit)
        scale, unit = unit_parts(silu_parts(conv_rows(ext, taps, 1, lanes, rows, sames))[1])
        scale_k.append(scale)
        k.append(unit)
        v.append(silu_parts(conv_rows(ext, taps, 2, lanes, rows, sames))[1])
        sig_b.append(jax.nn.sigmoid(pick_column(logits[...], head)))
        b.append(sig_b[head] * keep)
    after = {}
    for head in range(group):
        after[head, chunks - 1] = ds_in[head].astype(F32)
    for at in range(chunks - 1, 0, -1):
        for head in range(group):
            after[head, at - 1] = dot_tn(m_in[head, spots[at], :], after[head, at], HIGH) + dc_in[head, spots[at], :]
    grad_state = [after[c] for c in chains]
    state = [dot_nn(mp_in[h, spots[a], :], s_in[h].astype(F32), HIGH) + bp_in[h, spots[a], :] for h, a in chains]
    kc = [k[h][spots[a]] for h, a in chains]
    grad_o = [do_in[h, spots[a], :] for h, a in chains]
    fresh = [
        u_in[h, spots[a], :] - masks[a][2] * dot_nn(w_in[h, spots[a], :], s, HIGH)
        for (h, a), s in zip(chains, state)
    ]
    d_fresh = [
        dot_tn(p_in[h, spots[a], :], g, HIGH) + masks[a][3] * dot_nn(x, s, HIGH)
        for (h, a), g, x, s in zip(chains, grad_o, kc, grad_state)
    ]
    d_scores = [dot_nt(g, f, HIGH) * masks[a][1] for (h, a), g, f in zip(chains, grad_o, fresh)]
    back = [
        dot_nt(jnp.concatenate([masks[a][2] * g, masks[a][2] * f], axis=0), s, HIGH)
        for (h, a), g, f, s in zip(chains, grad_o, d_fresh, state)
    ]
    d_q = [x[:CHUNK] + dot_nn(d, y, HIGH) for x, d, y in zip(back, d_scores, kc)]
    d_k = [
        root * dot_tn(d, q[h][spots[a]], HIGH) + dot_nt(masks[a][3] * f, s, HIGH)
        for (h, a), d, f, s in zip(chains, d_scores, fresh, grad_state)
    ]
    right = [
        dot_tn(t_in[h, spots[a], :], jnp.concatenate([-x[CHUNK:], f], axis=1), HIGH)
        for (h, a), x, f in zip(chains, back, d_fresh)
    ]
    d_gram = [
        -masks[a][0] * dot_nt(r, jnp.concatenate([w_in[h, spots[a], :], u_in[h, spots[a], :]], axis=1), HIGH)
        for (h, a), r in zip(chains, right)
    ]
    d_scaled = [r[:, :width] + dot_nn(g, x, HIGH) for r, g, x in zip(right, d_gram, kc)]
    d_k = [
        x + dot_tn(g, b[h][spots[a]] * y, HIGH) + b[h][spots[a]] * d
        for (h, a), x, g, y, d in zip(chains, d_k, d_gram, kc, d_scaled)
    ]
    d_b = [
        jnp.sum(d * y + r[:, width:] * v[h][spots[a]], axis=1, keepdims=True)
        for (h, a), d, y, r in zip(chains, d_scaled, kc, right)
    ]
    d_v = [b[h][spots[a]] * r[:, width:] for (h, a), r in zip(chains, right)]
    lane = lax.broadcasted_iota(jnp.int32, d_logits.shape, 1)
    all_logits = jnp.zeros(d_logits.shape, F32)
    zeros = jnp.zeros((RIM, width), F32)
    heads_width = grad_ext.shape[1] // 3
    for head in range(group):
        mine = slice(head * chunks, (head + 1) * chunks)
        lanes = slice(head * width, (head + 1) * width)
        d_logit = jnp.concatenate(d_b[mine], axis=0) * keep * sig_b[head] * (1.0 - sig_b[head])
        all_logits = jnp.where(lane == head, d_logit, all_logits)
        g_q, g_k, g_v = (jnp.concatenate(x[mine], axis=0) for x in (d_q, d_k, d_v))
        g_q = root * scale_q[head] * (g_q - q[head] * jnp.sum(g_q * q[head], axis=-1, keepdims=True))
        g_k = scale_k[head] * (g_k - k[head] * jnp.sum(g_k * k[head], axis=-1, keepdims=True))
        for block, grad in enumerate((g_q, g_k, g_v)):
            spot = head * 3 + block
            at = slice(block * heads_width + head * width, block * heads_width + (head + 1) * width)
            pad[spot, pl.ds(0, RIM), :] = zeros
            pad[spot, pl.ds(RIM + rows, RIM), :] = zeros
            mixed = conv_rows(ext, taps, block, lanes, rows, sames)
            sig = silu_parts(mixed)[0]
            d_mixed = grad * sig * (1.0 + mixed * (1.0 - sig))
            total = jnp.zeros((rows + RIM, width), F32)
            for j in range(TAPS):
                masked = d_mixed * sames[j]
                pad[spot, pl.ds(RIM, rows), :] = masked
                total = total + taps[block, j : j + 1, lanes] * pad[spot, pl.ds(j, rows + RIM), :]
                d_taps[block, j : j + 1, lanes] = jnp.sum(
                    masked * ext[RIM - j : RIM - j + rows, at], axis=0, keepdims=True
                )
            grad_ext[:, at] = total.astype(BF16)
            grad_rim[:, at] = total[:RIM]
            grad_tail[:, at] = total[rows:]
    d_logits[...] = all_logits.astype(BF16)


def back_project_kernel(
    meta, grad_ext, tail, returned, logit_in, wq, wk, wv, wb, xq, xk, xv, xb, *rest
):
    pieces, grad, logit = rest[:-2], rest[-2], rest[-1]
    count = pieces[0].shape[0]
    chan = wq.shape[1]
    for slot in range(len(pieces)):
        here = pl.ds(slot * count, count)
        start = pl.multiple_of(meta[6 + slot], count)
        grad[here, :] = grad_ext[pl.ds(pl.multiple_of(start + RIM, RIM), count), :]
        logit[here, :] = logit_in[pl.ds(start, count), :]
    last = pl.multiple_of(meta[6 + len(pieces) - 1] + count - RIM, RIM)
    grad[pl.ds(last, RIM), :] = (tail[...] + returned[...]).astype(BF16)
    own, oth = halves(meta, wq.shape[0])
    for side, weights in ((own, (wq, wk, wv, wb)), (oth, (xq, xk, xv, xb))):
        total = dot_nt(logit[...], weights[3][...])
        for block in range(3):
            total = total + dot_nt(grad[:, block * chan : (block + 1) * chan], weights[block][...])
        total = total.astype(BF16)
        for slot, piece in enumerate(pieces):
            piece[:, side] = total[slot * count : (slot + 1) * count]


def sent_kernel(meta, left, *rest):
    rights, out = rest[:-1], rest[-1]
    lhs = left[:, halves(meta, out.shape[0])[1]]
    at = 0
    for right in rights:
        out[:, at : at + right.shape[1]] = dot_tn(lhs, right[...]).astype(BF16)
        at += right.shape[1]


def kept_kernel(meta, left, *rest):
    rights, received, out = rest[:-2], rest[-2], rest[-1]
    lhs = left[:, halves(meta, out.shape[0])[0]]
    at = 0
    for right in rights:
        here = slice(at, at + right.shape[1])
        out[:, here] = (dot_tn(lhs, right[...]) + received[:, here].astype(F32)).astype(BF16)
        at += right.shape[1]


def flipped(value, axis, bit):
    return lax.ppermute(value, axis, [(i, i ^ bit) for i in range(lax.axis_size(axis))])


def shifted(value, axis, by, reach=None):
    length = lax.axis_size(axis)
    pairs = [(i, i + by) for i in range(length) if 0 <= i + by < length]
    if reach is not None:
        pairs = [pair for pair in pairs if reach(pair[0])]
    return lax.ppermute(value, axis, pairs)


def exchanged(pieces):
    return [pieces[0]] + [flipped(piece, "tp", slot) for slot, piece in enumerate(pieces) if slot]


def gathered(piece):
    return [piece] + [flipped(piece, "tp", slot) for slot in range(1, lax.axis_size("tp"))]


def summed(value, axis):
    bit = 1
    while bit < lax.axis_size(axis):
        value = value + flipped(value, axis, bit)
        bit *= 2
    return value


def contract_rows(left_side, right_side):
    return lax.dot_general(
        left_side, right_side, (((0,), (0,)), ((), ())), preferred_element_type=F32
    )


def pair_sent(meta, left, *rights, after=()):
    rows, half = left.shape[0], left.shape[1] // 2
    columns = sum(right.shape[1] for right in rights)
    out = call(
        sent_kernel,
        shape(half, columns, dtype=BF16),
        (meta, left, *rights),
        after=after,
        filler=True,
    )
    return out, flipped(out, "fsdp", 1)


def pair_kept(meta, received, left, *rights, after=()):
    rows, half = left.shape[0], left.shape[1] // 2
    columns = sum(right.shape[1] for right in rights)
    return call(
        kept_kernel,
        shape(half, columns, dtype=BF16),
        (meta, left, *rights, received),
        after=after,
        filler=True,
    )


def last_kernel(meta, proj_in, w_out_in, normed, grad, grad_att, heads, out):
    half, columns = out.shape[0], grad.shape[1]
    own = halves(meta, half)[0]
    out[:, :columns] = (dot_tn(normed[:, own], grad[...]) + proj_in[...].astype(F32)).astype(BF16)
    out[:, columns:] = (dot_tn(grad_att[:, own], heads[...]) + w_out_in[...].astype(F32)).astype(BF16)


def pair_last(meta, proj_in, w_out_in, normed, grad, grad_att, heads):
    half, columns = normed.shape[1] // 2, grad.shape[1] + heads.shape[1]
    return call(
        last_kernel,
        shape(half, columns, dtype=BF16),
        (meta, proj_in, w_out_in, normed, grad, grad_att, heads),
        filler=True,
    )


def scattered(value):
    return lax.psum_scatter(value, "ctx", scatter_dimension=0, tiled=True)


def shards(
    tokens, seq_bounds, w_query, w_key, w_value, w_beta, conv_taps, out_gain, w_out,
    attn_gain, ffn_gain, w_gate, w_up, w_down, cotangent,
):
    rows, width = tokens.shape
    half = w_query.shape[0]
    chan = w_query.shape[1]
    heads = w_beta.shape[1]
    dim = out_gain.shape[0]
    units = w_gate.shape[1]
    slots = lax.axis_size("tp")
    count = rows // slots
    core, place, member = lax.axis_index("fsdp"), lax.axis_index("ctx"), lax.axis_index("tp")
    meta = jnp.concatenate(
        [
            seq_bounds[0],
            jnp.stack(
                [place * rows, core * half, (1 - core) * half]
                + [(member ^ slot) * count for slot in range(slots)]
            ).astype(jnp.int32),
        ]
    )
    attn_row, ffn_row, out_row = attn_gain[None, :], ffn_gain[None, :], out_gain[None, :]

    rim = shifted(tokens[rows - RIM :], "ctx", 1)
    x_query, x_key, x_value, x_beta = (flipped(w, "fsdp", 1) for w in (w_query, w_key, w_value, w_beta))
    tok_own = lax.dynamic_slice_in_dim(tokens, member * count, count, 0)
    cot_own = lax.dynamic_slice_in_dim(cotangent, member * count, count, 0)

    normed, proj, logits = call(
        project_kernel,
        [shape(rows + RIM, width, dtype=BF16), shape(rows + RIM, 3 * chan), shape(rows, heads)],
        (meta, tokens, rim, attn_row, w_query, w_key, w_value, w_beta, x_query, x_key, x_value, x_beta),
        flops=2 * rows * width * 3 * chan,
    )
    tall, square = shape(heads, rows, dim), shape(heads, dim, dim)
    erase, write, scores, inverse, query_eff, step, prefix, added, query_hat, out_hat, m_total, b_total = call(
        delta_kernel,
        [tall] * 10 + [square] * 2,
        (meta, proj, conv_taps, logits),
        flops=heads * 60 * rows * dim * dim,
    )

    def hop(matrix, extra, state, flip, after=()):
        return call(
            functools.partial(hop_kernel, flip=flip),
            shape(heads, dim, dim, dtype=BF16),
            (matrix, extra, state),
            flops=2 * heads * dim**3,
            scalars=False,
            after=after,
        )

    x_out, x_down, x_gate, x_up = (flipped(w, "fsdp", 1) for w in (w_out, w_down, w_gate, w_up))
    state = jnp.zeros((heads, dim, dim), BF16)
    for index in range(lax.axis_size("ctx") - 1):
        sent = b_total.astype(BF16) if index == 0 else hop(
            m_total, b_total, state, False, (x_out, x_down, x_gate, x_up)
        )
        state = shifted(sent, "ctx", 1)

    piece_shape = shape(count, width, dtype=BF16)
    heads_slot, heads_out, *pieces = call(
        attend_kernel,
        [shape(rows, chan, dtype=BF16), tall] + [piece_shape] * slots,
        (meta, query_hat, out_hat, state, out_row, w_out, x_out),
        flops=2 * rows * width * chan,
        scratch=[VMEM((rows, chan), BF16)],
    )
    grad_low, grad_act = call(
        grad_act_kernel,
        [shape(rows, width, dtype=BF16), shape(rows, units)],
        (meta, cotangent, w_down, x_down),
        flops=2 * rows * width * units,
    )
    hidden, normed_two = call(
        norm_two_kernel,
        [shape(count, width), piece_shape],
        (*exchanged(pieces), tok_own, ffn_row),
        scalars=False,
    )
    normed_slot, act, grad_gate, grad_up, *pieces = call(
        ffn_kernel,
        [
            shape(rows, width, dtype=BF16),
            shape(rows, units, dtype=BF16),
            shape(rows, units, dtype=BF16),
            shape(rows, units, dtype=BF16),
        ]
        + [piece_shape] * slots,
        (meta, *gathered(normed_two), w_gate, x_gate, w_up, x_up, grad_act),
        flops=8 * rows * width * units,
    )
    received = exchanged(pieces)
    down_out, down_in = pair_sent(meta, grad_low, act)
    down_pair = pair_kept(meta, down_in, grad_low, act)
    down_sum = scattered(down_pair)
    down_pieces = call(
        down_kernel,
        [piece_shape] * slots,
        (meta, act, w_down, x_down),
        filler=True,
        after=(down_pair,),
    )
    grad_hidden, grad_att, d_ffn_part = call(
        norm_two_back_kernel,
        [shape(count, width), piece_shape, shape(1, width)],
        (meta, *received, hidden, cot_own, ffn_row),
        after=(down_pieces[0],),
    )
    gu_out, gu_in = pair_sent(meta, normed_slot, grad_gate, grad_up, after=(grad_att,))
    gu_pair = pair_kept(meta, gu_in, normed_slot, grad_gate, grad_up)
    gu_sum = scattered(gu_pair)
    grad_o, d_chunk, d_total, d_head_part, grad_att_slot = call(
        heads_back_kernel,
        [tall, tall, square, shape(1, dim), shape(rows, width, dtype=BF16)],
        (meta, *gathered(grad_att), w_out, x_out, heads_out, out_row, query_eff, query_hat),
        flops=2 * rows * width * chan,
        scratch=[VMEM((rows, chan), F32)],
        after=(gu_pair, down_sum),
    )
    out_own = hidden
    for piece in exchanged(down_pieces):
        out_own = out_own + piece.astype(F32)
    out_own = out_own.astype(BF16)
    out_pieces = gathered(out_own)
    grad_state = jnp.zeros((heads, dim, dim), BF16)
    for index in range(lax.axis_size("ctx") - 1):
        sent = d_total.astype(BF16) if index == 0 else hop(m_total, d_total, grad_state, True)
        grad_state = shifted(sent, "ctx", -1)
    w_out_out, w_out_in = pair_sent(meta, grad_att_slot, heads_slot, after=(d_total,))

    grad_ext, grad_rim, grad_tail, d_conv_part, grad_logit = call(
        delta_back_kernel,
        [
            shape(rows + RIM, 3 * chan, dtype=BF16),
            shape(RIM, 3 * chan),
            shape(RIM, 3 * chan),
            shape(3, TAPS, chan),
            shape(rows, heads, dtype=BF16),
        ],
        (
            meta, proj, conv_taps, logits,
            erase, write, scores, inverse, step, prefix, added, state, grad_state, grad_o, d_chunk,
        ),
        flops=heads * 60 * rows * dim * dim,
        scratch=[VMEM((3 * heads, rows + 2 * RIM, dim), F32)],
        after=(out_own, w_out_out),
    )
    returned = shifted(grad_rim, "ctx", -1)
    pieces = call(
        back_project_kernel,
        [piece_shape] * slots,
        (
            meta, grad_ext, grad_tail, returned, grad_logit,
            w_query, w_key, w_value, w_beta, x_query, x_key, x_value, x_beta,
        ),
        flops=2 * rows * width * 3 * chan,
        scratch=[VMEM((rows, 3 * chan), BF16), VMEM((rows, heads), BF16)],
        after=tuple(out_pieces),
    )
    proj_out, proj_in = pair_sent(meta, normed, grad_ext, after=(pieces[0],))
    proj_pair = pair_last(meta, proj_in, w_out_in, normed, grad_ext, grad_att_slot, heads_slot)
    proj_sum = scattered(proj_pair)
    d_beta_part = contract_rows(grad_logit, normed[RIM:])
    conv_rows_count = 3 * TAPS * chan // width
    early = summed(
        jnp.concatenate([d_ffn_part, jnp.pad(d_head_part, ((0, 0), (0, width - dim)))], axis=0), "tp"
    )
    bundle = jnp.concatenate([early, d_beta_part, d_conv_part.reshape(conv_rows_count, width)], axis=0)
    bundle = summed(summed(bundle, "fsdp"), "ctx")
    d_tok_own, d_attn_part = call(
        norm_one_back_kernel,
        [piece_shape, shape(1, width)],
        (*exchanged(pieces), tok_own, attn_row, grad_hidden),
        scalars=False,
        after=(bundle, proj_pair, gu_sum),
    )
    d_tokens = call(
        place_kernel,
        shape(rows, width, dtype=BF16),
        (meta, *gathered(d_tok_own)),
    )

    out = call(place_kernel, shape(rows, width, dtype=BF16), (meta, *out_pieces), after=(d_tokens,))
    down_sum, gu_sum, proj_sum = (x.astype(F32) for x in (down_sum, gu_sum, proj_sum))

    d_attn = summed(summed(summed(d_attn_part, "tp"), "fsdp"), "ctx")
    share = width // (lax.axis_size("fsdp") * lax.axis_size("ctx"))
    d_beta = lax.dynamic_slice_in_dim(
        bundle[2 : 2 + heads], core * half + place * share, share, 1
    ).T
    return (
        out,
        d_tokens,
        proj_sum[:, :chan],
        proj_sum[:, chan : 2 * chan],
        proj_sum[:, 2 * chan : 3 * chan],
        d_beta,
        bundle[2 + heads :].reshape(3, TAPS, chan),
        bundle[1, :dim],
        proj_sum[:, 3 * chan :],
        d_attn[0],
        bundle[0],
        gu_sum[:, :units],
        gu_sum[:, units:],
        down_sum,
    )


def solution(mesh):
    both = P(("fsdp", "ctx"), None)
    weight = P("fsdp", "tp")
    grad = P(("fsdp", "ctx"), "tp")
    in_specs = (
        both, P("fsdp", None), weight, weight, weight, weight, P(None, None, "tp"), P(), weight,
        P(), P(), weight, weight, weight, both,
    )
    out_specs = (
        both, both, grad, grad, grad, grad, P(None, None, "tp"), P(), grad, P(), P(), grad, grad, grad,
    )
    return jax.shard_map(shards, mesh=mesh, in_specs=in_specs, out_specs=out_specs, check_vma=False)
```

```python
import functools
import math

import jax
import jax.numpy as jnp
from jax import lax
from jax.experimental import pallas as pl
from jax.experimental.pallas import tpu as pltpu
from jax.sharding import PartitionSpec as P

EPS = 1e-06
HIGH = True
F32 = jnp.float32
BF16 = jnp.bfloat16
CHUNK = 128
LANES = 128
RIM = 16
TAPS = 4
VMEM = pltpu.VMEM
WHOLE = pl.BlockSpec(memory_space=pltpu.VMEM)
SCALARS = pl.BlockSpec(memory_space=pltpu.SMEM)


def split(value):
    high = value.astype(BF16)
    return high, (value - high.astype(F32)).astype(BF16)


def product(dims, left, right, exact):
    def one(a, b):
        return lax.dot_general(a, b, (dims, ((), ())), preferred_element_type=F32)

    if not exact:
        return one(left.astype(BF16), right.astype(BF16))
    (left_hi, left_lo), (right_hi, right_lo) = split(left), split(right)
    return one(left_hi, right_hi) + (one(left_hi, right_lo) + one(left_lo, right_hi))


def dot_nn(left, right, exact=False):
    return product(((1,), (0,)), left, right, exact)


def dot_nt(left, right, exact=False):
    return product(((1,), (1,)), left, right, exact)


def dot_tn(left, right, exact=False):
    return product(((0,), (0,)), left, right, exact)


def call(kernel, out_shape, operands, flops=0, scratch=(), scalars=True, after=(), vmem=36):
    outs = out_shape if isinstance(out_shape, list) else [out_shape]
    size = sum(math.prod(x.shape) * x.dtype.itemsize for x in (*operands, *outs))
    given = len(operands)

    def body(*refs):
        kernel(*refs[:given], *refs[given + len(after) :])

    return pl.pallas_call(
        body,
        out_shape=out_shape,
        in_specs=[SCALARS] * scalars
        + [WHOLE] * (given - scalars)
        + [pl.BlockSpec(memory_space=pl.ANY)] * len(after),
        out_specs=[WHOLE] * len(outs) if isinstance(out_shape, list) else WHOLE,
        scratch_shapes=list(scratch),
        name=getattr(kernel, "func", kernel).__name__,
        cost_estimate=pl.CostEstimate(
            flops=flops, bytes_accessed=size, transcendentals=0
        ),
        compiler_params=pltpu.CompilerParams(vmem_limit_bytes=vmem << 20),
    )(*operands, *after)


def shape(*dims, dtype=F32):
    return jax.ShapeDtypeStruct(dims, dtype)


def seg_of(places, meta):
    ids = (
        (places >= meta[0]).astype(jnp.int32)
        + (places >= meta[1]).astype(jnp.int32)
        + (places >= meta[2]).astype(jnp.int32)
    )
    return jnp.where(places < 0, -1, ids)


def row_of(meta, slot, rows):
    return pl.ds(pl.multiple_of(meta[6 + slot], rows), rows)


def halves(meta, half):
    return (
        pl.ds(pl.multiple_of(meta[4], half), half),
        pl.ds(pl.multiple_of(meta[5], half), half),
    )


def project_kernel(meta, tok, rim, gain, wq, wk, wv, wb, xq, xk, xv, xb, ext, proj, logits, ext_oth):
    rows, width = tok.shape
    for source, at, count in ((rim, 0, RIM), (tok, RIM, rows)):
        values = source[...].astype(F32)
        scale = lax.rsqrt(jnp.mean(values * values, axis=-1, keepdims=True) + EPS)
        ext[pl.ds(at, count), :] = (values * scale * gain[...]).astype(BF16)
    own, oth = halves(meta, width // 2)
    left, right = ext[:, own], ext[:, oth]
    ext_oth[...] = right
    chan = wq.shape[1]
    for at, (a, b) in enumerate(((wq, xq), (wk, xk), (wv, xv))):
        proj[:, at * chan : (at + 1) * chan] = dot_nn(left, a[...]) + dot_nn(right, b[...])
    logits[...] = dot_nn(left[RIM:], wb[...]) + dot_nn(right[RIM:], xb[...])


def conv_rows(ext, taps, block, lanes, rows, sames):
    start = block * taps.shape[2]
    columns = slice(start + lanes.start, start + lanes.stop)
    mixed = None
    for j in range(TAPS):
        term = taps[block, j : j + 1, lanes] * ext[RIM - j : RIM - j + rows, columns] * sames[j]
        mixed = term if mixed is None else mixed + term
    return mixed


def tap_masks(meta, rows):
    places = meta[3] + lax.broadcasted_iota(jnp.int32, (rows, 1), 0)
    seg = seg_of(places, meta)
    return places, [(seg_of(places - j, meta) == seg).astype(F32) for j in range(TAPS)]


def pick_column(values, head):
    lane = lax.broadcasted_iota(jnp.int32, values.shape, 1)
    return jnp.sum(jnp.where(lane == head, values, 0.0), axis=1, keepdims=True)


def chunk_masks(meta, at):
    first = meta[3] + at * CHUNK
    row = lax.broadcasted_iota(jnp.int32, (CHUNK, CHUNK), 0)
    col = lax.broadcasted_iota(jnp.int32, (CHUNK, CHUNK), 1)
    seg_col = seg_of(first + lax.broadcasted_iota(jnp.int32, (CHUNK, 1), 0), meta)
    seg_row = seg_of(first + lax.broadcasted_iota(jnp.int32, (1, CHUNK), 1), meta)
    before = seg_of(first - 1, meta)
    last = seg_of(first + CHUNK - 1, meta)
    same = (seg_col == seg_row).astype(F32)
    strict = jnp.where(row > col, same, 0.0)
    lower = jnp.where(row >= col, same, 0.0)
    carry_in = (seg_col == before).astype(F32)
    tail = (seg_col == last).astype(F32)
    whole = (last == before).astype(F32)
    return strict, lower, carry_in, tail, whole


def unit_inverses(grams):
    row = lax.broadcasted_iota(jnp.int32, (CHUNK, CHUNK), 0)
    col = lax.broadcasted_iota(jnp.int32, (CHUNK, CHUNK), 1)
    eye = (row == col).astype(F32)
    size = 8
    near = [jnp.where(row // size == col // size, g, 0.0) for g in grams]
    power = [dot_nn(n, n) for n in near]
    inverse = [eye - n for n in near]
    inverse = [x + dot_nn(x, p) for x, p in zip(inverse, power)]
    power = [dot_nn(p, p) for p in power]
    inverse = [x + dot_nn(x, p) for x, p in zip(inverse, power)]
    while size < CHUNK:
        off = (row // (2 * size) == col // (2 * size)) & (row // size != col // size)
        inner = [dot_nn(jnp.where(off, g, 0.0), x) for g, x in zip(grams, inverse)]
        inverse = [x - dot_nn(x, y) for x, y in zip(inverse, inner)]
        size *= 2
    resid = [(eye - x) - dot_nn(g, x, HIGH) for g, x in zip(grams, inverse)]
    return [x + dot_nn(x, r) for x, r in zip(inverse, resid)]

def silu_parts(mixed):
    sig = jax.nn.sigmoid(mixed)
    return sig, mixed * sig


def unit_parts(values):
    scale = lax.rsqrt(jnp.sum(values * values, axis=-1, keepdims=True) + EPS)
    return scale, values * scale


def delta_kernel(
    meta, ext, taps, logits,
    w_out, u_out, p_out, t_out, qe_out, m_out, mp_out, bp_out, qh_out, oh_out, mtot, btot,
):
    group, rows, width = w_out.shape
    places, sames = tap_masks(meta, rows)
    keep = (places < meta[2]).astype(F32)
    row = lax.broadcasted_iota(jnp.int32, (width, width), 0)
    col = lax.broadcasted_iota(jnp.int32, (width, width), 1)
    eye = (row == col).astype(F32)
    q, k, v, b = [], [], [], []
    for head in range(group):
        lanes = slice(head * width, (head + 1) * width)
        x = silu_parts(conv_rows(ext, taps, 0, lanes, rows, sames))[1]
        q.append(unit_parts(x)[1] * (1.0 / math.sqrt(width)))
        x = silu_parts(conv_rows(ext, taps, 1, lanes, rows, sames))[1]
        k.append(unit_parts(x)[1])
        v.append(silu_parts(conv_rows(ext, taps, 2, lanes, rows, sames))[1])
        b.append(jax.nn.sigmoid(pick_column(logits[...], head)) * keep)
    chunks = rows // CHUNK
    spots = [slice(at * CHUNK, (at + 1) * CHUNK) for at in range(chunks)]
    masks = [chunk_masks(meta, at) for at in range(chunks)]
    chains = [(head, at) for head in range(group) for at in range(chunks)]
    kc = [k[h][spots[a]] for h, a in chains]
    qc = [q[h][spots[a]] for h, a in chains]
    scaled = [b[h][spots[a]] * k[h][spots[a]] for h, a in chains]
    scaled_v = [b[h][spots[a]] * v[h][spots[a]] for h, a in chains]
    grams = [dot_nt(s, x, HIGH) * masks[a][0] for (h, a), s, x in zip(chains, scaled, kc)]
    scores = [dot_nt(y, x, HIGH) * masks[a][1] for (h, a), y, x in zip(chains, qc, kc)]
    inverse = unit_inverses(grams)
    both = [dot_nn(t, jnp.concatenate([s, u], axis=1), HIGH) for t, s, u in zip(inverse, scaled, scaled_v)]
    inner = [
        jnp.concatenate([masks[a][2] * x[:, :width], x[:, width:]], axis=1) for (h, a), x in zip(chains, both)
    ]
    states = [dot_tn(x, masks[a][3] * y, HIGH) for (h, a), x, y in zip(chains, kc, inner)]
    reach = [dot_nn(s, y, HIGH) for s, y in zip(scores, inner)]
    steps = [masks[a][4] * eye - s[:, :width] for (h, a), s in zip(chains, states)]
    query = [masks[a][2] * x - y[:, :width] for (h, a), x, y in zip(chains, qc, reach)]
    for i, (h, a) in enumerate(chains):
        w_out[h, spots[a], :] = both[i][:, :width]
        u_out[h, spots[a], :] = both[i][:, width:]
        p_out[h, spots[a], :] = scores[i]
        t_out[h, spots[a], :] = inverse[i]
        qe_out[h, spots[a], :] = query[i]
        m_out[h, spots[a], :] = steps[i]
    prefix = [eye] * group
    added = [jnp.zeros((width, width), F32)] * group
    for a in range(chunks):
        for h in range(group):
            i = h * chunks + a
            mp_out[h, spots[a], :] = prefix[h]
            bp_out[h, spots[a], :] = added[h]
            if a == 0:
                qh_out[h, spots[a], :] = query[i]
                oh_out[h, spots[a], :] = reach[i][:, width:]
                prefix[h], added[h] = steps[i], states[i][:, width:]
                continue
            out = dot_nn(
                jnp.concatenate([query[i], steps[i]], axis=0),
                jnp.concatenate([prefix[h], added[h]], axis=1),
                HIGH,
            )
            qh_out[h, spots[a], :] = out[:CHUNK, :width]
            oh_out[h, spots[a], :] = out[:CHUNK, width:] + reach[i][:, width:]
            prefix[h], added[h] = out[CHUNK:, :width], out[CHUNK:, width:] + states[i][:, width:]
    for h in range(group):
        mtot[h] = prefix[h]
        btot[h] = added[h]


def hop_kernel(step, extra, state, out, *, flip):
    for head in range(step.shape[0]):
        value = state[head].astype(F32)
        product = dot_tn(step[head], value, HIGH) if flip else dot_nn(step[head], value, HIGH)
        out[head] = (product + extra[head]).astype(BF16)


def chain_kernel(first, second, out):
    for head in range(first.shape[0]):
        out[head] = dot_nn(second[head], first[head], HIGH)


def attend_kernel(meta, qh, oh, state, gain, w_own, w_oth, heads_slot, o_out, *rest):
    pieces, low = rest[:-1], rest[-1]
    heads, rows, width = qh.shape
    for head in range(heads):
        out = dot_nn(qh[head], state[head].astype(F32), HIGH) + oh[head]
        o_out[head] = out
        scale = lax.rsqrt(jnp.mean(out * out, axis=-1, keepdims=True) + EPS)
        low[:, head * width : (head + 1) * width] = (out * scale * gain[...]).astype(BF16)
    count = rows // len(pieces)
    own, oth = halves(meta, w_own.shape[0])
    for slot, piece in enumerate(pieces):
        part = low[row_of(meta, slot, count), :]
        heads_slot[pl.ds(slot * count, count), :] = part
        piece[:, own] = dot_nt(part, w_own[...]).astype(BF16)
        piece[:, oth] = dot_nt(part, w_oth[...]).astype(BF16)


def norm_two_kernel(a, b, c, d, tok, gain, hidden_out, normed_out):
    total = a[...].astype(F32) + b[...].astype(F32) + c[...].astype(F32) + d[...].astype(F32)
    hidden = tok[...].astype(F32) + total
    scale = lax.rsqrt(jnp.mean(hidden * hidden, axis=-1, keepdims=True) + EPS)
    hidden_out[...] = hidden
    normed_out[...] = (hidden * scale * gain[...]).astype(BF16)


def add_kernel(mine, came, hidden, out):
    out[...] = (hidden[...] + (mine[...] + came[...].astype(F32))).astype(BF16)


def norm_back(grad, values, gain):
    scale = lax.rsqrt(jnp.mean(values * values, axis=-1, keepdims=True) + EPS)
    normal = values * scale
    hat = grad * gain
    back = scale * (hat - normal * jnp.mean(hat * normal, axis=-1, keepdims=True))
    return back, jnp.sum(grad * normal, axis=0, keepdims=True)


def norm_two_back_kernel(meta, a, b, c, d, hidden, cot, gain, grad_hidden, grad_att, d_gain):
    total = a[...].astype(F32) + b[...].astype(F32) + c[...].astype(F32) + d[...].astype(F32)
    back, d_gain[...] = norm_back(total, hidden[...], gain[...])
    places = meta[3] + meta[6] + lax.broadcasted_iota(jnp.int32, (hidden.shape[0], 1), 0)
    grad = cot[...].astype(F32) * (places < meta[2]).astype(F32) + back
    grad_hidden[...] = grad
    grad_att[...] = grad.astype(BF16)


def norm_one_back_kernel(a, b, c, d, tok, gain, grad_hidden, d_ffn, d_head, d_tok):
    total = a[...].astype(F32) + b[...].astype(F32) + c[...].astype(F32) + d[...].astype(F32)
    back, d_gain = norm_back(total, tok[...].astype(F32), gain[...])
    rows, width = tok.shape
    d_tok[pl.ds(0, rows), :] = (grad_hidden[...] + back).astype(BF16)
    line = lax.broadcasted_iota(jnp.int32, (RIM, width), 0)
    head = jnp.concatenate([d_head[...], jnp.zeros((1, width - d_head.shape[1]), F32)], axis=1)
    sums = jnp.where(line == 0, d_gain, jnp.where(line == 1, d_ffn[...], jnp.where(line == 2, head, 0.0)))
    d_tok[pl.ds(rows, RIM), :] = sums.astype(BF16)


def copy_kernel(value, out):
    out[...] = value[...]


def place_last_kernel(meta, a, b, c, d, out, sums):
    rows = a.shape[0] - RIM
    total = None
    for slot, piece in enumerate((a, b, c, d)):
        out[row_of(meta, slot, rows), :] = piece[pl.ds(0, rows), :]
        part = piece[pl.ds(rows, RIM), :].astype(F32)
        total = part if total is None else total + part
    sums[...] = total[: sums.shape[0]]


def place_kernel(meta, a, b, c, d, out):
    rows = a.shape[0]
    for slot, piece in enumerate((a, b, c, d)):
        out[row_of(meta, slot, rows), :] = piece[...]


def grad_act_kernel(meta, cot, w_own, w_oth, low_out, act_out, low_oth):
    rows, width = cot.shape
    slots = 4
    count = rows // slots
    for slot in range(slots):
        at = row_of(meta, slot, count)
        places = meta[3] + meta[6 + slot] + lax.broadcasted_iota(jnp.int32, (count, 1), 0)
        keep = (places < meta[2]).astype(F32)
        low_out[pl.ds(slot * count, count), :] = (cot[at, :].astype(F32) * keep).astype(BF16)
    own, oth = halves(meta, width // 2)
    low_oth[...] = low_out[:, oth]

    @pl.loop(0, 2)
    def _(step):
        at = pl.ds(pl.multiple_of(step * (rows // 2), rows // 2), rows // 2)
        act_out[at, :] = dot_nn(low_out[at, own], w_own[...]) + dot_nn(low_out[at, oth], w_oth[...])


def ffn_kernel(meta, a, b, c, d, g_own, g_oth, u_own, u_oth, grad_act, n_out, n_oth, wide_out, *pieces):
    count, width = a.shape
    for slot, source in enumerate((a, b, c, d)):
        n_out[pl.ds(slot * count, count), :] = source[...]
    own, oth = halves(meta, width // 2)
    n_oth[...] = n_out[:, oth]
    units = g_own.shape[1]
    for part in range(2):
        at = pl.ds(part * 2 * count, 2 * count)
        left, right = n_out[at, own], n_out[at, oth]
        gate = dot_nn(left, g_own[...]) + dot_nn(right, g_oth[...])
        up = dot_nn(left, u_own[...]) + dot_nn(right, u_oth[...])
        sig = jax.nn.sigmoid(gate)
        wide_out[at, :units] = (gate * sig * up).astype(BF16)
        grad = grad_act[at, :]
        grad_gate = (grad * up * sig * (1.0 + gate * (1.0 - sig))).astype(BF16)
        grad_up = (grad * gate * sig).astype(BF16)
        wide_out[at, units : 2 * units] = grad_gate
        wide_out[at, 2 * units :] = grad_up
        for side, gate_side, up_side in ((own, g_own, u_own), (oth, g_oth, u_oth)):
            total = (dot_nt(grad_gate, gate_side[...]) + dot_nt(grad_up, up_side[...])).astype(BF16)
            pieces[2 * part][:, side] = total[:count]
            pieces[2 * part + 1][:, side] = total[count:]


def down_kernel(meta, wide, w_own, w_oth, keep, give):
    act = wide[:, : w_own.shape[1]]
    count = keep.shape[0] // 2
    own, oth = halves(meta, w_own.shape[0])
    for side, weight in ((own, w_own), (oth, w_oth)):
        total = dot_nt(act, weight[...]).astype(BF16)
        for slot, out in enumerate((keep, give, keep, give)):
            out[pl.ds(slot // 2 * count, count), side] = total[slot * count : (slot + 1) * count]


def add_half_kernel(keep, came, mine, other):
    count = mine.shape[0]
    total = keep[...].astype(F32) + came[...].astype(F32)
    mine[...] = total[:count]
    other[...] = total[count:].astype(BF16)


def heads_back_kernel(
    meta, g0, g1, g2, g3, w_own, w_oth, o_in, gain, qe, qh, grad_o, d_chunk, d_total, d_gain, cat_out, cat_oth, grad
):
    heads, rows, width = o_in.shape
    count = g0.shape[0]
    own, oth = halves(meta, w_own.shape[0])
    for slot, source in enumerate((g0, g1, g2, g3)):
        cat_out[pl.ds(slot * count, count), :] = source[...]
    cat_oth[...] = cat_out[:, oth]
    whole = dot_nn(cat_out[:, own], w_own[...]) + dot_nn(cat_out[:, oth], w_oth[...])
    for slot in range(4):
        grad[row_of(meta, slot, count), :] = whole[slot * count : (slot + 1) * count]
    total_gain = jnp.zeros((1, width), F32)
    for head in range(heads):
        out = o_in[head]
        back, part = norm_back(grad[:, head * width : (head + 1) * width], out, gain[...])
        total_gain = total_gain + part
        grad_o[head] = back
        d_total[head] = dot_tn(qh[head], back, HIGH)
        for at in range(rows // CHUNK):
            here = slice(at * CHUNK, (at + 1) * CHUNK)
            d_chunk[head, here, :] = dot_tn(qe[head, here, :], back[here], HIGH)
    d_gain[...] = total_gain


def delta_back_kernel(
    meta, ext, taps, logits,
    w_in, u_in, p_in, t_in, m_in, mp_in, bp_in, s_in, do_in, dc_in, *rest,
):
    grads_in, rest = rest[:-5], rest[-5:]
    grad_ext, grad_rim, grad_tail, d_taps, pad = rest
    group, rows, width = w_in.shape
    places, sames = tap_masks(meta, rows)
    keep = (places < meta[2]).astype(F32)
    root = 1.0 / math.sqrt(width)
    chunks = rows // CHUNK
    spots = [slice(at * CHUNK, (at + 1) * CHUNK) for at in range(chunks)]
    masks = [chunk_masks(meta, at) for at in range(chunks)]
    chains = [(head, at) for head in range(group) for at in range(chunks)]
    q, k, v, b, sig_b, scale_q, scale_k = [], [], [], [], [], [], []
    for head in range(group):
        lanes = slice(head * width, (head + 1) * width)
        scale, unit = unit_parts(silu_parts(conv_rows(ext, taps, 0, lanes, rows, sames))[1])
        scale_q.append(scale)
        q.append(unit)
        scale, unit = unit_parts(silu_parts(conv_rows(ext, taps, 1, lanes, rows, sames))[1])
        scale_k.append(scale)
        k.append(unit)
        v.append(silu_parts(conv_rows(ext, taps, 2, lanes, rows, sames))[1])
        sig_b.append(jax.nn.sigmoid(pick_column(logits[...], head)))
        b.append(sig_b[head] * keep)
    after = {}
    for head in range(group):
        total = grads_in[0][head].astype(F32)
        for grad, step in zip(grads_in[1 : (len(grads_in) + 1) // 2], grads_in[(len(grads_in) + 1) // 2 :]):
            total = total + dot_tn(step[head], grad[head].astype(F32), HIGH)
        after[head, chunks - 1] = total
    for at in range(chunks - 1, 0, -1):
        for head in range(group):
            after[head, at - 1] = dot_tn(m_in[head, spots[at], :], after[head, at], HIGH) + dc_in[head, spots[at], :]
    grad_state = [after[c] for c in chains]
    state = [dot_nn(mp_in[h, spots[a], :], s_in[h].astype(F32), HIGH) + bp_in[h, spots[a], :] for h, a in chains]
    kc = [k[h][spots[a]] for h, a in chains]
    grad_o = [do_in[h, spots[a], :] for h, a in chains]
    fresh = [
        u_in[h, spots[a], :] - masks[a][2] * dot_nn(w_in[h, spots[a], :], s, HIGH)
        for (h, a), s in zip(chains, state)
    ]
    d_fresh = [
        dot_tn(p_in[h, spots[a], :], g, HIGH) + masks[a][3] * dot_nn(x, s, HIGH)
        for (h, a), g, x, s in zip(chains, grad_o, kc, grad_state)
    ]
    d_scores = [dot_nt(g, f, HIGH) * masks[a][1] for (h, a), g, f in zip(chains, grad_o, fresh)]
    back = [
        dot_nt(jnp.concatenate([masks[a][2] * g, masks[a][2] * f], axis=0), s, HIGH)
        for (h, a), g, f, s in zip(chains, grad_o, d_fresh, state)
    ]
    d_q = [x[:CHUNK] + dot_nn(d, y, HIGH) for x, d, y in zip(back, d_scores, kc)]
    d_k = [
        root * dot_tn(d, q[h][spots[a]], HIGH) + dot_nt(masks[a][3] * f, s, HIGH)
        for (h, a), d, f, s in zip(chains, d_scores, fresh, grad_state)
    ]
    right = [
        dot_tn(t_in[h, spots[a], :], jnp.concatenate([-x[CHUNK:], f], axis=1), HIGH)
        for (h, a), x, f in zip(chains, back, d_fresh)
    ]
    d_gram = [
        -masks[a][0] * dot_nt(r, jnp.concatenate([w_in[h, spots[a], :], u_in[h, spots[a], :]], axis=1), HIGH)
        for (h, a), r in zip(chains, right)
    ]
    d_scaled = [r[:, :width] + dot_nn(g, x, HIGH) for r, g, x in zip(right, d_gram, kc)]
    d_k = [
        x + dot_tn(g, b[h][spots[a]] * y, HIGH) + b[h][spots[a]] * d
        for (h, a), x, g, y, d in zip(chains, d_k, d_gram, kc, d_scaled)
    ]
    d_b = [
        jnp.sum(d * y + r[:, width:] * v[h][spots[a]], axis=1, keepdims=True)
        for (h, a), d, y, r in zip(chains, d_scaled, kc, right)
    ]
    d_v = [b[h][spots[a]] * r[:, width:] for (h, a), r in zip(chains, right)]
    lane = lax.broadcasted_iota(jnp.int32, (rows, LANES), 1)
    all_logits = jnp.zeros((rows, LANES), F32)
    zeros = jnp.zeros((RIM, width), F32)
    heads_width = grad_ext.shape[1] // 3 // LANES * LANES
    for head in range(group):
        mine = slice(head * chunks, (head + 1) * chunks)
        lanes = slice(head * width, (head + 1) * width)
        d_logit = jnp.concatenate(d_b[mine], axis=0) * keep * sig_b[head] * (1.0 - sig_b[head])
        all_logits = jnp.where(lane == head, d_logit, all_logits)
        g_q, g_k, g_v = (jnp.concatenate(x[mine], axis=0) for x in (d_q, d_k, d_v))
        g_q = root * scale_q[head] * (g_q - q[head] * jnp.sum(g_q * q[head], axis=-1, keepdims=True))
        g_k = scale_k[head] * (g_k - k[head] * jnp.sum(g_k * k[head], axis=-1, keepdims=True))
        for block, grad in enumerate((g_q, g_k, g_v)):
            spot = head * 3 + block
            at = slice(block * heads_width + head * width, block * heads_width + (head + 1) * width)
            pad[spot, pl.ds(0, RIM), :] = zeros
            pad[spot, pl.ds(RIM + rows, RIM), :] = zeros
            mixed = conv_rows(ext, taps, block, lanes, rows, sames)
            sig = silu_parts(mixed)[0]
            d_mixed = grad * sig * (1.0 + mixed * (1.0 - sig))
            total = jnp.zeros((rows + RIM, width), F32)
            for j in range(TAPS):
                masked = d_mixed * sames[j]
                pad[spot, pl.ds(RIM, rows), :] = masked
                total = total + taps[block, j : j + 1, lanes] * pad[spot, pl.ds(j, rows + RIM), :]
                d_taps[block, j : j + 1, lanes] = jnp.sum(
                    masked * ext[RIM - j : RIM - j + rows, at], axis=0, keepdims=True
                )
            grad_ext[:, at] = total.astype(BF16)
            grad_rim[:, at] = total[:RIM]
            grad_tail[:, at] = total[rows:]
    grad_ext[pl.ds(RIM, rows), 3 * heads_width :] = all_logits.astype(BF16)
    grad_ext[pl.ds(0, RIM), 3 * heads_width :] = jnp.zeros((RIM, LANES), BF16)


def back_project_kernel(
    meta, grad_ext, tail, returned, wq, wk, wv, wb, xq, xk, xv, xb, *rest
):
    pieces, grad = rest[:-1], rest[-1]
    count = pieces[0].shape[0]
    chan = wq.shape[1]
    for slot in range(len(pieces)):
        here = pl.ds(slot * count, count)
        start = pl.multiple_of(meta[6 + slot], count)
        grad[here, :] = grad_ext[pl.ds(pl.multiple_of(start + RIM, RIM), count), :]
    last = pl.multiple_of(meta[6 + len(pieces) - 1] + count - RIM, RIM)
    grad[pl.ds(last, RIM), : 3 * chan] = (tail[...] + returned[...]).astype(BF16)
    own, oth = halves(meta, wq.shape[0])
    for side, weights in ((own, (wq, wk, wv, wb)), (oth, (xq, xk, xv, xb))):
        total = dot_nt(grad[:, 3 * chan : 3 * chan + weights[3].shape[1]], weights[3][...])
        for block in range(3):
            total = total + dot_nt(grad[:, block * chan : (block + 1) * chan], weights[block][...])
        total = total.astype(BF16)
        for slot, piece in enumerate(pieces):
            piece[:, side] = total[slot * count : (slot + 1) * count]


def ffn_grad_kernel(meta, low, low_sib, normed, normed_sib, wide, wide_sib, out):
    own = halves(meta, out.shape[0])[0]
    units = wide.shape[1] // 3
    lows = jnp.concatenate([low[:, own], low_sib[...]], axis=0)
    norms = jnp.concatenate([normed[:, own], normed_sib[...]], axis=0)
    for at, left in enumerate((lows, norms, norms)):
        here = slice(at * units, (at + 1) * units)
        out[:, here] = dot_tn(left, jnp.concatenate([wide[:, here], wide_sib[:, here]], axis=0)).astype(BF16)


def proj_grad_kernel(
    meta, normed, grad, normed_sib, grad_sib, grad_att, heads, grad_att_sib, heads_sib, out
):
    half, columns = out.shape[0], grad.shape[1]
    own = halves(meta, half)[0]
    out[:, :columns] = (
        dot_tn(normed[:, own], grad[...]) + dot_tn(normed_sib[...], grad_sib[...])
    ).astype(BF16)
    out[:, columns:] = (
        dot_tn(grad_att[:, own], heads[...]) + dot_tn(grad_att_sib[...], heads_sib[...])
    ).astype(BF16)


def flipped(value, axis, bit):
    return lax.ppermute(value, axis, [(i, i ^ bit) for i in range(lax.axis_size(axis))])


def shifted(value, axis, by, reach=None):
    length = lax.axis_size(axis)
    pairs = [(i, i + by) for i in range(length) if 0 <= i + by < length]
    if reach is not None:
        pairs = [pair for pair in pairs if reach(pair[0])]
    return lax.ppermute(value, axis, pairs)


def exchanged(pieces):
    return [pieces[0]] + [flipped(piece, "tp", slot) for slot, piece in enumerate(pieces) if slot]


def gathered(piece):
    return [piece] + [flipped(piece, "tp", slot) for slot in range(1, lax.axis_size("tp"))]


def summed(value, axis):
    bit = 1
    while bit < lax.axis_size(axis):
        value = value + flipped(value, axis, bit)
        bit *= 2
    return value


def contract_rows(left_side, right_side):
    return lax.dot_general(
        left_side, right_side, (((0,), (0,)), ((), ())), preferred_element_type=F32
    )


def scattered(value):
    return lax.psum_scatter(value, "ctx", scatter_dimension=0, tiled=True)


def line_kernel(meta, value, *rest, step, last):
    rights, lefts = rest[-2:]
    rows = rights.shape[0]
    place = meta[meta.shape[0] - 1]
    for out, due, came in zip((rights, lefts), (last - step + place, place - last + step), rest[:-2] or (None, None)):
        start = pl.multiple_of(jnp.clip(due, 0, last) * rows, rows)
        part = value[pl.ds(start, rows), :]
        if came is not None:
            part = (part.astype(F32) + came[...].astype(F32)).astype(BF16)
        out[...] = part


def line_step(meta, value, step, came, after=()):
    last = lax.axis_size("ctx") - 1
    part = shape(value.shape[0] // (last + 1), value.shape[1], dtype=BF16)
    right, left = call(
        functools.partial(line_kernel, step=step, last=last), [part, part], (meta, value, *came), after=after
    )
    return right, (
        shifted(right, "ctx", 1, lambda i: i <= step),
        shifted(left, "ctx", -1, lambda i: i >= last - step),
    )


def line_total(value, place, came):
    rows = value.shape[0] // lax.axis_size("ctx")
    total = lax.dynamic_slice_in_dim(value, place * rows, rows, 0).astype(F32)
    return total + came[0].astype(F32) + came[1].astype(F32)


def shards(
    tokens, seq_bounds, w_query, w_key, w_value, w_beta, conv_taps, out_gain, w_out,
    attn_gain, ffn_gain, w_gate, w_up, w_down, cotangent,
):
    rows, width = tokens.shape
    half = w_query.shape[0]
    chan = w_query.shape[1]
    heads = w_beta.shape[1]
    dim = out_gain.shape[0]
    units = w_gate.shape[1]
    slots = lax.axis_size("tp")
    count = rows // slots
    core, place, member = lax.axis_index("fsdp"), lax.axis_index("ctx"), lax.axis_index("tp")
    meta = jnp.concatenate(
        [
            seq_bounds[0],
            jnp.stack(
                [place * rows, core * half, (1 - core) * half]
                + [(member ^ slot) * count for slot in range(slots)]
                + [place]
            ).astype(jnp.int32),
        ]
    )
    attn_row, ffn_row, out_row = attn_gain[None, :], ffn_gain[None, :], out_gain[None, :]

    rim = shifted(tokens[rows - RIM :], "ctx", 1)
    x_query, x_key, x_value, x_beta = (flipped(w, "fsdp", 1) for w in (w_query, w_key, w_value, w_beta))
    tok_own = lax.dynamic_slice_in_dim(tokens, member * count, count, 0)
    cot_own = lax.dynamic_slice_in_dim(cotangent, member * count, count, 0)

    normed, proj, logits, normed_oth = call(
        project_kernel,
        [
            shape(rows + RIM, width, dtype=BF16),
            shape(rows + RIM, 3 * chan),
            shape(rows, heads),
            shape(rows + RIM, half, dtype=BF16),
        ],
        (meta, tokens, rim, attn_row, w_query, w_key, w_value, w_beta, x_query, x_key, x_value, x_beta),
        flops=2 * rows * width * 3 * chan,
        vmem=58,
    )
    later = lax.optimization_barrier((w_out, w_down, w_gate, w_up, normed_oth))
    x_out, x_down, x_gate, x_up = (flipped(w, "fsdp", 1) for w in later[:4])
    normed_oth = later[4]
    tall, square = shape(heads, rows, dim), shape(heads, dim, dim)
    erase, write, scores, inverse, query_eff, step, prefix, added, query_hat, out_hat, m_total, b_total = call(
        delta_kernel,
        [tall] * 10 + [square] * 2,
        (meta, proj, conv_taps, logits),
        flops=heads * 60 * rows * dim * dim,
        vmem=58,
    )

    def hop(matrix, extra, state, flip, after=()):
        return call(
            functools.partial(hop_kernel, flip=flip),
            shape(heads, dim, dim, dtype=BF16),
            (matrix, extra, state),
            flops=2 * heads * dim**3,
            scalars=False,
            after=after,
        )

    state = jnp.zeros((heads, dim, dim), BF16)
    for index in range(lax.axis_size("ctx") - 1):
        sent = b_total.astype(BF16) if index == 0 else hop(m_total, b_total, state, False)
        state = shifted(sent, "ctx", 1)

    piece_shape = shape(count, width, dtype=BF16)
    normed_sib = flipped(normed_oth, "fsdp", 1)
    heads_slot, heads_out, *pieces = call(
        attend_kernel,
        [shape(rows, chan, dtype=BF16), tall] + [piece_shape] * slots,
        (meta, query_hat, out_hat, state, out_row, w_out, x_out),
        flops=2 * rows * width * chan,
        after=(x_down, x_gate, x_up, normed_sib),
        scratch=[VMEM((rows, chan), BF16)],
    )
    grad_low, grad_act, low_oth = call(
        grad_act_kernel,
        [shape(rows, width, dtype=BF16), shape(rows, units), shape(rows, half, dtype=BF16)],
        (meta, cotangent, w_down, x_down),
        flops=2 * rows * width * units,
        after=(heads_slot,),
    )
    heads_sib, low_sib = flipped(heads_slot, "fsdp", 1), flipped(low_oth, "fsdp", 1)
    hidden, normed_two = call(
        norm_two_kernel,
        [shape(count, width), piece_shape],
        (*exchanged(pieces), tok_own, ffn_row),
        scalars=False,
        after=(heads_sib,),
    )
    maps = None
    if lax.axis_size("ctx") == 4:
        near = shifted(m_total, "ctx", -1)
        chained = call(chain_kernel, square, (m_total, near), scalars=False, after=(normed_two,))
        maps = (near, shifted(chained, "ctx", -1))
    normed_slot, two_oth, wide, *pieces = call(
        ffn_kernel,
        [
            shape(rows, width, dtype=BF16),
            shape(rows, half, dtype=BF16),
            shape(rows, 3 * units, dtype=BF16),
        ]
        + [piece_shape] * slots,
        (meta, *gathered(normed_two), w_gate, x_gate, w_up, x_up, grad_act),
        flops=8 * rows * width * units,
        after=(*(maps or ()), low_sib),
    )
    two_sib, wide_sib = flipped(two_oth, "fsdp", 1), flipped(wide, "fsdp", 1)
    received = exchanged(pieces)
    grad_hidden, grad_att, d_ffn_part = call(
        norm_two_back_kernel,
        [shape(count, width), piece_shape, shape(1, width)],
        (meta, *received, hidden, cot_own, ffn_row),
    )
    ffn_pair = call(
        ffn_grad_kernel,
        shape(half, 3 * units, dtype=BF16),
        (meta, grad_low, low_sib, normed_slot, two_sib, wide, wide_sib),
        flops=4 * rows * half * 3 * units,
    )
    ffn_sum = scattered(ffn_pair)
    down_keep, down_give = call(
        down_kernel,
        [shape(2 * count, width, dtype=BF16)] * 2,
        (meta, wide, w_down, x_down),
        flops=2 * rows * width * units,
        after=(grad_att,),
    )
    grad_o, d_chunk, d_total, d_head_part, grad_att_slot, att_oth = call(
        heads_back_kernel,
        [tall, tall, square, shape(1, dim), shape(rows, width, dtype=BF16), shape(rows, half, dtype=BF16)],
        (meta, *gathered(grad_att), w_out, x_out, heads_out, out_row, query_eff, query_hat),
        flops=2 * rows * width * chan,
        scratch=[VMEM((rows, chan), F32)],
        after=(ffn_pair, down_keep),
    )
    if maps is None:
        grad_state = jnp.zeros((heads, dim, dim), BF16)
        for index in range(lax.axis_size("ctx") - 1):
            sent = d_total.astype(BF16) if index == 0 else hop(m_total, d_total, grad_state, True)
            grad_state = shifted(sent, "ctx", -1)
        gathered_grads = (grad_state,)
    else:
        sent = d_total.astype(BF16)
        gathered_grads = tuple(shifted(sent, "ctx", -by) for by in range(1, lax.axis_size("ctx")))
    down_mine, down_other = call(
        add_half_kernel,
        [shape(count, width), piece_shape],
        (down_keep, flipped(down_give, "tp", 1)),
        scalars=False,
        after=(d_total,),
    )
    att_sib = flipped(att_oth, "fsdp", 1)

    grad_ext, grad_rim, grad_tail, d_conv_part = call(
        delta_back_kernel,
        [
            shape(rows + RIM, 3 * chan + LANES, dtype=BF16),
            shape(RIM, 3 * chan),
            shape(RIM, 3 * chan),
            shape(3, TAPS, chan),
        ],
        (
            meta, proj, conv_taps, logits,
            erase, write, scores, inverse, step, prefix, added, state, grad_o, d_chunk,
            *gathered_grads, *(maps or ()),
        ),
        flops=heads * 60 * rows * dim * dim,
        scratch=[VMEM((3 * heads, rows + 2 * RIM, dim), F32)],
        after=(att_sib, down_other),
    )
    returned = shifted(grad_rim, "ctx", -1)
    grad_sib = flipped(grad_ext, "fsdp", 1)
    out_own = call(add_kernel, piece_shape, (down_mine, flipped(down_other, "tp", 2), hidden), scalars=False)
    pieces = call(
        back_project_kernel,
        [piece_shape] * slots,
        (
            meta, grad_ext, grad_tail, returned,
            w_query, w_key, w_value, w_beta, x_query, x_key, x_value, x_beta,
        ),
        flops=2 * rows * width * 3 * chan,
        scratch=[VMEM((rows, 3 * chan + LANES), BF16)],
    )
    proj_pair = call(
        proj_grad_kernel,
        shape(half, 4 * chan + LANES, dtype=BF16),
        (meta, normed, grad_ext, normed_sib, grad_sib, grad_att_slot, heads_slot, att_sib, heads_sib),
        flops=4 * rows * half * 4 * chan,
        after=(pieces[0], out_own),
    )
    sent, came = line_step(meta, proj_pair, 0, ())
    d_tok_own = call(
        norm_one_back_kernel,
        shape(count + RIM, width, dtype=BF16),
        (*exchanged(pieces), tok_own, attn_row, grad_hidden, d_ffn_part, d_head_part),
        scalars=False,
        after=came,
    )
    for step in range(1, lax.axis_size("ctx") - 1):
        sent, came = line_step(meta, proj_pair, step, came, after=() if step == 1 else (d_tokens,))
        if step == 1:
            d_tokens, gains = call(
                place_last_kernel,
                [shape(rows, width, dtype=BF16), shape(8, width)],
                (meta, *gathered(d_tok_own)),
                after=(ffn_sum,),
            )
    out_late = call(copy_kernel, piece_shape, (out_own,), scalars=False, after=(d_tokens, sent))
    out = call(place_kernel, shape(rows, width, dtype=BF16), (meta, *gathered(out_late)), after=came)
    conv_rows_count = 3 * TAPS * chan // width
    bundle = summed(
        jnp.concatenate([gains, d_conv_part.reshape(conv_rows_count, width)], axis=0), "fsdp"
    )
    bundle = call(copy_kernel, shape(8 + conv_rows_count, width), (bundle,), scalars=False, after=(out,))
    bundle = summed(bundle, "ctx")
    proj_sum, ffn_sum = line_total(proj_pair, place, came), ffn_sum.astype(F32)
    return (
        out,
        d_tokens,
        proj_sum[:, :chan],
        proj_sum[:, chan : 2 * chan],
        proj_sum[:, 2 * chan : 3 * chan],
        proj_sum[:, 3 * chan : 3 * chan + heads],
        bundle[8:].reshape(3, TAPS, chan),
        bundle[2, :dim],
        proj_sum[:, 3 * chan + LANES :],
        bundle[0],
        bundle[1],
        ffn_sum[:, units : 2 * units],
        ffn_sum[:, 2 * units :],
        ffn_sum[:, :units],
    )


def solution(mesh):
    both = P(("fsdp", "ctx"), None)
    weight = P("fsdp", "tp")
    grad = P(("fsdp", "ctx"), "tp")
    in_specs = (
        both, P("fsdp", None), weight, weight, weight, weight, P(None, None, "tp"), P(), weight,
        P(), P(), weight, weight, weight, both,
    )
    out_specs = (
        both, both, grad, grad, grad, grad, P(None, None, "tp"), P(), grad, P(), P(), grad, grad, grad,
    )
    return jax.shard_map(shards, mesh=mesh, in_specs=in_specs, out_specs=out_specs, check_vma=False)
```

```python
import functools
import math

import jax
import jax.numpy as jnp
from jax import lax
from jax.experimental import pallas as pl
from jax.experimental.pallas import tpu as pltpu
from jax.sharding import PartitionSpec as P

EPS = 1e-06
HIGH = True
F32 = jnp.float32
BF16 = jnp.bfloat16
CHUNK = 128
LANES = 128
RIM = 16
TAPS = 4
VMEM = pltpu.VMEM
WHOLE = pl.BlockSpec(memory_space=pltpu.VMEM)
SCALARS = pl.BlockSpec(memory_space=pltpu.SMEM)


def split(value):
    high = value.astype(BF16)
    return high, (value - high.astype(F32)).astype(BF16)


def product(dims, left, right, exact):
    def one(a, b):
        return lax.dot_general(a, b, (dims, ((), ())), preferred_element_type=F32)

    if not exact:
        return one(left.astype(BF16), right.astype(BF16))
    (left_hi, left_lo), (right_hi, right_lo) = split(left), split(right)
    return one(left_hi, right_hi) + (one(left_hi, right_lo) + one(left_lo, right_hi))


def dot_nn(left, right, exact=False):
    return product(((1,), (0,)), left, right, exact)


def dot_nt(left, right, exact=False):
    return product(((1,), (1,)), left, right, exact)


def dot_tn(left, right, exact=False):
    return product(((0,), (0,)), left, right, exact)


def call(kernel, out_shape, operands, flops=0, scratch=(), scalars=True, after=(), vmem=36):
    outs = out_shape if isinstance(out_shape, list) else [out_shape]
    size = sum(math.prod(x.shape) * x.dtype.itemsize for x in (*operands, *outs))
    given = len(operands)

    def body(*refs):
        kernel(*refs[:given], *refs[given + len(after) :])

    return pl.pallas_call(
        body,
        out_shape=out_shape,
        in_specs=[SCALARS] * scalars
        + [WHOLE] * (given - scalars)
        + [pl.BlockSpec(memory_space=pl.ANY)] * len(after),
        out_specs=[WHOLE] * len(outs) if isinstance(out_shape, list) else WHOLE,
        scratch_shapes=list(scratch),
        name=getattr(kernel, "func", kernel).__name__,
        cost_estimate=pl.CostEstimate(
            flops=flops, bytes_accessed=size, transcendentals=0
        ),
        compiler_params=pltpu.CompilerParams(vmem_limit_bytes=vmem << 20),
    )(*operands, *after)


def shape(*dims, dtype=F32):
    return jax.ShapeDtypeStruct(dims, dtype)


def seg_of(places, meta):
    ids = (
        (places >= meta[0]).astype(jnp.int32)
        + (places >= meta[1]).astype(jnp.int32)
        + (places >= meta[2]).astype(jnp.int32)
    )
    return jnp.where(places < 0, -1, ids)


def row_of(meta, slot, rows):
    return pl.ds(pl.multiple_of(meta[6 + slot], rows), rows)


def halves(meta, half):
    return (
        pl.ds(pl.multiple_of(meta[4], half), half),
        pl.ds(pl.multiple_of(meta[5], half), half),
    )


def project_kernel(meta, tok, rim, gain, wq, wk, wv, wb, xq, xk, xv, xb, ext, proj, logits, ext_oth):
    rows, width = tok.shape
    for source, at, count in ((rim, 0, RIM), (tok, RIM, rows)):
        values = source[...].astype(F32)
        scale = lax.rsqrt(jnp.mean(values * values, axis=-1, keepdims=True) + EPS)
        ext[pl.ds(at, count), :] = (values * scale * gain[...]).astype(BF16)
    own, oth = halves(meta, width // 2)
    left, right = ext[:, own], ext[:, oth]
    ext_oth[...] = right
    chan = wq.shape[1]
    for at, (a, b) in enumerate(((wq, xq), (wk, xk), (wv, xv))):
        proj[:, at * chan : (at + 1) * chan] = dot_nn(left, a[...]) + dot_nn(right, b[...])
    logits[...] = dot_nn(left[RIM:], wb[...]) + dot_nn(right[RIM:], xb[...])


def conv_rows(ext, taps, block, lanes, rows, sames):
    start = block * taps.shape[2]
    columns = slice(start + lanes.start, start + lanes.stop)
    mixed = None
    for j in range(TAPS):
        term = taps[block, j : j + 1, lanes] * ext[RIM - j : RIM - j + rows, columns] * sames[j]
        mixed = term if mixed is None else mixed + term
    return mixed


def tap_masks(meta, rows):
    places = meta[3] + lax.broadcasted_iota(jnp.int32, (rows, 1), 0)
    seg = seg_of(places, meta)
    return places, [(seg_of(places - j, meta) == seg).astype(F32) for j in range(TAPS)]


def pick_column(values, head):
    lane = lax.broadcasted_iota(jnp.int32, values.shape, 1)
    return jnp.sum(jnp.where(lane == head, values, 0.0), axis=1, keepdims=True)


def chunk_masks(meta, at):
    first = meta[3] + at * CHUNK
    row = lax.broadcasted_iota(jnp.int32, (CHUNK, CHUNK), 0)
    col = lax.broadcasted_iota(jnp.int32, (CHUNK, CHUNK), 1)
    seg_col = seg_of(first + lax.broadcasted_iota(jnp.int32, (CHUNK, 1), 0), meta)
    seg_row = seg_of(first + lax.broadcasted_iota(jnp.int32, (1, CHUNK), 1), meta)
    before = seg_of(first - 1, meta)
    last = seg_of(first + CHUNK - 1, meta)
    same = (seg_col == seg_row).astype(F32)
    strict = jnp.where(row > col, same, 0.0)
    lower = jnp.where(row >= col, same, 0.0)
    carry_in = (seg_col == before).astype(F32)
    tail = (seg_col == last).astype(F32)
    whole = (last == before).astype(F32)
    return strict, lower, carry_in, tail, whole


def unit_inverses(grams):
    row = lax.broadcasted_iota(jnp.int32, (CHUNK, CHUNK), 0)
    col = lax.broadcasted_iota(jnp.int32, (CHUNK, CHUNK), 1)
    eye = (row == col).astype(F32)
    size = 8
    near = [jnp.where(row // size == col // size, g, 0.0) for g in grams]
    power = [dot_nn(n, n) for n in near]
    inverse = [eye - n for n in near]
    inverse = [x + dot_nn(x, p) for x, p in zip(inverse, power)]
    power = [dot_nn(p, p) for p in power]
    inverse = [x + dot_nn(x, p) for x, p in zip(inverse, power)]
    while size < CHUNK:
        off = (row // (2 * size) == col // (2 * size)) & (row // size != col // size)
        inner = [dot_nn(jnp.where(off, g, 0.0), x) for g, x in zip(grams, inverse)]
        inverse = [x - dot_nn(x, y) for x, y in zip(inverse, inner)]
        size *= 2
    resid = [(eye - x) - dot_nn(g, x, HIGH) for g, x in zip(grams, inverse)]
    return [x + dot_nn(x, r) for x, r in zip(inverse, resid)]

def silu_parts(mixed):
    sig = jax.nn.sigmoid(mixed)
    return sig, mixed * sig


def unit_parts(values):
    scale = lax.rsqrt(jnp.sum(values * values, axis=-1, keepdims=True) + EPS)
    return scale, values * scale


def delta_kernel(
    meta, ext, taps, logits,
    w_out, u_out, p_out, t_out, qe_out, m_out, mp_out, bp_out, qh_out, oh_out, mtot, btot,
):
    group, rows, width = w_out.shape
    places, sames = tap_masks(meta, rows)
    keep = (places < meta[2]).astype(F32)
    row = lax.broadcasted_iota(jnp.int32, (width, width), 0)
    col = lax.broadcasted_iota(jnp.int32, (width, width), 1)
    eye = (row == col).astype(F32)
    q, k, v, b = [], [], [], []
    for head in range(group):
        lanes = slice(head * width, (head + 1) * width)
        x = silu_parts(conv_rows(ext, taps, 0, lanes, rows, sames))[1]
        q.append(unit_parts(x)[1] * (1.0 / math.sqrt(width)))
        x = silu_parts(conv_rows(ext, taps, 1, lanes, rows, sames))[1]
        k.append(unit_parts(x)[1])
        v.append(silu_parts(conv_rows(ext, taps, 2, lanes, rows, sames))[1])
        b.append(jax.nn.sigmoid(pick_column(logits[...], head)) * keep)
    chunks = rows // CHUNK
    spots = [slice(at * CHUNK, (at + 1) * CHUNK) for at in range(chunks)]
    masks = [chunk_masks(meta, at) for at in range(chunks)]
    chains = [(head, at) for head in range(group) for at in range(chunks)]
    kc = [k[h][spots[a]] for h, a in chains]
    qc = [q[h][spots[a]] for h, a in chains]
    scaled = [b[h][spots[a]] * k[h][spots[a]] for h, a in chains]
    scaled_v = [b[h][spots[a]] * v[h][spots[a]] for h, a in chains]
    grams = [dot_nt(s, x, HIGH) * masks[a][0] for (h, a), s, x in zip(chains, scaled, kc)]
    scores = [dot_nt(y, x) * masks[a][1] for (h, a), y, x in zip(chains, qc, kc)]
    inverse = unit_inverses(grams)
    both = [dot_nn(t, jnp.concatenate([s, u], axis=1), HIGH) for t, s, u in zip(inverse, scaled, scaled_v)]
    inner = [
        jnp.concatenate([masks[a][2] * x[:, :width], x[:, width:]], axis=1) for (h, a), x in zip(chains, both)
    ]
    states = [dot_tn(x, masks[a][3] * y) for (h, a), x, y in zip(chains, kc, inner)]
    reach = [dot_nn(s, y) for s, y in zip(scores, inner)]
    steps = [masks[a][4] * eye - s[:, :width] for (h, a), s in zip(chains, states)]
    query = [masks[a][2] * x - y[:, :width] for (h, a), x, y in zip(chains, qc, reach)]
    for i, (h, a) in enumerate(chains):
        w_out[h, spots[a], :] = (both[i][:, :width]).astype(BF16)
        u_out[h, spots[a], :] = (both[i][:, width:]).astype(BF16)
        p_out[h, spots[a], :] = (scores[i]).astype(BF16)
        t_out[h, spots[a], :] = (inverse[i]).astype(BF16)
        qe_out[h, spots[a], :] = (query[i]).astype(BF16)
        m_out[h, spots[a], :] = (steps[i]).astype(BF16)
    prefix = [eye] * group
    added = [jnp.zeros((width, width), F32)] * group
    for a in range(chunks):
        for h in range(group):
            i = h * chunks + a
            mp_out[h, spots[a], :] = (prefix[h]).astype(BF16)
            bp_out[h, spots[a], :] = (added[h]).astype(BF16)
            if a == 0:
                qh_out[h, spots[a], :] = (query[i]).astype(BF16)
                oh_out[h, spots[a], :] = reach[i][:, width:]
                prefix[h], added[h] = steps[i], states[i][:, width:]
                continue
            out = dot_nn(
                jnp.concatenate([query[i], steps[i]], axis=0),
                jnp.concatenate([prefix[h], added[h]], axis=1),
            )
            qh_out[h, spots[a], :] = (out[:CHUNK, :width]).astype(BF16)
            oh_out[h, spots[a], :] = out[:CHUNK, width:] + reach[i][:, width:]
            prefix[h], added[h] = out[CHUNK:, :width], out[CHUNK:, width:] + states[i][:, width:]
    for h in range(group):
        mtot[h] = prefix[h]
        btot[h] = added[h]


def hop_kernel(step, extra, state, out, *, flip):
    for head in range(step.shape[0]):
        value = state[head].astype(F32)
        product = dot_tn(step[head], value, HIGH) if flip else dot_nn(step[head], value, HIGH)
        out[head] = (product + extra[head]).astype(BF16)


def chain_kernel(first, second, out):
    for head in range(first.shape[0]):
        out[head] = dot_nn(second[head], first[head], HIGH)


def attend_kernel(meta, qh, oh, state, gain, w_own, w_oth, heads_slot, o_out, *rest):
    pieces, low = rest[:-1], rest[-1]
    heads, rows, width = qh.shape
    for head in range(heads):
        out = dot_nn(qh[head], state[head]) + oh[head]
        o_out[head] = out
        scale = lax.rsqrt(jnp.mean(out * out, axis=-1, keepdims=True) + EPS)
        low[:, head * width : (head + 1) * width] = (out * scale * gain[...]).astype(BF16)
    count = rows // len(pieces)
    own, oth = halves(meta, w_own.shape[0])
    for slot, piece in enumerate(pieces):
        part = low[row_of(meta, slot, count), :]
        heads_slot[pl.ds(slot * count, count), :] = part
        piece[:, own] = dot_nt(part, w_own[...]).astype(BF16)
        piece[:, oth] = dot_nt(part, w_oth[...]).astype(BF16)


def norm_two_kernel(a, b, c, d, tok, gain, hidden_out, normed_out):
    total = a[...].astype(F32) + b[...].astype(F32) + c[...].astype(F32) + d[...].astype(F32)
    hidden = tok[...].astype(F32) + total
    scale = lax.rsqrt(jnp.mean(hidden * hidden, axis=-1, keepdims=True) + EPS)
    hidden_out[...] = hidden
    normed_out[...] = (hidden * scale * gain[...]).astype(BF16)


def add_kernel(mine, came, hidden, out):
    out[...] = (hidden[...] + (mine[...] + came[...].astype(F32))).astype(BF16)


def norm_back(grad, values, gain):
    scale = lax.rsqrt(jnp.mean(values * values, axis=-1, keepdims=True) + EPS)
    normal = values * scale
    hat = grad * gain
    back = scale * (hat - normal * jnp.mean(hat * normal, axis=-1, keepdims=True))
    return back, jnp.sum(grad * normal, axis=0, keepdims=True)


def norm_two_back_kernel(meta, a, b, c, d, hidden, cot, gain, grad_hidden, grad_att, d_gain):
    total = a[...].astype(F32) + b[...].astype(F32) + c[...].astype(F32) + d[...].astype(F32)
    back, d_gain[...] = norm_back(total, hidden[...], gain[...])
    places = meta[3] + meta[6] + lax.broadcasted_iota(jnp.int32, (hidden.shape[0], 1), 0)
    grad = cot[...].astype(F32) * (places < meta[2]).astype(F32) + back
    grad_hidden[...] = grad
    grad_att[...] = grad.astype(BF16)


def norm_one_back_kernel(a, b, c, d, tok, gain, grad_hidden, d_ffn, d_head, d_tok):
    total = a[...].astype(F32) + b[...].astype(F32) + c[...].astype(F32) + d[...].astype(F32)
    back, d_gain = norm_back(total, tok[...].astype(F32), gain[...])
    rows, width = tok.shape
    d_tok[pl.ds(0, rows), :] = (grad_hidden[...] + back).astype(BF16)
    line = lax.broadcasted_iota(jnp.int32, (RIM, width), 0)
    head = jnp.concatenate([d_head[...], jnp.zeros((1, width - d_head.shape[1]), F32)], axis=1)
    sums = jnp.where(line == 0, d_gain, jnp.where(line == 1, d_ffn[...], jnp.where(line == 2, head, 0.0)))
    d_tok[pl.ds(rows, RIM), :] = sums.astype(BF16)


def copy_kernel(value, out):
    out[...] = value[...]


def place_last_kernel(meta, a, b, c, d, out, sums):
    rows = a.shape[0] - RIM
    total = None
    for slot, piece in enumerate((a, b, c, d)):
        out[row_of(meta, slot, rows), :] = piece[pl.ds(0, rows), :]
        part = piece[pl.ds(rows, RIM), :].astype(F32)
        total = part if total is None else total + part
    sums[...] = total[: sums.shape[0]]


def place_kernel(meta, a, b, c, d, out):
    rows = a.shape[0]
    for slot, piece in enumerate((a, b, c, d)):
        out[row_of(meta, slot, rows), :] = piece[...]


def grad_act_kernel(meta, cot, w_own, w_oth, low_out, act_out, low_oth):
    rows, width = cot.shape
    slots = 4
    count = rows // slots
    for slot in range(slots):
        at = row_of(meta, slot, count)
        places = meta[3] + meta[6 + slot] + lax.broadcasted_iota(jnp.int32, (count, 1), 0)
        keep = (places < meta[2]).astype(F32)
        low_out[pl.ds(slot * count, count), :] = (cot[at, :].astype(F32) * keep).astype(BF16)
    own, oth = halves(meta, width // 2)
    low_oth[...] = low_out[:, oth]

    @pl.loop(0, 2)
    def _(step):
        at = pl.ds(pl.multiple_of(step * (rows // 2), rows // 2), rows // 2)
        act_out[at, :] = dot_nn(low_out[at, own], w_own[...]) + dot_nn(low_out[at, oth], w_oth[...])


def ffn_kernel(meta, a, b, c, d, g_own, g_oth, u_own, u_oth, grad_act, n_out, n_oth, wide_out, *pieces):
    count, width = a.shape
    for slot, source in enumerate((a, b, c, d)):
        n_out[pl.ds(slot * count, count), :] = source[...]
    own, oth = halves(meta, width // 2)
    n_oth[...] = n_out[:, oth]
    units = g_own.shape[1]
    for part in range(2):
        at = pl.ds(part * 2 * count, 2 * count)
        left, right = n_out[at, own], n_out[at, oth]
        gate = dot_nn(left, g_own[...]) + dot_nn(right, g_oth[...])
        up = dot_nn(left, u_own[...]) + dot_nn(right, u_oth[...])
        sig = jax.nn.sigmoid(gate)
        wide_out[at, :units] = (gate * sig * up).astype(BF16)
        grad = grad_act[at, :]
        grad_gate = (grad * up * sig * (1.0 + gate * (1.0 - sig))).astype(BF16)
        grad_up = (grad * gate * sig).astype(BF16)
        wide_out[at, units : 2 * units] = grad_gate
        wide_out[at, 2 * units :] = grad_up
        for side, gate_side, up_side in ((own, g_own, u_own), (oth, g_oth, u_oth)):
            total = (dot_nt(grad_gate, gate_side[...]) + dot_nt(grad_up, up_side[...])).astype(BF16)
            pieces[2 * part][:, side] = total[:count]
            pieces[2 * part + 1][:, side] = total[count:]


def down_kernel(meta, wide, w_own, w_oth, keep, give):
    act = wide[:, : w_own.shape[1]]
    count = keep.shape[0] // 2
    own, oth = halves(meta, w_own.shape[0])
    for side, weight in ((own, w_own), (oth, w_oth)):
        total = dot_nt(act, weight[...]).astype(BF16)
        for slot, out in enumerate((keep, give, keep, give)):
            out[pl.ds(slot // 2 * count, count), side] = total[slot * count : (slot + 1) * count]


def add_half_kernel(keep, came, mine, other):
    count = mine.shape[0]
    total = keep[...].astype(F32) + came[...].astype(F32)
    mine[...] = total[:count]
    other[...] = total[count:].astype(BF16)


def heads_back_kernel(
    meta, g0, g1, g2, g3, w_own, w_oth, o_in, gain, qe, qh, grad_o, d_chunk, d_total, d_gain, cat_out, cat_oth, grad
):
    heads, rows, width = o_in.shape
    count = g0.shape[0]
    own, oth = halves(meta, w_own.shape[0])
    for slot, source in enumerate((g0, g1, g2, g3)):
        cat_out[pl.ds(slot * count, count), :] = source[...]
    cat_oth[...] = cat_out[:, oth]
    whole = dot_nn(cat_out[:, own], w_own[...]) + dot_nn(cat_out[:, oth], w_oth[...])
    for slot in range(4):
        grad[row_of(meta, slot, count), :] = whole[slot * count : (slot + 1) * count]
    total_gain = jnp.zeros((1, width), F32)
    for head in range(heads):
        out = o_in[head]
        back, part = norm_back(grad[:, head * width : (head + 1) * width], out, gain[...])
        total_gain = total_gain + part
        grad_o[head] = back
        d_total[head] = dot_tn(qh[head], back)
        for at in range(rows // CHUNK):
            here = slice(at * CHUNK, (at + 1) * CHUNK)
            d_chunk[head, here, :] = dot_tn(qe[head, here, :], back[here])
    d_gain[...] = total_gain


def delta_back_kernel(
    meta, ext, taps, logits,
    w_in, u_in, p_in, t_in, m_in, mp_in, bp_in, s_in, do_in, dc_in, *rest,
):
    grads_in, rest = rest[:-5], rest[-5:]
    grad_ext, grad_rim, grad_tail, d_taps, pad = rest
    group, rows, width = w_in.shape
    places, sames = tap_masks(meta, rows)
    keep = (places < meta[2]).astype(F32)
    root = 1.0 / math.sqrt(width)
    chunks = rows // CHUNK
    spots = [slice(at * CHUNK, (at + 1) * CHUNK) for at in range(chunks)]
    masks = [chunk_masks(meta, at) for at in range(chunks)]
    chains = [(head, at) for head in range(group) for at in range(chunks)]
    q, k, v, b, sig_b, scale_q, scale_k = [], [], [], [], [], [], []
    for head in range(group):
        lanes = slice(head * width, (head + 1) * width)
        scale, unit = unit_parts(silu_parts(conv_rows(ext, taps, 0, lanes, rows, sames))[1])
        scale_q.append(scale)
        q.append(unit)
        scale, unit = unit_parts(silu_parts(conv_rows(ext, taps, 1, lanes, rows, sames))[1])
        scale_k.append(scale)
        k.append(unit)
        v.append(silu_parts(conv_rows(ext, taps, 2, lanes, rows, sames))[1])
        sig_b.append(jax.nn.sigmoid(pick_column(logits[...], head)))
        b.append(sig_b[head] * keep)
    after = {}
    for head in range(group):
        total = grads_in[0][head].astype(F32)
        for grad, step in zip(grads_in[1 : (len(grads_in) + 1) // 2], grads_in[(len(grads_in) + 1) // 2 :]):
            total = total + dot_tn(step[head], grad[head].astype(F32))
        after[head, chunks - 1] = total
    for at in range(chunks - 1, 0, -1):
        for head in range(group):
            after[head, at - 1] = dot_tn(m_in[head, spots[at], :], after[head, at]) + dc_in[head, spots[at], :]
    grad_state = [after[c] for c in chains]
    state = [dot_nn(mp_in[h, spots[a], :], s_in[h]) + bp_in[h, spots[a], :].astype(F32) for h, a in chains]
    kc = [k[h][spots[a]] for h, a in chains]
    grad_o = [do_in[h, spots[a], :] for h, a in chains]
    fresh = [
        u_in[h, spots[a], :].astype(F32) - masks[a][2] * dot_nn(w_in[h, spots[a], :], s)
        for (h, a), s in zip(chains, state)
    ]
    d_fresh = [
        dot_tn(p_in[h, spots[a], :], g) + masks[a][3] * dot_nn(x, s)
        for (h, a), g, x, s in zip(chains, grad_o, kc, grad_state)
    ]
    d_scores = [dot_nt(g, f) * masks[a][1] for (h, a), g, f in zip(chains, grad_o, fresh)]
    back = [
        dot_nt(jnp.concatenate([masks[a][2] * g, masks[a][2] * f], axis=0), s)
        for (h, a), g, f, s in zip(chains, grad_o, d_fresh, state)
    ]
    d_q = [x[:CHUNK] + dot_nn(d, y) for x, d, y in zip(back, d_scores, kc)]
    d_k = [
        root * dot_tn(d, q[h][spots[a]]) + dot_nt(masks[a][3] * f, s)
        for (h, a), d, f, s in zip(chains, d_scores, fresh, grad_state)
    ]
    right = [
        dot_tn(t_in[h, spots[a], :], jnp.concatenate([-x[CHUNK:], f], axis=1))
        for (h, a), x, f in zip(chains, back, d_fresh)
    ]
    d_gram = [
        -masks[a][0] * dot_nt(r, jnp.concatenate([w_in[h, spots[a], :], u_in[h, spots[a], :]], axis=1))
        for (h, a), r in zip(chains, right)
    ]
    d_scaled = [r[:, :width] + dot_nn(g, x) for r, g, x in zip(right, d_gram, kc)]
    d_k = [
        x + dot_tn(g, b[h][spots[a]] * y) + b[h][spots[a]] * d
        for (h, a), x, g, y, d in zip(chains, d_k, d_gram, kc, d_scaled)
    ]
    d_b = [
        jnp.sum(d * y + r[:, width:] * v[h][spots[a]], axis=1, keepdims=True)
        for (h, a), d, y, r in zip(chains, d_scaled, kc, right)
    ]
    d_v = [b[h][spots[a]] * r[:, width:] for (h, a), r in zip(chains, right)]
    lane = lax.broadcasted_iota(jnp.int32, (rows, LANES), 1)
    all_logits = jnp.zeros((rows, LANES), F32)
    zeros = jnp.zeros((RIM, width), F32)
    heads_width = grad_ext.shape[1] // 3 // LANES * LANES
    for head in range(group):
        mine = slice(head * chunks, (head + 1) * chunks)
        lanes = slice(head * width, (head + 1) * width)
        d_logit = jnp.concatenate(d_b[mine], axis=0) * keep * sig_b[head] * (1.0 - sig_b[head])
        all_logits = jnp.where(lane == head, d_logit, all_logits)
        g_q, g_k, g_v = (jnp.concatenate(x[mine], axis=0) for x in (d_q, d_k, d_v))
        g_q = root * scale_q[head] * (g_q - q[head] * jnp.sum(g_q * q[head], axis=-1, keepdims=True))
        g_k = scale_k[head] * (g_k - k[head] * jnp.sum(g_k * k[head], axis=-1, keepdims=True))
        for block, grad in enumerate((g_q, g_k, g_v)):
            spot = head * 3 + block
            at = slice(block * heads_width + head * width, block * heads_width + (head + 1) * width)
            pad[spot, pl.ds(0, RIM), :] = zeros
            pad[spot, pl.ds(RIM + rows, RIM), :] = zeros
            mixed = conv_rows(ext, taps, block, lanes, rows, sames)
            sig = silu_parts(mixed)[0]
            d_mixed = grad * sig * (1.0 + mixed * (1.0 - sig))
            total = jnp.zeros((rows + RIM, width), F32)
            for j in range(TAPS):
                masked = d_mixed * sames[j]
                pad[spot, pl.ds(RIM, rows), :] = masked
                total = total + taps[block, j : j + 1, lanes] * pad[spot, pl.ds(j, rows + RIM), :]
                d_taps[block, j : j + 1, lanes] = jnp.sum(
                    masked * ext[RIM - j : RIM - j + rows, at], axis=0, keepdims=True
                )
            grad_ext[:, at] = total.astype(BF16)
            grad_rim[:, at] = total[:RIM]
            grad_tail[:, at] = total[rows:]
    grad_ext[pl.ds(RIM, rows), 3 * heads_width :] = all_logits.astype(BF16)
    grad_ext[pl.ds(0, RIM), 3 * heads_width :] = jnp.zeros((RIM, LANES), BF16)


def back_project_kernel(
    meta, grad_ext, tail, returned, wq, wk, wv, wb, xq, xk, xv, xb, *rest
):
    pieces, grad = rest[:-1], rest[-1]
    count = pieces[0].shape[0]
    chan = wq.shape[1]
    for slot in range(len(pieces)):
        here = pl.ds(slot * count, count)
        start = pl.multiple_of(meta[6 + slot], count)
        grad[here, :] = grad_ext[pl.ds(pl.multiple_of(start + RIM, RIM), count), :]
    last = pl.multiple_of(meta[6 + len(pieces) - 1] + count - RIM, RIM)
    grad[pl.ds(last, RIM), : 3 * chan] = (tail[...] + returned[...]).astype(BF16)
    own, oth = halves(meta, wq.shape[0])
    for side, weights in ((own, (wq, wk, wv, wb)), (oth, (xq, xk, xv, xb))):
        total = dot_nt(grad[:, 3 * chan : 3 * chan + weights[3].shape[1]], weights[3][...])
        for block in range(3):
            total = total + dot_nt(grad[:, block * chan : (block + 1) * chan], weights[block][...])
        total = total.astype(BF16)
        for slot, piece in enumerate(pieces):
            piece[:, side] = total[slot * count : (slot + 1) * count]


def ffn_grad_kernel(meta, low, low_sib, normed, normed_sib, wide, wide_sib, out):
    own = halves(meta, out.shape[0])[0]
    units = wide.shape[1] // 3
    lows = jnp.concatenate([low[:, own], low_sib[...]], axis=0)
    norms = jnp.concatenate([normed[:, own], normed_sib[...]], axis=0)
    for at, left in enumerate((lows, norms, norms)):
        here = slice(at * units, (at + 1) * units)
        out[:, here] = dot_tn(left, jnp.concatenate([wide[:, here], wide_sib[:, here]], axis=0)).astype(BF16)


def proj_grad_kernel(
    meta, normed, grad, normed_sib, grad_sib, grad_att, heads, grad_att_sib, heads_sib, out
):
    half, columns = out.shape[0], grad.shape[1]
    own = halves(meta, half)[0]
    out[:, :columns] = (
        dot_tn(normed[:, own], grad[...]) + dot_tn(normed_sib[...], grad_sib[...])
    ).astype(BF16)
    out[:, columns:] = (
        dot_tn(grad_att[:, own], heads[...]) + dot_tn(grad_att_sib[...], heads_sib[...])
    ).astype(BF16)


def flipped(value, axis, bit):
    return lax.ppermute(value, axis, [(i, i ^ bit) for i in range(lax.axis_size(axis))])


def shifted(value, axis, by, reach=None):
    length = lax.axis_size(axis)
    pairs = [(i, i + by) for i in range(length) if 0 <= i + by < length]
    if reach is not None:
        pairs = [pair for pair in pairs if reach(pair[0])]
    return lax.ppermute(value, axis, pairs)


def exchanged(pieces):
    return [pieces[0]] + [flipped(piece, "tp", slot) for slot, piece in enumerate(pieces) if slot]


def gathered(piece):
    return [piece] + [flipped(piece, "tp", slot) for slot in range(1, lax.axis_size("tp"))]


def summed(value, axis):
    bit = 1
    while bit < lax.axis_size(axis):
        value = value + flipped(value, axis, bit)
        bit *= 2
    return value


def contract_rows(left_side, right_side):
    return lax.dot_general(
        left_side, right_side, (((0,), (0,)), ((), ())), preferred_element_type=F32
    )


def scattered(value):
    return lax.psum_scatter(value, "ctx", scatter_dimension=0, tiled=True)


def line_kernel(meta, value, *rest, step, last):
    rights, lefts = rest[-2:]
    rows = rights.shape[0]
    place = meta[meta.shape[0] - 1]
    for out, due, came in zip((rights, lefts), (last - step + place, place - last + step), rest[:-2] or (None, None)):
        start = pl.multiple_of(jnp.clip(due, 0, last) * rows, rows)
        part = value[pl.ds(start, rows), :]
        if came is not None:
            part = (part.astype(F32) + came[...].astype(F32)).astype(BF16)
        out[...] = part


def line_step(meta, value, step, came, after=()):
    last = lax.axis_size("ctx") - 1
    part = shape(value.shape[0] // (last + 1), value.shape[1], dtype=BF16)
    right, left = call(
        functools.partial(line_kernel, step=step, last=last), [part, part], (meta, value, *came), after=after
    )
    return right, (
        shifted(right, "ctx", 1, lambda i: i <= step),
        shifted(left, "ctx", -1, lambda i: i >= last - step),
    )


def line_total(value, place, came):
    rows = value.shape[0] // lax.axis_size("ctx")
    total = lax.dynamic_slice_in_dim(value, place * rows, rows, 0).astype(F32)
    return total + came[0].astype(F32) + came[1].astype(F32)


def shards(
    tokens, seq_bounds, w_query, w_key, w_value, w_beta, conv_taps, out_gain, w_out,
    attn_gain, ffn_gain, w_gate, w_up, w_down, cotangent,
):
    rows, width = tokens.shape
    half = w_query.shape[0]
    chan = w_query.shape[1]
    heads = w_beta.shape[1]
    dim = out_gain.shape[0]
    units = w_gate.shape[1]
    slots = lax.axis_size("tp")
    count = rows // slots
    core, place, member = lax.axis_index("fsdp"), lax.axis_index("ctx"), lax.axis_index("tp")
    meta = jnp.concatenate(
        [
            seq_bounds[0],
            jnp.stack(
                [place * rows, core * half, (1 - core) * half]
                + [(member ^ slot) * count for slot in range(slots)]
                + [place]
            ).astype(jnp.int32),
        ]
    )
    attn_row, ffn_row, out_row = attn_gain[None, :], ffn_gain[None, :], out_gain[None, :]

    rim = shifted(tokens[rows - RIM :], "ctx", 1)
    x_query, x_key, x_value, x_beta = (flipped(w, "fsdp", 1) for w in (w_query, w_key, w_value, w_beta))
    tok_own = lax.dynamic_slice_in_dim(tokens, member * count, count, 0)
    cot_own = lax.dynamic_slice_in_dim(cotangent, member * count, count, 0)

    normed, proj, logits, normed_oth = call(
        project_kernel,
        [
            shape(rows + RIM, width, dtype=BF16),
            shape(rows + RIM, 3 * chan),
            shape(rows, heads),
            shape(rows + RIM, half, dtype=BF16),
        ],
        (meta, tokens, rim, attn_row, w_query, w_key, w_value, w_beta, x_query, x_key, x_value, x_beta),
        flops=2 * rows * width * 3 * chan,
        vmem=58,
    )
    later = lax.optimization_barrier((w_down, w_gate, w_up, normed_oth))
    x_out = flipped(w_out, "fsdp", 1)
    x_down, x_gate, x_up = (flipped(w, "fsdp", 1) for w in later[:3])
    normed_oth = later[3]
    tall, square = shape(heads, rows, dim), shape(heads, dim, dim)
    erase, write, scores, inverse, query_eff, step, prefix, added, query_hat, out_hat, m_total, b_total = call(
        delta_kernel,
        [shape(heads, rows, dim, dtype=BF16)] * 9 + [tall] + [square] * 2,
        (meta, proj, conv_taps, logits),
        flops=heads * 60 * rows * dim * dim,
        vmem=58,
    )

    def hop(matrix, extra, state, flip, after=()):
        return call(
            functools.partial(hop_kernel, flip=flip),
            shape(heads, dim, dim, dtype=BF16),
            (matrix, extra, state),
            flops=2 * heads * dim**3,
            scalars=False,
            after=after,
        )

    state = jnp.zeros((heads, dim, dim), BF16)
    for index in range(lax.axis_size("ctx") - 1):
        sent = b_total.astype(BF16) if index == 0 else hop(m_total, b_total, state, False)
        state = shifted(sent, "ctx", 1)

    piece_shape = shape(count, width, dtype=BF16)
    normed_sib = flipped(normed_oth, "fsdp", 1)
    heads_slot, heads_out, *pieces = call(
        attend_kernel,
        [shape(rows, chan, dtype=BF16), tall] + [piece_shape] * slots,
        (meta, query_hat, out_hat, state, out_row, w_out, x_out),
        flops=2 * rows * width * chan,
        after=(x_down, x_gate, x_up, normed_sib),
        scratch=[VMEM((rows, chan), BF16)],
    )
    grad_low, grad_act, low_oth = call(
        grad_act_kernel,
        [shape(rows, width, dtype=BF16), shape(rows, units), shape(rows, half, dtype=BF16)],
        (meta, cotangent, w_down, x_down),
        flops=2 * rows * width * units,
        after=(heads_slot,),
    )
    heads_sib, low_sib = flipped(heads_slot, "fsdp", 1), flipped(low_oth, "fsdp", 1)
    hidden, normed_two = call(
        norm_two_kernel,
        [shape(count, width), piece_shape],
        (*exchanged(pieces), tok_own, ffn_row),
        scalars=False,
    )
    maps = None
    if lax.axis_size("ctx") == 4:
        near = shifted(m_total, "ctx", -1)
        chained = call(chain_kernel, square, (m_total, near), scalars=False, after=(normed_two,))
        maps = (near, shifted(chained, "ctx", -1))
    normed_slot, two_oth, wide, *pieces = call(
        ffn_kernel,
        [
            shape(rows, width, dtype=BF16),
            shape(rows, half, dtype=BF16),
            shape(rows, 3 * units, dtype=BF16),
        ]
        + [piece_shape] * slots,
        (meta, *gathered(normed_two), w_gate, x_gate, w_up, x_up, grad_act),
        flops=8 * rows * width * units,
        after=(*(maps or ()), low_sib),
    )
    two_sib, wide_sib = flipped(two_oth, "fsdp", 1), flipped(wide, "fsdp", 1)
    received = exchanged(pieces)
    grad_hidden, grad_att, d_ffn_part = call(
        norm_two_back_kernel,
        [shape(count, width), piece_shape, shape(1, width)],
        (meta, *received, hidden, cot_own, ffn_row),
    )
    ffn_pair = call(
        ffn_grad_kernel,
        shape(half, 3 * units, dtype=BF16),
        (meta, grad_low, low_sib, normed_slot, two_sib, wide, wide_sib),
        flops=4 * rows * half * 3 * units,
    )
    ffn_sum = scattered(ffn_pair)
    down_keep, down_give = call(
        down_kernel,
        [shape(2 * count, width, dtype=BF16)] * 2,
        (meta, wide, w_down, x_down),
        flops=2 * rows * width * units,
        after=(grad_att,),
    )
    grad_o, d_chunk, d_total, d_head_part, grad_att_slot, att_oth = call(
        heads_back_kernel,
        [tall, tall, square, shape(1, dim), shape(rows, width, dtype=BF16), shape(rows, half, dtype=BF16)],
        (meta, *gathered(grad_att), w_out, x_out, heads_out, out_row, query_eff, query_hat),
        flops=2 * rows * width * chan,
        scratch=[VMEM((rows, chan), F32)],
        after=(ffn_pair, down_keep),
    )
    if maps is None:
        grad_state = jnp.zeros((heads, dim, dim), BF16)
        for index in range(lax.axis_size("ctx") - 1):
            sent = d_total.astype(BF16) if index == 0 else hop(m_total, d_total, grad_state, True)
            grad_state = shifted(sent, "ctx", -1)
        gathered_grads = (grad_state,)
    else:
        sent = d_total.astype(BF16)
        gathered_grads = tuple(shifted(sent, "ctx", -by) for by in range(1, lax.axis_size("ctx")))
    down_mine, down_other = call(
        add_half_kernel,
        [shape(count, width), piece_shape],
        (down_keep, flipped(down_give, "tp", 1)),
        scalars=False,
        after=(d_total,),
    )
    att_sib = flipped(att_oth, "fsdp", 1)

    grad_ext, grad_rim, grad_tail, d_conv_part = call(
        delta_back_kernel,
        [
            shape(rows + RIM, 3 * chan + LANES, dtype=BF16),
            shape(RIM, 3 * chan),
            shape(RIM, 3 * chan),
            shape(3, TAPS, chan),
        ],
        (
            meta, proj, conv_taps, logits,
            erase, write, scores, inverse, step, prefix, added, state, grad_o, d_chunk,
            *gathered_grads, *(maps or ()),
        ),
        flops=heads * 60 * rows * dim * dim,
        scratch=[VMEM((3 * heads, rows + 2 * RIM, dim), F32)],
        after=(att_sib, down_other),
    )
    returned = shifted(grad_rim, "ctx", -1)
    grad_sib = flipped(grad_ext, "fsdp", 1)
    proj_pair = call(
        proj_grad_kernel,
        shape(half, 4 * chan + LANES, dtype=BF16),
        (meta, normed, grad_ext, normed_sib, grad_sib, grad_att_slot, heads_slot, att_sib, heads_sib),
        flops=4 * rows * half * 4 * chan,
    )
    out_own = call(
        add_kernel,
        piece_shape,
        (down_mine, flipped(down_other, "tp", 2), hidden),
        scalars=False,
        after=(returned, proj_pair),
    )
    pieces = call(
        back_project_kernel,
        [piece_shape] * slots,
        (
            meta, grad_ext, grad_tail, returned,
            w_query, w_key, w_value, w_beta, x_query, x_key, x_value, x_beta,
        ),
        flops=2 * rows * width * 3 * chan,
        scratch=[VMEM((rows, 3 * chan + LANES), BF16)],
        after=(out_own,),
    )
    sent, came = line_step(meta, proj_pair, 0, (), after=(returned,))
    d_tok_own = call(
        norm_one_back_kernel,
        shape(count + RIM, width, dtype=BF16),
        (*exchanged(pieces), tok_own, attn_row, grad_hidden, d_ffn_part, d_head_part),
        scalars=False,
        after=came,
    )
    tok_slots = gathered(d_tok_own)
    for step in range(1, lax.axis_size("ctx") - 1):
        sent, came = line_step(meta, proj_pair, step, came, after=() if step == 1 else (d_tokens,))
        if step == 1:
            d_tokens, gains = call(
                place_last_kernel,
                [shape(rows, width, dtype=BF16), shape(8, width)],
                (meta, *tok_slots),
                after=(ffn_sum,),
            )
    out_late = call(copy_kernel, piece_shape, (out_own,), scalars=False, after=(d_tokens, sent))
    out = call(place_kernel, shape(rows, width, dtype=BF16), (meta, *gathered(out_late)), after=came)
    conv_rows_count = 3 * TAPS * chan // width
    bundle = summed(
        jnp.concatenate([gains, d_conv_part.reshape(conv_rows_count, width)], axis=0), "fsdp"
    )
    bundle = call(copy_kernel, shape(8 + conv_rows_count, width), (bundle,), scalars=False, after=(out,))
    length = lax.axis_size("ctx")
    if length == 4:
        bundle = bundle + sum(flipped(bundle, "ctx", bit) for bit in (1, 2, 3))
    else:
        bundle = summed(bundle, "ctx")
    proj_sum, ffn_sum = line_total(proj_pair, place, came), ffn_sum.astype(F32)
    return (
        out,
        d_tokens,
        proj_sum[:, :chan],
        proj_sum[:, chan : 2 * chan],
        proj_sum[:, 2 * chan : 3 * chan],
        proj_sum[:, 3 * chan : 3 * chan + heads],
        bundle[8:].reshape(3, TAPS, chan),
        bundle[2, :dim],
        proj_sum[:, 3 * chan + LANES :],
        bundle[0],
        bundle[1],
        ffn_sum[:, units : 2 * units],
        ffn_sum[:, 2 * units :],
        ffn_sum[:, :units],
    )


def solution(mesh):
    both = P(("fsdp", "ctx"), None)
    weight = P("fsdp", "tp")
    grad = P(("fsdp", "ctx"), "tp")
    in_specs = (
        both, P("fsdp", None), weight, weight, weight, weight, P(None, None, "tp"), P(), weight,
        P(), P(), weight, weight, weight, both,
    )
    out_specs = (
        both, both, grad, grad, grad, grad, P(None, None, "tp"), P(), grad, P(), P(), grad, grad, grad,
    )
    return jax.shard_map(shards, mesh=mesh, in_specs=in_specs, out_specs=out_specs, check_vma=False)
```

```python
import functools
import math

import jax
import jax.numpy as jnp
from jax import lax
from jax.experimental import pallas as pl
from jax.experimental.pallas import tpu as pltpu
from jax.sharding import PartitionSpec as P

EPS = 1e-06
HIGH = True
F32 = jnp.float32
BF16 = jnp.bfloat16
CHUNK = 128
LANES = 128
RIM = 16
TAPS = 4
VMEM = pltpu.VMEM
WHOLE = pl.BlockSpec(memory_space=pltpu.VMEM)
SCALARS = pl.BlockSpec(memory_space=pltpu.SMEM)


def split(value):
    high = value.astype(BF16)
    return high, (value - high.astype(F32)).astype(BF16)


def product(dims, left, right, exact):
    def one(a, b):
        return lax.dot_general(a, b, (dims, ((), ())), preferred_element_type=F32)

    if not exact:
        return one(left.astype(BF16), right.astype(BF16))
    (left_hi, left_lo), (right_hi, right_lo) = split(left), split(right)
    return one(left_hi, right_hi) + (one(left_hi, right_lo) + one(left_lo, right_hi))


def dot_nn(left, right, exact=False):
    return product(((1,), (0,)), left, right, exact)


def dot_nt(left, right, exact=False):
    return product(((1,), (1,)), left, right, exact)


def dot_tn(left, right, exact=False):
    return product(((0,), (0,)), left, right, exact)


def call(kernel, out_shape, operands, flops=0, scratch=(), scalars=True, after=(), vmem=36):
    outs = out_shape if isinstance(out_shape, list) else [out_shape]
    size = sum(math.prod(x.shape) * x.dtype.itemsize for x in (*operands, *outs))
    given = len(operands)

    def body(*refs):
        kernel(*refs[:given], *refs[given + len(after) :])

    return pl.pallas_call(
        body,
        out_shape=out_shape,
        in_specs=[SCALARS] * scalars
        + [WHOLE] * (given - scalars)
        + [pl.BlockSpec(memory_space=pl.ANY)] * len(after),
        out_specs=[WHOLE] * len(outs) if isinstance(out_shape, list) else WHOLE,
        scratch_shapes=list(scratch),
        name=getattr(kernel, "func", kernel).__name__,
        cost_estimate=pl.CostEstimate(
            flops=flops, bytes_accessed=size, transcendentals=0
        ),
        compiler_params=pltpu.CompilerParams(vmem_limit_bytes=vmem << 20),
    )(*operands, *after)


def shape(*dims, dtype=F32):
    return jax.ShapeDtypeStruct(dims, dtype)


def seg_of(places, meta):
    ids = (
        (places >= meta[0]).astype(jnp.int32)
        + (places >= meta[1]).astype(jnp.int32)
        + (places >= meta[2]).astype(jnp.int32)
    )
    return jnp.where(places < 0, -1, ids)


def row_of(meta, slot, rows):
    return pl.ds(pl.multiple_of(meta[6 + slot], rows), rows)


def halves(meta, half):
    return (
        pl.ds(pl.multiple_of(meta[4], half), half),
        pl.ds(pl.multiple_of(meta[5], half), half),
    )


def project_kernel(meta, tok, rim, gain, wq, wk, wv, wb, xq, xk, xv, xb, ext, proj, logits, ext_oth):
    rows, width = tok.shape
    for source, at, count in ((rim, 0, RIM), (tok, RIM, rows)):
        values = source[...].astype(F32)
        scale = lax.rsqrt(jnp.mean(values * values, axis=-1, keepdims=True) + EPS)
        ext[pl.ds(at, count), :] = (values * scale * gain[...]).astype(BF16)
    own, oth = halves(meta, width // 2)
    left, right = ext[:, own], ext[:, oth]
    ext_oth[...] = right
    chan = wq.shape[1]
    for at, (a, b) in enumerate(((wq, xq), (wk, xk), (wv, xv))):
        proj[:, at * chan : (at + 1) * chan] = dot_nn(left, a[...]) + dot_nn(right, b[...])
    logits[...] = dot_nn(left[RIM:], wb[...]) + dot_nn(right[RIM:], xb[...])


def conv_rows(ext, taps, block, lanes, rows, sames):
    start = block * taps.shape[2]
    columns = slice(start + lanes.start, start + lanes.stop)
    mixed = None
    for j in range(TAPS):
        term = taps[block, j : j + 1, lanes] * ext[RIM - j : RIM - j + rows, columns] * sames[j]
        mixed = term if mixed is None else mixed + term
    return mixed


def tap_masks(meta, rows):
    places = meta[3] + lax.broadcasted_iota(jnp.int32, (rows, 1), 0)
    seg = seg_of(places, meta)
    return places, [(seg_of(places - j, meta) == seg).astype(F32) for j in range(TAPS)]


def pick_column(values, head):
    lane = lax.broadcasted_iota(jnp.int32, values.shape, 1)
    return jnp.sum(jnp.where(lane == head, values, 0.0), axis=1, keepdims=True)


def chunk_masks(meta, at):
    first = meta[3] + at * CHUNK
    row = lax.broadcasted_iota(jnp.int32, (CHUNK, CHUNK), 0)
    col = lax.broadcasted_iota(jnp.int32, (CHUNK, CHUNK), 1)
    seg_col = seg_of(first + lax.broadcasted_iota(jnp.int32, (CHUNK, 1), 0), meta)
    seg_row = seg_of(first + lax.broadcasted_iota(jnp.int32, (1, CHUNK), 1), meta)
    before = seg_of(first - 1, meta)
    last = seg_of(first + CHUNK - 1, meta)
    same = (seg_col == seg_row).astype(F32)
    strict = jnp.where(row > col, same, 0.0)
    lower = jnp.where(row >= col, same, 0.0)
    carry_in = (seg_col == before).astype(F32)
    tail = (seg_col == last).astype(F32)
    whole = (last == before).astype(F32)
    return strict, lower, carry_in, tail, whole


def unit_inverses(grams):
    row = lax.broadcasted_iota(jnp.int32, (CHUNK, CHUNK), 0)
    col = lax.broadcasted_iota(jnp.int32, (CHUNK, CHUNK), 1)
    eye = (row == col).astype(F32)
    size = 8
    near = [jnp.where(row // size == col // size, g, 0.0) for g in grams]
    power = [dot_nn(n, n) for n in near]
    inverse = [eye - n for n in near]
    inverse = [x + dot_nn(x, p) for x, p in zip(inverse, power)]
    power = [dot_nn(p, p) for p in power]
    inverse = [x + dot_nn(x, p) for x, p in zip(inverse, power)]
    while size < CHUNK:
        off = (row // (2 * size) == col // (2 * size)) & (row // size != col // size)
        inner = [dot_nn(jnp.where(off, g, 0.0), x) for g, x in zip(grams, inverse)]
        inverse = [x - dot_nn(x, y) for x, y in zip(inverse, inner)]
        size *= 2
    resid = [(eye - x) - dot_nn(g, x, HIGH) for g, x in zip(grams, inverse)]
    return [x + dot_nn(x, r) for x, r in zip(inverse, resid)]

def silu_parts(mixed):
    sig = jax.nn.sigmoid(mixed)
    return sig, mixed * sig


def unit_parts(values):
    scale = lax.rsqrt(jnp.sum(values * values, axis=-1, keepdims=True) + EPS)
    return scale, values * scale


def delta_kernel(
    meta, ext, taps, logits,
    w_out, u_out, p_out, t_out, qe_out, m_out, mp_out, bp_out, qh_out, oh_out, mtot, btot,
):
    group, rows, width = w_out.shape
    places, sames = tap_masks(meta, rows)
    keep = (places < meta[2]).astype(F32)
    row = lax.broadcasted_iota(jnp.int32, (width, width), 0)
    col = lax.broadcasted_iota(jnp.int32, (width, width), 1)
    eye = (row == col).astype(F32)
    q, k, v, b = [], [], [], []
    for head in range(group):
        lanes = slice(head * width, (head + 1) * width)
        x = silu_parts(conv_rows(ext, taps, 0, lanes, rows, sames))[1]
        q.append(unit_parts(x)[1] * (1.0 / math.sqrt(width)))
        x = silu_parts(conv_rows(ext, taps, 1, lanes, rows, sames))[1]
        k.append(unit_parts(x)[1])
        v.append(silu_parts(conv_rows(ext, taps, 2, lanes, rows, sames))[1])
        b.append(jax.nn.sigmoid(pick_column(logits[...], head)) * keep)
    chunks = rows // CHUNK
    spots = [slice(at * CHUNK, (at + 1) * CHUNK) for at in range(chunks)]
    masks = [chunk_masks(meta, at) for at in range(chunks)]
    chains = [(head, at) for head in range(group) for at in range(chunks)]
    kc = [k[h][spots[a]] for h, a in chains]
    qc = [q[h][spots[a]] for h, a in chains]
    scaled = [b[h][spots[a]] * k[h][spots[a]] for h, a in chains]
    scaled_v = [b[h][spots[a]] * v[h][spots[a]] for h, a in chains]
    grams = [dot_nt(s, x, HIGH) * masks[a][0] for (h, a), s, x in zip(chains, scaled, kc)]
    scores = [dot_nt(y, x) * masks[a][1] for (h, a), y, x in zip(chains, qc, kc)]
    inverse = unit_inverses(grams)
    both = [dot_nn(t, jnp.concatenate([s, u], axis=1), HIGH) for t, s, u in zip(inverse, scaled, scaled_v)]
    inner = [
        jnp.concatenate([masks[a][2] * x[:, :width], x[:, width:]], axis=1) for (h, a), x in zip(chains, both)
    ]
    states = [dot_tn(x, masks[a][3] * y) for (h, a), x, y in zip(chains, kc, inner)]
    reach = [dot_nn(s, y) for s, y in zip(scores, inner)]
    steps = [masks[a][4] * eye - s[:, :width] for (h, a), s in zip(chains, states)]
    query = [masks[a][2] * x - y[:, :width] for (h, a), x, y in zip(chains, qc, reach)]
    for i, (h, a) in enumerate(chains):
        w_out[h, spots[a], :] = (both[i][:, :width]).astype(BF16)
        u_out[h, spots[a], :] = (both[i][:, width:]).astype(BF16)
        p_out[h, spots[a], :] = (scores[i]).astype(BF16)
        t_out[h, spots[a], :] = (inverse[i]).astype(BF16)
        qe_out[h, spots[a], :] = (query[i]).astype(BF16)
        m_out[h, spots[a], :] = (steps[i]).astype(BF16)
    prefix = [eye] * group
    added = [jnp.zeros((width, width), F32)] * group
    for a in range(chunks):
        for h in range(group):
            i = h * chunks + a
            mp_out[h, spots[a], :] = (prefix[h]).astype(BF16)
            bp_out[h, spots[a], :] = (added[h]).astype(BF16)
            if a == 0:
                qh_out[h, spots[a], :] = (query[i]).astype(BF16)
                oh_out[h, spots[a], :] = reach[i][:, width:]
                prefix[h], added[h] = steps[i], states[i][:, width:]
                continue
            out = dot_nn(
                jnp.concatenate([query[i], steps[i]], axis=0),
                jnp.concatenate([prefix[h], added[h]], axis=1),
            )
            qh_out[h, spots[a], :] = (out[:CHUNK, :width]).astype(BF16)
            oh_out[h, spots[a], :] = out[:CHUNK, width:] + reach[i][:, width:]
            prefix[h], added[h] = out[CHUNK:, :width], out[CHUNK:, width:] + states[i][:, width:]
    for h in range(group):
        mtot[h] = prefix[h].astype(BF16)
        btot[h] = added[h].astype(BF16)


def hop_kernel(step, extra, state, out, *, flip):
    for head in range(step.shape[0]):
        dot = dot_tn if flip else dot_nn
        out[head] = (dot(step[head], state[head]) + extra[head].astype(F32)).astype(BF16)


def chain_kernel(first, second, out):
    for head in range(first.shape[0]):
        out[head] = dot_nn(second[head], first[head]).astype(BF16)


def attend_kernel(meta, qh, oh, state, gain, w_own, w_oth, heads_slot, o_out, *rest):
    pieces, low = rest[:-1], rest[-1]
    heads, rows, width = qh.shape
    for head in range(heads):
        out = dot_nn(qh[head], state[head]) + oh[head]
        o_out[head] = out
        scale = lax.rsqrt(jnp.mean(out * out, axis=-1, keepdims=True) + EPS)
        low[:, head * width : (head + 1) * width] = (out * scale * gain[...]).astype(BF16)
    count = rows // len(pieces)
    own, oth = halves(meta, w_own.shape[0])
    for slot, piece in enumerate(pieces):
        part = low[row_of(meta, slot, count), :]
        heads_slot[pl.ds(slot * count, count), :] = part
        piece[:, own] = dot_nt(part, w_own[...]).astype(BF16)
        piece[:, oth] = dot_nt(part, w_oth[...]).astype(BF16)


def norm_two_kernel(a, b, c, d, tok, gain, hidden_out, normed_out):
    total = a[...].astype(F32) + b[...].astype(F32) + c[...].astype(F32) + d[...].astype(F32)
    hidden = tok[...].astype(F32) + total
    scale = lax.rsqrt(jnp.mean(hidden * hidden, axis=-1, keepdims=True) + EPS)
    hidden_out[...] = hidden
    normed_out[...] = (hidden * scale * gain[...]).astype(BF16)


def add_kernel(mine, came, hidden, out):
    out[...] = (hidden[...] + (mine[...] + came[...].astype(F32))).astype(BF16)


def norm_back(grad, values, gain):
    scale = lax.rsqrt(jnp.mean(values * values, axis=-1, keepdims=True) + EPS)
    normal = values * scale
    hat = grad * gain
    back = scale * (hat - normal * jnp.mean(hat * normal, axis=-1, keepdims=True))
    return back, jnp.sum(grad * normal, axis=0, keepdims=True)


def norm_two_back_kernel(meta, a, b, c, d, hidden, cot, gain, grad_hidden, grad_att, d_gain):
    total = a[...].astype(F32) + b[...].astype(F32) + c[...].astype(F32) + d[...].astype(F32)
    back, d_gain[...] = norm_back(total, hidden[...], gain[...])
    places = meta[3] + meta[6] + lax.broadcasted_iota(jnp.int32, (hidden.shape[0], 1), 0)
    grad = cot[...].astype(F32) * (places < meta[2]).astype(F32) + back
    grad_hidden[...] = grad
    grad_att[...] = grad.astype(BF16)


def norm_one_back_kernel(a, b, c, d, tok, gain, grad_hidden, d_ffn, d_head, d_tok):
    total = a[...].astype(F32) + b[...].astype(F32) + c[...].astype(F32) + d[...].astype(F32)
    back, d_gain = norm_back(total, tok[...].astype(F32), gain[...])
    rows, width = tok.shape
    d_tok[pl.ds(0, rows), :] = (grad_hidden[...] + back).astype(BF16)
    line = lax.broadcasted_iota(jnp.int32, (RIM, width), 0)
    head = jnp.concatenate([d_head[...], jnp.zeros((1, width - d_head.shape[1]), F32)], axis=1)
    sums = jnp.where(line == 0, d_gain, jnp.where(line == 1, d_ffn[...], jnp.where(line == 2, head, 0.0)))
    d_tok[pl.ds(rows, RIM), :] = sums.astype(BF16)


def copy_kernel(value, out):
    out[...] = value[...]


def place_last_kernel(meta, a, b, c, d, out, sums):
    rows = a.shape[0] - RIM
    total = None
    for slot, piece in enumerate((a, b, c, d)):
        out[row_of(meta, slot, rows), :] = piece[pl.ds(0, rows), :]
        part = piece[pl.ds(rows, RIM), :].astype(F32)
        total = part if total is None else total + part
    sums[...] = total[: sums.shape[0]]


def place_kernel(meta, a, b, c, d, out):
    rows = a.shape[0]
    for slot, piece in enumerate((a, b, c, d)):
        out[row_of(meta, slot, rows), :] = piece[...]


def grad_act_kernel(meta, cot, w_own, w_oth, low_out, act_out, low_oth):
    rows, width = cot.shape
    slots = 4
    count = rows // slots
    for slot in range(slots):
        at = row_of(meta, slot, count)
        places = meta[3] + meta[6 + slot] + lax.broadcasted_iota(jnp.int32, (count, 1), 0)
        keep = (places < meta[2]).astype(F32)
        low_out[pl.ds(slot * count, count), :] = (cot[at, :].astype(F32) * keep).astype(BF16)
    own, oth = halves(meta, width // 2)
    low_oth[...] = low_out[:, oth]

    @pl.loop(0, 2)
    def _(step):
        at = pl.ds(pl.multiple_of(step * (rows // 2), rows // 2), rows // 2)
        act_out[at, :] = dot_nn(low_out[at, own], w_own[...]) + dot_nn(low_out[at, oth], w_oth[...])


def ffn_kernel(meta, a, b, c, d, g_own, g_oth, u_own, u_oth, grad_act, n_out, n_oth, wide_out, *pieces):
    count, width = a.shape
    for slot, source in enumerate((a, b, c, d)):
        n_out[pl.ds(slot * count, count), :] = source[...]
    own, oth = halves(meta, width // 2)
    n_oth[...] = n_out[:, oth]
    units = g_own.shape[1]
    for part in range(2):
        at = pl.ds(part * 2 * count, 2 * count)
        left, right = n_out[at, own], n_out[at, oth]
        gate = dot_nn(left, g_own[...]) + dot_nn(right, g_oth[...])
        up = dot_nn(left, u_own[...]) + dot_nn(right, u_oth[...])
        sig = jax.nn.sigmoid(gate)
        wide_out[at, :units] = (gate * sig * up).astype(BF16)
        grad = grad_act[at, :]
        grad_gate = (grad * up * sig * (1.0 + gate * (1.0 - sig))).astype(BF16)
        grad_up = (grad * gate * sig).astype(BF16)
        wide_out[at, units : 2 * units] = grad_gate
        wide_out[at, 2 * units :] = grad_up
        for side, gate_side, up_side in ((own, g_own, u_own), (oth, g_oth, u_oth)):
            total = (dot_nt(grad_gate, gate_side[...]) + dot_nt(grad_up, up_side[...])).astype(BF16)
            pieces[2 * part][:, side] = total[:count]
            pieces[2 * part + 1][:, side] = total[count:]


def down_kernel(meta, wide, w_own, w_oth, keep, give):
    act = wide[:, : w_own.shape[1]]
    count = keep.shape[0] // 2
    own, oth = halves(meta, w_own.shape[0])
    for side, weight in ((own, w_own), (oth, w_oth)):
        total = dot_nt(act, weight[...]).astype(BF16)
        for slot, out in enumerate((keep, give, keep, give)):
            out[pl.ds(slot // 2 * count, count), side] = total[slot * count : (slot + 1) * count]


def add_half_kernel(keep, came, mine, other):
    count = mine.shape[0]
    total = keep[...].astype(F32) + came[...].astype(F32)
    mine[...] = total[:count]
    other[...] = total[count:].astype(BF16)


def heads_back_kernel(
    meta, g0, g1, g2, g3, w_own, w_oth, o_in, gain, qe, qh, grad_o, d_chunk, d_total, d_gain, cat_out, cat_oth, grad
):
    heads, rows, width = o_in.shape
    count = g0.shape[0]
    own, oth = halves(meta, w_own.shape[0])
    for slot, source in enumerate((g0, g1, g2, g3)):
        cat_out[pl.ds(slot * count, count), :] = source[...]
    cat_oth[...] = cat_out[:, oth]
    whole = dot_nn(cat_out[:, own], w_own[...]) + dot_nn(cat_out[:, oth], w_oth[...])
    for slot in range(4):
        grad[row_of(meta, slot, count), :] = whole[slot * count : (slot + 1) * count]
    total_gain = jnp.zeros((1, width), F32)
    for head in range(heads):
        out = o_in[head]
        back, part = norm_back(grad[:, head * width : (head + 1) * width], out, gain[...])
        total_gain = total_gain + part
        grad_o[head] = back
        d_total[head] = dot_tn(qh[head], back).astype(BF16)
        for at in range(rows // CHUNK):
            here = slice(at * CHUNK, (at + 1) * CHUNK)
            d_chunk[head, here, :] = dot_tn(qe[head, here, :], back[here])
    d_gain[...] = total_gain


def delta_back_kernel(
    meta, ext, taps, logits,
    w_in, u_in, p_in, t_in, m_in, mp_in, bp_in, s_in, do_in, dc_in, *rest,
):
    grads_in, rest = rest[:-5], rest[-5:]
    grad_ext, grad_rim, grad_tail, d_taps, pad = rest
    group, rows, width = w_in.shape
    places, sames = tap_masks(meta, rows)
    keep = (places < meta[2]).astype(F32)
    root = 1.0 / math.sqrt(width)
    chunks = rows // CHUNK
    spots = [slice(at * CHUNK, (at + 1) * CHUNK) for at in range(chunks)]
    masks = [chunk_masks(meta, at) for at in range(chunks)]
    chains = [(head, at) for head in range(group) for at in range(chunks)]
    q, k, v, b, sig_b, scale_q, scale_k = [], [], [], [], [], [], []
    for head in range(group):
        lanes = slice(head * width, (head + 1) * width)
        scale, unit = unit_parts(silu_parts(conv_rows(ext, taps, 0, lanes, rows, sames))[1])
        scale_q.append(scale)
        q.append(unit)
        scale, unit = unit_parts(silu_parts(conv_rows(ext, taps, 1, lanes, rows, sames))[1])
        scale_k.append(scale)
        k.append(unit)
        v.append(silu_parts(conv_rows(ext, taps, 2, lanes, rows, sames))[1])
        sig_b.append(jax.nn.sigmoid(pick_column(logits[...], head)))
        b.append(sig_b[head] * keep)
    after = {}
    for head in range(group):
        total = grads_in[0][head].astype(F32)
        for grad, step in zip(grads_in[1 : (len(grads_in) + 1) // 2], grads_in[(len(grads_in) + 1) // 2 :]):
            total = total + dot_tn(step[head], grad[head].astype(F32))
        after[head, chunks - 1] = total
    for at in range(chunks - 1, 0, -1):
        for head in range(group):
            after[head, at - 1] = dot_tn(m_in[head, spots[at], :], after[head, at]) + dc_in[head, spots[at], :]
    grad_state = [after[c] for c in chains]
    state = [dot_nn(mp_in[h, spots[a], :], s_in[h]) + bp_in[h, spots[a], :].astype(F32) for h, a in chains]
    kc = [k[h][spots[a]] for h, a in chains]
    grad_o = [do_in[h, spots[a], :] for h, a in chains]
    fresh = [
        u_in[h, spots[a], :].astype(F32) - masks[a][2] * dot_nn(w_in[h, spots[a], :], s)
        for (h, a), s in zip(chains, state)
    ]
    d_fresh = [
        dot_tn(p_in[h, spots[a], :], g) + masks[a][3] * dot_nn(x, s)
        for (h, a), g, x, s in zip(chains, grad_o, kc, grad_state)
    ]
    d_scores = [dot_nt(g, f) * masks[a][1] for (h, a), g, f in zip(chains, grad_o, fresh)]
    back = [
        dot_nt(jnp.concatenate([masks[a][2] * g, masks[a][2] * f], axis=0), s)
        for (h, a), g, f, s in zip(chains, grad_o, d_fresh, state)
    ]
    d_q = [x[:CHUNK] + dot_nn(d, y) for x, d, y in zip(back, d_scores, kc)]
    d_k = [
        root * dot_tn(d, q[h][spots[a]]) + dot_nt(masks[a][3] * f, s)
        for (h, a), d, f, s in zip(chains, d_scores, fresh, grad_state)
    ]
    right = [
        dot_tn(t_in[h, spots[a], :], jnp.concatenate([-x[CHUNK:], f], axis=1))
        for (h, a), x, f in zip(chains, back, d_fresh)
    ]
    d_gram = [
        -masks[a][0] * dot_nt(r, jnp.concatenate([w_in[h, spots[a], :], u_in[h, spots[a], :]], axis=1))
        for (h, a), r in zip(chains, right)
    ]
    d_scaled = [r[:, :width] + dot_nn(g, x) for r, g, x in zip(right, d_gram, kc)]
    d_k = [
        x + dot_tn(g, b[h][spots[a]] * y) + b[h][spots[a]] * d
        for (h, a), x, g, y, d in zip(chains, d_k, d_gram, kc, d_scaled)
    ]
    d_b = [
        jnp.sum(d * y + r[:, width:] * v[h][spots[a]], axis=1, keepdims=True)
        for (h, a), d, y, r in zip(chains, d_scaled, kc, right)
    ]
    d_v = [b[h][spots[a]] * r[:, width:] for (h, a), r in zip(chains, right)]
    lane = lax.broadcasted_iota(jnp.int32, (rows, LANES), 1)
    all_logits = jnp.zeros((rows, LANES), F32)
    zeros = jnp.zeros((RIM, width), F32)
    heads_width = grad_ext.shape[1] // 3 // LANES * LANES
    for head in range(group):
        mine = slice(head * chunks, (head + 1) * chunks)
        lanes = slice(head * width, (head + 1) * width)
        d_logit = jnp.concatenate(d_b[mine], axis=0) * keep * sig_b[head] * (1.0 - sig_b[head])
        all_logits = jnp.where(lane == head, d_logit, all_logits)
        g_q, g_k, g_v = (jnp.concatenate(x[mine], axis=0) for x in (d_q, d_k, d_v))
        g_q = root * scale_q[head] * (g_q - q[head] * jnp.sum(g_q * q[head], axis=-1, keepdims=True))
        g_k = scale_k[head] * (g_k - k[head] * jnp.sum(g_k * k[head], axis=-1, keepdims=True))
        for block, grad in enumerate((g_q, g_k, g_v)):
            spot = head * 3 + block
            at = slice(block * heads_width + head * width, block * heads_width + (head + 1) * width)
            pad[spot, pl.ds(0, RIM), :] = zeros
            pad[spot, pl.ds(RIM + rows, RIM), :] = zeros
            mixed = conv_rows(ext, taps, block, lanes, rows, sames)
            sig = silu_parts(mixed)[0]
            d_mixed = grad * sig * (1.0 + mixed * (1.0 - sig))
            total = jnp.zeros((rows + RIM, width), F32)
            for j in range(TAPS):
                masked = d_mixed * sames[j]
                pad[spot, pl.ds(RIM, rows), :] = masked
                total = total + taps[block, j : j + 1, lanes] * pad[spot, pl.ds(j, rows + RIM), :]
                d_taps[block, j : j + 1, lanes] = jnp.sum(
                    masked * ext[RIM - j : RIM - j + rows, at], axis=0, keepdims=True
                )
            grad_ext[:, at] = total.astype(BF16)
            grad_rim[:, at] = total[:RIM]
            grad_tail[:, at] = total[rows:]
    grad_ext[pl.ds(RIM, rows), 3 * heads_width :] = all_logits.astype(BF16)
    grad_ext[pl.ds(0, RIM), 3 * heads_width :] = jnp.zeros((RIM, LANES), BF16)


def back_project_kernel(
    meta, grad_ext, tail, returned, wq, wk, wv, wb, xq, xk, xv, xb, *rest
):
    pieces, grad = rest[:-1], rest[-1]
    count = pieces[0].shape[0]
    chan = wq.shape[1]
    for slot in range(len(pieces)):
        here = pl.ds(slot * count, count)
        start = pl.multiple_of(meta[6 + slot], count)
        grad[here, :] = grad_ext[pl.ds(pl.multiple_of(start + RIM, RIM), count), :]
    last = pl.multiple_of(meta[6 + len(pieces) - 1] + count - RIM, RIM)
    grad[pl.ds(last, RIM), : 3 * chan] = (tail[...] + returned[...]).astype(BF16)
    own, oth = halves(meta, wq.shape[0])
    for side, weights in ((own, (wq, wk, wv, wb)), (oth, (xq, xk, xv, xb))):
        total = dot_nt(grad[:, 3 * chan : 3 * chan + weights[3].shape[1]], weights[3][...])
        for block in range(3):
            total = total + dot_nt(grad[:, block * chan : (block + 1) * chan], weights[block][...])
        total = total.astype(BF16)
        for slot, piece in enumerate(pieces):
            piece[:, side] = total[slot * count : (slot + 1) * count]


def ffn_grad_kernel(meta, low, low_sib, normed, normed_sib, wide, wide_sib, out):
    own = halves(meta, out.shape[0])[0]
    units = wide.shape[1] // 3
    lows = jnp.concatenate([low[:, own], low_sib[...]], axis=0)
    norms = jnp.concatenate([normed[:, own], normed_sib[...]], axis=0)
    for at, left in enumerate((lows, norms, norms)):
        here = slice(at * units, (at + 1) * units)
        out[:, here] = dot_tn(left, jnp.concatenate([wide[:, here], wide_sib[:, here]], axis=0)).astype(BF16)


def proj_grad_kernel(
    meta, normed, grad, normed_sib, grad_sib, grad_att, heads, grad_att_sib, heads_sib, out
):
    half, columns = out.shape[0], grad.shape[1]
    own = halves(meta, half)[0]
    out[:, :columns] = (
        dot_tn(normed[:, own], grad[...]) + dot_tn(normed_sib[...], grad_sib[...])
    ).astype(BF16)
    out[:, columns:] = (
        dot_tn(grad_att[:, own], heads[...]) + dot_tn(grad_att_sib[...], heads_sib[...])
    ).astype(BF16)


def flipped(value, axis, bit):
    return lax.ppermute(value, axis, [(i, i ^ bit) for i in range(lax.axis_size(axis))])


def shifted(value, axis, by, reach=None):
    length = lax.axis_size(axis)
    pairs = [(i, i + by) for i in range(length) if 0 <= i + by < length]
    if reach is not None:
        pairs = [pair for pair in pairs if reach(pair[0])]
    return lax.ppermute(value, axis, pairs)


def exchanged(pieces):
    return [pieces[0]] + [flipped(piece, "tp", slot) for slot, piece in enumerate(pieces) if slot]


def gathered(piece):
    return [piece] + [flipped(piece, "tp", slot) for slot in range(1, lax.axis_size("tp"))]


def summed(value, axis):
    bit = 1
    while bit < lax.axis_size(axis):
        value = value + flipped(value, axis, bit)
        bit *= 2
    return value


def contract_rows(left_side, right_side):
    return lax.dot_general(
        left_side, right_side, (((0,), (0,)), ((), ())), preferred_element_type=F32
    )


def scattered(value):
    return lax.psum_scatter(value, "ctx", scatter_dimension=0, tiled=True)


def line_kernel(meta, value, *rest, step, last):
    rights, lefts = rest[-2:]
    rows = rights.shape[0]
    place = meta[meta.shape[0] - 1]
    for out, due, came in zip((rights, lefts), (last - step + place, place - last + step), rest[:-2] or (None, None)):
        start = pl.multiple_of(jnp.clip(due, 0, last) * rows, rows)
        part = value[pl.ds(start, rows), :]
        if came is not None:
            part = (part.astype(F32) + came[...].astype(F32)).astype(BF16)
        out[...] = part


def line_step(meta, value, step, came, after=()):
    last = lax.axis_size("ctx") - 1
    part = shape(value.shape[0] // (last + 1), value.shape[1], dtype=BF16)
    right, left = call(
        functools.partial(line_kernel, step=step, last=last), [part, part], (meta, value, *came), after=after
    )
    return right, (
        shifted(right, "ctx", 1, lambda i: i <= step),
        shifted(left, "ctx", -1, lambda i: i >= last - step),
    )


def line_total(value, place, came):
    rows = value.shape[0] // lax.axis_size("ctx")
    total = lax.dynamic_slice_in_dim(value, place * rows, rows, 0).astype(F32)
    return total + came[0].astype(F32) + came[1].astype(F32)


def shards(
    tokens, seq_bounds, w_query, w_key, w_value, w_beta, conv_taps, out_gain, w_out,
    attn_gain, ffn_gain, w_gate, w_up, w_down, cotangent,
):
    rows, width = tokens.shape
    half = w_query.shape[0]
    chan = w_query.shape[1]
    heads = w_beta.shape[1]
    dim = out_gain.shape[0]
    units = w_gate.shape[1]
    slots = lax.axis_size("tp")
    count = rows // slots
    core, place, member = lax.axis_index("fsdp"), lax.axis_index("ctx"), lax.axis_index("tp")
    meta = jnp.concatenate(
        [
            seq_bounds[0],
            jnp.stack(
                [place * rows, core * half, (1 - core) * half]
                + [(member ^ slot) * count for slot in range(slots)]
                + [place]
            ).astype(jnp.int32),
        ]
    )
    attn_row, ffn_row, out_row = attn_gain[None, :], ffn_gain[None, :], out_gain[None, :]

    rim = shifted(tokens[rows - RIM :], "ctx", 1)
    x_query, x_key, x_value, x_beta = (flipped(w, "fsdp", 1) for w in (w_query, w_key, w_value, w_beta))
    tok_own = lax.dynamic_slice_in_dim(tokens, member * count, count, 0)
    cot_own = lax.dynamic_slice_in_dim(cotangent, member * count, count, 0)

    normed, proj, logits, normed_oth = call(
        project_kernel,
        [
            shape(rows + RIM, width, dtype=BF16),
            shape(rows + RIM, 3 * chan),
            shape(rows, heads),
            shape(rows + RIM, half, dtype=BF16),
        ],
        (meta, tokens, rim, attn_row, w_query, w_key, w_value, w_beta, x_query, x_key, x_value, x_beta),
        flops=2 * rows * width * 3 * chan,
        vmem=58,
    )
    later = lax.optimization_barrier((w_down, w_gate, w_up, normed_oth))
    x_out = flipped(w_out, "fsdp", 1)
    x_down, x_gate, x_up = (flipped(w, "fsdp", 1) for w in later[:3])
    normed_oth = later[3]
    tall, small = shape(heads, rows, dim), shape(heads, dim, dim, dtype=BF16)
    erase, write, scores, inverse, query_eff, step, prefix, added, query_hat, out_hat, m_total, b_total = call(
        delta_kernel,
        [shape(heads, rows, dim, dtype=BF16)] * 9 + [tall] + [small] * 2,
        (meta, proj, conv_taps, logits),
        flops=heads * 60 * rows * dim * dim,
        vmem=58,
    )

    def hop(matrix, extra, state, flip, after=()):
        return call(
            functools.partial(hop_kernel, flip=flip),
            shape(heads, dim, dim, dtype=BF16),
            (matrix, extra, state),
            flops=2 * heads * dim**3,
            scalars=False,
            after=after,
        )

    state = jnp.zeros((heads, dim, dim), BF16)
    for index in range(lax.axis_size("ctx") - 1):
        sent = b_total if index == 0 else hop(m_total, b_total, state, False)
        state = shifted(sent, "ctx", 1)

    piece_shape = shape(count, width, dtype=BF16)
    normed_sib = flipped(normed_oth, "fsdp", 1)
    heads_slot, heads_out, *pieces = call(
        attend_kernel,
        [shape(rows, chan, dtype=BF16), tall] + [piece_shape] * slots,
        (meta, query_hat, out_hat, state, out_row, w_out, x_out),
        flops=2 * rows * width * chan,
        after=(x_down, x_gate, x_up, normed_sib),
        scratch=[VMEM((rows, chan), BF16)],
    )
    grad_low, grad_act, low_oth = call(
        grad_act_kernel,
        [shape(rows, width, dtype=BF16), shape(rows, units), shape(rows, half, dtype=BF16)],
        (meta, cotangent, w_down, x_down),
        flops=2 * rows * width * units,
        after=(heads_slot,),
    )
    heads_sib, low_sib = flipped(heads_slot, "fsdp", 1), flipped(low_oth, "fsdp", 1)
    hidden, normed_two = call(
        norm_two_kernel,
        [shape(count, width), piece_shape],
        (*exchanged(pieces), tok_own, ffn_row),
        scalars=False,
    )
    maps = None
    if lax.axis_size("ctx") == 4:
        near = shifted(m_total, "ctx", -1)
        chained = call(chain_kernel, small, (m_total, near), scalars=False, after=(normed_two,))
        maps = (near, shifted(chained, "ctx", -1))
    normed_slot, two_oth, wide, *pieces = call(
        ffn_kernel,
        [
            shape(rows, width, dtype=BF16),
            shape(rows, half, dtype=BF16),
            shape(rows, 3 * units, dtype=BF16),
        ]
        + [piece_shape] * slots,
        (meta, *gathered(normed_two), w_gate, x_gate, w_up, x_up, grad_act),
        flops=8 * rows * width * units,
        after=(*(maps or ()), low_sib),
    )
    two_sib, wide_sib = flipped(two_oth, "fsdp", 1), flipped(wide, "fsdp", 1)
    received = exchanged(pieces)
    grad_hidden, grad_att, d_ffn_part = call(
        norm_two_back_kernel,
        [shape(count, width), piece_shape, shape(1, width)],
        (meta, *received, hidden, cot_own, ffn_row),
    )
    ffn_pair = call(
        ffn_grad_kernel,
        shape(half, 3 * units, dtype=BF16),
        (meta, grad_low, low_sib, normed_slot, two_sib, wide, wide_sib),
        flops=4 * rows * half * 3 * units,
    )
    ffn_sum = scattered(ffn_pair)
    down_keep, down_give = call(
        down_kernel,
        [shape(2 * count, width, dtype=BF16)] * 2,
        (meta, wide, w_down, x_down),
        flops=2 * rows * width * units,
        after=(grad_att,),
    )
    grad_o, d_chunk, d_total, d_head_part, grad_att_slot, att_oth = call(
        heads_back_kernel,
        [tall, tall, small, shape(1, dim), shape(rows, width, dtype=BF16), shape(rows, half, dtype=BF16)],
        (meta, *gathered(grad_att), w_out, x_out, heads_out, out_row, query_eff, query_hat),
        flops=2 * rows * width * chan,
        scratch=[VMEM((rows, chan), F32)],
        after=(ffn_pair, down_keep),
    )
    if maps is None:
        grad_state = jnp.zeros((heads, dim, dim), BF16)
        for index in range(lax.axis_size("ctx") - 1):
            sent = d_total if index == 0 else hop(m_total, d_total, grad_state, True)
            grad_state = shifted(sent, "ctx", -1)
        gathered_grads = (grad_state,)
    else:
        sent = d_total
        gathered_grads = tuple(shifted(sent, "ctx", -by) for by in range(1, lax.axis_size("ctx")))
    down_mine, down_other = call(
        add_half_kernel,
        [shape(count, width), piece_shape],
        (down_keep, flipped(down_give, "tp", 1)),
        scalars=False,
        after=(d_total,),
    )
    att_sib = flipped(att_oth, "fsdp", 1)

    grad_ext, grad_rim, grad_tail, d_conv_part = call(
        delta_back_kernel,
        [
            shape(rows + RIM, 3 * chan + LANES, dtype=BF16),
            shape(RIM, 3 * chan),
            shape(RIM, 3 * chan),
            shape(3, TAPS, chan),
        ],
        (
            meta, proj, conv_taps, logits,
            erase, write, scores, inverse, step, prefix, added, state, grad_o, d_chunk,
            *gathered_grads, *(maps or ()),
        ),
        flops=heads * 60 * rows * dim * dim,
        scratch=[VMEM((3 * heads, rows + 2 * RIM, dim), F32)],
        after=(att_sib, down_other),
    )
    returned = shifted(grad_rim, "ctx", -1)
    grad_sib = flipped(grad_ext, "fsdp", 1)
    proj_pair = call(
        proj_grad_kernel,
        shape(half, 4 * chan + LANES, dtype=BF16),
        (meta, normed, grad_ext, normed_sib, grad_sib, grad_att_slot, heads_slot, att_sib, heads_sib),
        flops=4 * rows * half * 4 * chan,
    )
    out_own = call(
        add_kernel,
        piece_shape,
        (down_mine, flipped(down_other, "tp", 2), hidden),
        scalars=False,
        after=(returned, proj_pair),
    )
    pieces = call(
        back_project_kernel,
        [piece_shape] * slots,
        (
            meta, grad_ext, grad_tail, returned,
            w_query, w_key, w_value, w_beta, x_query, x_key, x_value, x_beta,
        ),
        flops=2 * rows * width * 3 * chan,
        scratch=[VMEM((rows, 3 * chan + LANES), BF16)],
        after=(out_own,),
    )
    sent, came = line_step(meta, proj_pair, 0, (), after=(returned,))
    d_tok_own = call(
        norm_one_back_kernel,
        shape(count + RIM, width, dtype=BF16),
        (*exchanged(pieces), tok_own, attn_row, grad_hidden, d_ffn_part, d_head_part),
        scalars=False,
        after=(sent,),
    )
    tok_slots = gathered(d_tok_own)
    sent, came = line_step(meta, proj_pair, 1, came)
    d_tokens, gains = call(
        place_last_kernel,
        [shape(rows, width, dtype=BF16), shape(8, width)],
        (meta, *tok_slots),
        after=(ffn_sum,),
    )
    conv_rows_count = 3 * TAPS * chan // width
    bundle = summed(
        jnp.concatenate([gains, d_conv_part.reshape(conv_rows_count, width)], axis=0), "fsdp"
    )
    if lax.axis_size("ctx") == 4:
        bundle = bundle + sum(flipped(bundle, "ctx", bit) for bit in (1, 2, 3))
    else:
        bundle = summed(bundle, "ctx")
    for step in range(2, lax.axis_size("ctx") - 1):
        sent, came = line_step(meta, proj_pair, step, came, after=(bundle,))
    out_late = call(copy_kernel, piece_shape, (out_own,), scalars=False, after=(d_tokens, sent))
    out = call(place_kernel, shape(rows, width, dtype=BF16), (meta, *gathered(out_late)))
    proj_sum, ffn_sum = line_total(proj_pair, place, came), ffn_sum.astype(F32)
    return (
        out,
        d_tokens,
        proj_sum[:, :chan],
        proj_sum[:, chan : 2 * chan],
        proj_sum[:, 2 * chan : 3 * chan],
        proj_sum[:, 3 * chan : 3 * chan + heads],
        bundle[8:].reshape(3, TAPS, chan),
        bundle[2, :dim],
        proj_sum[:, 3 * chan + LANES :],
        bundle[0],
        bundle[1],
        ffn_sum[:, units : 2 * units],
        ffn_sum[:, 2 * units :],
        ffn_sum[:, :units],
    )


def solution(mesh):
    both = P(("fsdp", "ctx"), None)
    weight = P("fsdp", "tp")
    grad = P(("fsdp", "ctx"), "tp")
    in_specs = (
        both, P("fsdp", None), weight, weight, weight, weight, P(None, None, "tp"), P(), weight,
        P(), P(), weight, weight, weight, both,
    )
    out_specs = (
        both, both, grad, grad, grad, grad, P(None, None, "tp"), P(), grad, P(), P(), grad, grad, grad,
    )
    return jax.shard_map(shards, mesh=mesh, in_specs=in_specs, out_specs=out_specs, check_vma=False)
```

```python
import functools
import math

import jax
import jax.numpy as jnp
from jax import lax
from jax.experimental import pallas as pl
from jax.experimental.pallas import tpu as pltpu
from jax.sharding import PartitionSpec as P

EPS = 1e-06
HIGH = True
F32 = jnp.float32
BF16 = jnp.bfloat16
CHUNK = 128
LANES = 128
RIM = 16
TAPS = 4
VMEM = pltpu.VMEM
WHOLE = pl.BlockSpec(memory_space=pltpu.VMEM)
SCALARS = pl.BlockSpec(memory_space=pltpu.SMEM)


def split(value):
    high = value.astype(BF16)
    return high, (value - high.astype(F32)).astype(BF16)


def product(dims, left, right, exact):
    def one(a, b):
        return lax.dot_general(a, b, (dims, ((), ())), preferred_element_type=F32)

    if not exact:
        return one(left.astype(BF16), right.astype(BF16))
    (left_hi, left_lo), (right_hi, right_lo) = split(left), split(right)
    return one(left_hi, right_hi) + (one(left_hi, right_lo) + one(left_lo, right_hi))


def dot_nn(left, right, exact=False):
    return product(((1,), (0,)), left, right, exact)


def dot_nt(left, right, exact=False):
    return product(((1,), (1,)), left, right, exact)


def dot_tn(left, right, exact=False):
    return product(((0,), (0,)), left, right, exact)


def call(kernel, out_shape, operands, flops=0, scratch=(), scalars=True, after=(), vmem=30):
    outs = out_shape if isinstance(out_shape, list) else [out_shape]
    size = sum(math.prod(x.shape) * x.dtype.itemsize for x in (*operands, *outs))
    given = len(operands)

    def body(*refs):
        kernel(*refs[:given], *refs[given + len(after) :])

    return pl.pallas_call(
        body,
        out_shape=out_shape,
        in_specs=[SCALARS] * scalars
        + [WHOLE] * (given - scalars)
        + [pl.BlockSpec(memory_space=pl.ANY)] * len(after),
        out_specs=[WHOLE] * len(outs) if isinstance(out_shape, list) else WHOLE,
        scratch_shapes=list(scratch),
        name=getattr(kernel, "func", kernel).__name__,
        cost_estimate=pl.CostEstimate(
            flops=flops, bytes_accessed=size, transcendentals=0
        ),
        compiler_params=pltpu.CompilerParams(vmem_limit_bytes=vmem << 20),
    )(*operands, *after)


def shape(*dims, dtype=F32):
    return jax.ShapeDtypeStruct(dims, dtype)


def seg_of(places, meta):
    ids = (
        (places >= meta[0]).astype(jnp.int32)
        + (places >= meta[1]).astype(jnp.int32)
        + (places >= meta[2]).astype(jnp.int32)
    )
    return jnp.where(places < 0, -1, ids)


def row_of(meta, slot, rows):
    return pl.ds(pl.multiple_of(meta[6 + slot], rows), rows)


def halves(meta, half):
    return (
        pl.ds(pl.multiple_of(meta[4], half), half),
        pl.ds(pl.multiple_of(meta[5], half), half),
    )


def project_kernel(meta, tok, rim, gain, wq, wk, wv, wb, xq, xk, xv, xb, ext, proj, logits, ext_oth):
    rows, width = tok.shape
    for source, at, count in ((rim, 0, RIM), (tok, RIM, rows)):
        values = source[...].astype(F32)
        scale = lax.rsqrt(jnp.mean(values * values, axis=-1, keepdims=True) + EPS)
        ext[pl.ds(at, count), :] = (values * scale * gain[...]).astype(BF16)
    own, oth = halves(meta, width // 2)
    left, right = ext[:, own], ext[:, oth]
    ext_oth[...] = right
    chan = wq.shape[1]
    for at, (a, b) in enumerate(((wq, xq), (wk, xk), (wv, xv))):
        proj[:, at * chan : (at + 1) * chan] = dot_nn(left, a[...]) + dot_nn(right, b[...])
    logits[...] = dot_nn(left[RIM:], wb[...]) + dot_nn(right[RIM:], xb[...])


def conv_rows(ext, taps, block, lanes, rows, sames):
    start = block * taps.shape[2]
    columns = slice(start + lanes.start, start + lanes.stop)
    mixed = None
    for j in range(TAPS):
        term = taps[block, j : j + 1, lanes] * ext[RIM - j : RIM - j + rows, columns] * sames[j]
        mixed = term if mixed is None else mixed + term
    return mixed


def tap_masks(meta, rows):
    places = meta[3] + lax.broadcasted_iota(jnp.int32, (rows, 1), 0)
    seg = seg_of(places, meta)
    return places, [(seg_of(places - j, meta) == seg).astype(F32) for j in range(TAPS)]


def pick_column(values, head):
    lane = lax.broadcasted_iota(jnp.int32, values.shape, 1)
    return jnp.sum(jnp.where(lane == head, values, 0.0), axis=1, keepdims=True)


def chunk_masks(meta, at):
    first = meta[3] + at * CHUNK
    row = lax.broadcasted_iota(jnp.int32, (CHUNK, CHUNK), 0)
    col = lax.broadcasted_iota(jnp.int32, (CHUNK, CHUNK), 1)
    seg_col = seg_of(first + lax.broadcasted_iota(jnp.int32, (CHUNK, 1), 0), meta)
    seg_row = seg_of(first + lax.broadcasted_iota(jnp.int32, (1, CHUNK), 1), meta)
    before = seg_of(first - 1, meta)
    last = seg_of(first + CHUNK - 1, meta)
    same = (seg_col == seg_row).astype(F32)
    strict = jnp.where(row > col, same, 0.0)
    lower = jnp.where(row >= col, same, 0.0)
    carry_in = (seg_col == before).astype(F32)
    tail = (seg_col == last).astype(F32)
    whole = (last == before).astype(F32)
    return strict, lower, carry_in, tail, whole


def unit_inverses(grams):
    row = lax.broadcasted_iota(jnp.int32, (CHUNK, CHUNK), 0)
    col = lax.broadcasted_iota(jnp.int32, (CHUNK, CHUNK), 1)
    eye = (row == col).astype(F32)
    size = 8
    near = [jnp.where(row // size == col // size, g, 0.0) for g in grams]
    power = [dot_nn(n, n) for n in near]
    inverse = [eye - n for n in near]
    inverse = [x + dot_nn(x, p) for x, p in zip(inverse, power)]
    power = [dot_nn(p, p) for p in power]
    inverse = [x + dot_nn(x, p) for x, p in zip(inverse, power)]
    while size < CHUNK:
        off = (row // (2 * size) == col // (2 * size)) & (row // size != col // size)
        inner = [dot_nn(jnp.where(off, g, 0.0), x) for g, x in zip(grams, inverse)]
        inverse = [x - dot_nn(x, y) for x, y in zip(inverse, inner)]
        size *= 2
    resid = [(eye - x) - dot_nn(g, x, HIGH) for g, x in zip(grams, inverse)]
    return [x + dot_nn(x, r) for x, r in zip(inverse, resid)]

def silu_parts(mixed):
    sig = jax.nn.sigmoid(mixed)
    return sig, mixed * sig


def unit_parts(values):
    scale = lax.rsqrt(jnp.sum(values * values, axis=-1, keepdims=True) + EPS)
    return scale, values * scale


def delta_kernel(
    meta, ext, taps, logits,
    w_out, u_out, p_out, t_out, qe_out, m_out, mp_out, bp_out, qh_out, oh_out, mtot, btot,
):
    group, rows, width = w_out.shape
    places, sames = tap_masks(meta, rows)
    keep = (places < meta[2]).astype(F32)
    row = lax.broadcasted_iota(jnp.int32, (width, width), 0)
    col = lax.broadcasted_iota(jnp.int32, (width, width), 1)
    eye = (row == col).astype(F32)
    q, k, v, b = [], [], [], []
    for head in range(group):
        lanes = slice(head * width, (head + 1) * width)
        x = silu_parts(conv_rows(ext, taps, 0, lanes, rows, sames))[1]
        q.append(unit_parts(x)[1] * (1.0 / math.sqrt(width)))
        x = silu_parts(conv_rows(ext, taps, 1, lanes, rows, sames))[1]
        k.append(unit_parts(x)[1])
        v.append(silu_parts(conv_rows(ext, taps, 2, lanes, rows, sames))[1])
        b.append(jax.nn.sigmoid(pick_column(logits[...], head)) * keep)
    chunks = rows // CHUNK
    spots = [slice(at * CHUNK, (at + 1) * CHUNK) for at in range(chunks)]
    masks = [chunk_masks(meta, at) for at in range(chunks)]
    chains = [(head, at) for head in range(group) for at in range(chunks)]
    kc = [k[h][spots[a]] for h, a in chains]
    qc = [q[h][spots[a]] for h, a in chains]
    scaled = [b[h][spots[a]] * k[h][spots[a]] for h, a in chains]
    scaled_v = [b[h][spots[a]] * v[h][spots[a]] for h, a in chains]
    grams = [dot_nt(s, x, HIGH) * masks[a][0] for (h, a), s, x in zip(chains, scaled, kc)]
    scores = [dot_nt(y, x) * masks[a][1] for (h, a), y, x in zip(chains, qc, kc)]
    inverse = unit_inverses(grams)
    both = [dot_nn(t, jnp.concatenate([s, u], axis=1), HIGH) for t, s, u in zip(inverse, scaled, scaled_v)]
    inner = [
        jnp.concatenate([masks[a][2] * x[:, :width], x[:, width:]], axis=1) for (h, a), x in zip(chains, both)
    ]
    states = [dot_tn(x, masks[a][3] * y) for (h, a), x, y in zip(chains, kc, inner)]
    reach = [dot_nn(s, y) for s, y in zip(scores, inner)]
    steps = [masks[a][4] * eye - s[:, :width] for (h, a), s in zip(chains, states)]
    query = [masks[a][2] * x - y[:, :width] for (h, a), x, y in zip(chains, qc, reach)]
    for i, (h, a) in enumerate(chains):
        w_out[h, spots[a], :] = (both[i][:, :width]).astype(BF16)
        u_out[h, spots[a], :] = (both[i][:, width:]).astype(BF16)
        p_out[h, spots[a], :] = (scores[i]).astype(BF16)
        t_out[h, spots[a], :] = (inverse[i]).astype(BF16)
        qe_out[h, spots[a], :] = (query[i]).astype(BF16)
        m_out[h, spots[a], :] = (steps[i]).astype(BF16)
    prefix = [eye] * group
    added = [jnp.zeros((width, width), F32)] * group
    for a in range(chunks):
        for h in range(group):
            i = h * chunks + a
            mp_out[h, spots[a], :] = (prefix[h]).astype(BF16)
            bp_out[h, spots[a], :] = (added[h]).astype(BF16)
            if a == 0:
                qh_out[h, spots[a], :] = (query[i]).astype(BF16)
                oh_out[h, spots[a], :] = reach[i][:, width:]
                prefix[h], added[h] = steps[i], states[i][:, width:]
                continue
            out = dot_nn(
                jnp.concatenate([query[i], steps[i]], axis=0),
                jnp.concatenate([prefix[h], added[h]], axis=1),
            )
            qh_out[h, spots[a], :] = (out[:CHUNK, :width]).astype(BF16)
            oh_out[h, spots[a], :] = out[:CHUNK, width:] + reach[i][:, width:]
            prefix[h], added[h] = out[CHUNK:, :width], out[CHUNK:, width:] + states[i][:, width:]
    for h in range(group):
        mtot[h] = prefix[h].astype(BF16)
        btot[h] = added[h].astype(BF16)


def hop_kernel(step, extra, state, out, *, flip):
    for head in range(step.shape[0]):
        dot = dot_tn if flip else dot_nn
        out[head] = (dot(step[head], state[head]) + extra[head].astype(F32)).astype(BF16)


def chain_kernel(first, second, out):
    for head in range(first.shape[0]):
        out[head] = dot_nn(second[head], first[head]).astype(BF16)


def attend_kernel(meta, qh, oh, state, gain, w_own, w_oth, heads_slot, o_out, *rest):
    pieces, low = rest[:-1], rest[-1]
    heads, rows, width = qh.shape
    for head in range(heads):
        out = dot_nn(qh[head], state[head]) + oh[head]
        o_out[head] = out
        scale = lax.rsqrt(jnp.mean(out * out, axis=-1, keepdims=True) + EPS)
        low[:, head * width : (head + 1) * width] = (out * scale * gain[...]).astype(BF16)
    count = rows // len(pieces)
    own, oth = halves(meta, w_own.shape[0])
    for slot, piece in enumerate(pieces):
        part = low[row_of(meta, slot, count), :]
        heads_slot[pl.ds(slot * count, count), :] = part
        piece[:, own] = dot_nt(part, w_own[...]).astype(BF16)
        piece[:, oth] = dot_nt(part, w_oth[...]).astype(BF16)


def norm_two_kernel(a, b, c, d, tok, gain, hidden_out, normed_out):
    total = a[...].astype(F32) + b[...].astype(F32) + c[...].astype(F32) + d[...].astype(F32)
    hidden = tok[...].astype(F32) + total
    scale = lax.rsqrt(jnp.mean(hidden * hidden, axis=-1, keepdims=True) + EPS)
    hidden_out[...] = hidden
    normed_out[...] = (hidden * scale * gain[...]).astype(BF16)


def add_kernel(mine, came, hidden, out):
    out[...] = (hidden[...] + (mine[...] + came[...].astype(F32))).astype(BF16)


def norm_back(grad, values, gain):
    scale = lax.rsqrt(jnp.mean(values * values, axis=-1, keepdims=True) + EPS)
    normal = values * scale
    hat = grad * gain
    back = scale * (hat - normal * jnp.mean(hat * normal, axis=-1, keepdims=True))
    return back, jnp.sum(grad * normal, axis=0, keepdims=True)


def norm_two_back_kernel(meta, a, b, c, d, hidden, cot, gain, grad_hidden, grad_att, d_gain):
    total = a[...].astype(F32) + b[...].astype(F32) + c[...].astype(F32) + d[...].astype(F32)
    back, d_gain[...] = norm_back(total, hidden[...], gain[...])
    places = meta[3] + meta[6] + lax.broadcasted_iota(jnp.int32, (hidden.shape[0], 1), 0)
    grad = cot[...].astype(F32) * (places < meta[2]).astype(F32) + back
    grad_hidden[...] = grad
    grad_att[...] = grad.astype(BF16)


def norm_one_back_kernel(a, b, c, d, tok, gain, grad_hidden, d_ffn, d_head, d_tok):
    total = a[...].astype(F32) + b[...].astype(F32) + c[...].astype(F32) + d[...].astype(F32)
    back, d_gain = norm_back(total, tok[...].astype(F32), gain[...])
    rows, width = tok.shape
    d_tok[pl.ds(0, rows), :] = (grad_hidden[...] + back).astype(BF16)
    line = lax.broadcasted_iota(jnp.int32, (RIM, width), 0)
    head = jnp.concatenate([d_head[...], jnp.zeros((1, width - d_head.shape[1]), F32)], axis=1)
    sums = jnp.where(line == 0, d_gain, jnp.where(line == 1, d_ffn[...], jnp.where(line == 2, head, 0.0)))
    d_tok[pl.ds(rows, RIM), :] = sums.astype(BF16)


def copy_kernel(value, out):
    out[...] = value[...]


def place_last_kernel(meta, a, b, c, d, out, sums):
    rows = a.shape[0] - RIM
    total = None
    for slot, piece in enumerate((a, b, c, d)):
        out[row_of(meta, slot, rows), :] = piece[pl.ds(0, rows), :]
        part = piece[pl.ds(rows, RIM), :].astype(F32)
        total = part if total is None else total + part
    sums[...] = total[: sums.shape[0]]


def place_kernel(meta, a, b, c, d, out):
    rows = a.shape[0]
    for slot, piece in enumerate((a, b, c, d)):
        out[row_of(meta, slot, rows), :] = piece[...]


def grad_act_kernel(meta, cot, w_own, w_oth, low_out, act_out, low_oth):
    rows, width = cot.shape
    slots = 4
    count = rows // slots
    for slot in range(slots):
        at = row_of(meta, slot, count)
        places = meta[3] + meta[6 + slot] + lax.broadcasted_iota(jnp.int32, (count, 1), 0)
        keep = (places < meta[2]).astype(F32)
        low_out[pl.ds(slot * count, count), :] = (cot[at, :].astype(F32) * keep).astype(BF16)
    own, oth = halves(meta, width // 2)
    low_oth[...] = low_out[:, oth]

    @pl.loop(0, 2)
    def _(step):
        at = pl.ds(pl.multiple_of(step * (rows // 2), rows // 2), rows // 2)
        act_out[at, :] = dot_nn(low_out[at, own], w_own[...]) + dot_nn(low_out[at, oth], w_oth[...])


def ffn_kernel(meta, a, b, c, d, g_own, g_oth, u_own, u_oth, grad_act, n_out, n_oth, wide_out, *pieces):
    count, width = a.shape
    for slot, source in enumerate((a, b, c, d)):
        n_out[pl.ds(slot * count, count), :] = source[...]
    own, oth = halves(meta, width // 2)
    n_oth[...] = n_out[:, oth]
    units = g_own.shape[1]
    for part in range(2):
        at = pl.ds(part * 2 * count, 2 * count)
        left, right = n_out[at, own], n_out[at, oth]
        gate = dot_nn(left, g_own[...]) + dot_nn(right, g_oth[...])
        up = dot_nn(left, u_own[...]) + dot_nn(right, u_oth[...])
        sig = jax.nn.sigmoid(gate)
        wide_out[at, :units] = (gate * sig * up).astype(BF16)
        grad = grad_act[at, :]
        grad_gate = (grad * up * sig * (1.0 + gate * (1.0 - sig))).astype(BF16)
        grad_up = (grad * gate * sig).astype(BF16)
        wide_out[at, units : 2 * units] = grad_gate
        wide_out[at, 2 * units :] = grad_up
        for side, gate_side, up_side in ((own, g_own, u_own), (oth, g_oth, u_oth)):
            total = (dot_nt(grad_gate, gate_side[...]) + dot_nt(grad_up, up_side[...])).astype(BF16)
            pieces[2 * part][:, side] = total[:count]
            pieces[2 * part + 1][:, side] = total[count:]


def down_kernel(meta, wide, w_own, w_oth, keep, give):
    act = wide[:, : w_own.shape[1]]
    count = keep.shape[0] // 2
    own, oth = halves(meta, w_own.shape[0])
    for side, weight in ((own, w_own), (oth, w_oth)):
        total = dot_nt(act, weight[...]).astype(BF16)
        for slot, out in enumerate((keep, give, keep, give)):
            out[pl.ds(slot // 2 * count, count), side] = total[slot * count : (slot + 1) * count]


def add_half_kernel(keep, came, mine, other):
    count = mine.shape[0]
    total = keep[...].astype(F32) + came[...].astype(F32)
    mine[...] = total[:count]
    other[...] = total[count:].astype(BF16)


def heads_back_kernel(
    meta, g0, g1, g2, g3, w_own, w_oth, o_in, gain, qe, qh, grad_o, d_chunk, d_total, d_gain, cat_out, cat_oth, grad
):
    heads, rows, width = o_in.shape
    count = g0.shape[0]
    own, oth = halves(meta, w_own.shape[0])
    for slot, source in enumerate((g0, g1, g2, g3)):
        cat_out[pl.ds(slot * count, count), :] = source[...]
    cat_oth[...] = cat_out[:, oth]
    whole = dot_nn(cat_out[:, own], w_own[...]) + dot_nn(cat_out[:, oth], w_oth[...])
    for slot in range(4):
        grad[row_of(meta, slot, count), :] = whole[slot * count : (slot + 1) * count]
    total_gain = jnp.zeros((1, width), F32)
    for head in range(heads):
        out = o_in[head]
        back, part = norm_back(grad[:, head * width : (head + 1) * width], out, gain[...])
        total_gain = total_gain + part
        grad_o[head] = back
        d_total[head] = dot_tn(qh[head], back).astype(BF16)
        for at in range(rows // CHUNK):
            here = slice(at * CHUNK, (at + 1) * CHUNK)
            d_chunk[head, here, :] = dot_tn(qe[head, here, :], back[here])
    d_gain[...] = total_gain


def delta_back_kernel(
    meta, ext, taps, logits,
    w_in, u_in, p_in, t_in, m_in, mp_in, bp_in, s_in, do_in, dc_in, *rest,
):
    grads_in, rest = rest[:-5], rest[-5:]
    grad_ext, grad_rim, grad_tail, d_taps, pad = rest
    group, rows, width = w_in.shape
    places, sames = tap_masks(meta, rows)
    keep = (places < meta[2]).astype(F32)
    root = 1.0 / math.sqrt(width)
    chunks = rows // CHUNK
    spots = [slice(at * CHUNK, (at + 1) * CHUNK) for at in range(chunks)]
    masks = [chunk_masks(meta, at) for at in range(chunks)]
    chains = [(head, at) for head in range(group) for at in range(chunks)]
    q, k, v, b, sig_b, scale_q, scale_k = [], [], [], [], [], [], []
    for head in range(group):
        lanes = slice(head * width, (head + 1) * width)
        scale, unit = unit_parts(silu_parts(conv_rows(ext, taps, 0, lanes, rows, sames))[1])
        scale_q.append(scale)
        q.append(unit)
        scale, unit = unit_parts(silu_parts(conv_rows(ext, taps, 1, lanes, rows, sames))[1])
        scale_k.append(scale)
        k.append(unit)
        v.append(silu_parts(conv_rows(ext, taps, 2, lanes, rows, sames))[1])
        sig_b.append(jax.nn.sigmoid(pick_column(logits[...], head)))
        b.append(sig_b[head] * keep)
    after = {}
    for head in range(group):
        total = grads_in[0][head].astype(F32)
        for grad, step in zip(grads_in[1 : (len(grads_in) + 1) // 2], grads_in[(len(grads_in) + 1) // 2 :]):
            total = total + dot_tn(step[head], grad[head].astype(F32))
        after[head, chunks - 1] = total
    for at in range(chunks - 1, 0, -1):
        for head in range(group):
            after[head, at - 1] = dot_tn(m_in[head, spots[at], :], after[head, at]) + dc_in[head, spots[at], :]
    grad_state = [after[c] for c in chains]
    state = [dot_nn(mp_in[h, spots[a], :], s_in[h]) + bp_in[h, spots[a], :].astype(F32) for h, a in chains]
    kc = [k[h][spots[a]] for h, a in chains]
    grad_o = [do_in[h, spots[a], :] for h, a in chains]
    fresh = [
        u_in[h, spots[a], :].astype(F32) - masks[a][2] * dot_nn(w_in[h, spots[a], :], s)
        for (h, a), s in zip(chains, state)
    ]
    d_fresh = [
        dot_tn(p_in[h, spots[a], :], g) + masks[a][3] * dot_nn(x, s)
        for (h, a), g, x, s in zip(chains, grad_o, kc, grad_state)
    ]
    d_scores = [dot_nt(g, f) * masks[a][1] for (h, a), g, f in zip(chains, grad_o, fresh)]
    back = [
        dot_nt(jnp.concatenate([masks[a][2] * g, masks[a][2] * f], axis=0), s)
        for (h, a), g, f, s in zip(chains, grad_o, d_fresh, state)
    ]
    d_q = [x[:CHUNK] + dot_nn(d, y) for x, d, y in zip(back, d_scores, kc)]
    d_k = [
        root * dot_tn(d, q[h][spots[a]]) + dot_nt(masks[a][3] * f, s)
        for (h, a), d, f, s in zip(chains, d_scores, fresh, grad_state)
    ]
    right = [
        dot_tn(t_in[h, spots[a], :], jnp.concatenate([-x[CHUNK:], f], axis=1))
        for (h, a), x, f in zip(chains, back, d_fresh)
    ]
    d_gram = [
        -masks[a][0] * dot_nt(r, jnp.concatenate([w_in[h, spots[a], :], u_in[h, spots[a], :]], axis=1))
        for (h, a), r in zip(chains, right)
    ]
    d_scaled = [r[:, :width] + dot_nn(g, x) for r, g, x in zip(right, d_gram, kc)]
    d_k = [
        x + dot_tn(g, b[h][spots[a]] * y) + b[h][spots[a]] * d
        for (h, a), x, g, y, d in zip(chains, d_k, d_gram, kc, d_scaled)
    ]
    d_b = [
        jnp.sum(d * y + r[:, width:] * v[h][spots[a]], axis=1, keepdims=True)
        for (h, a), d, y, r in zip(chains, d_scaled, kc, right)
    ]
    d_v = [b[h][spots[a]] * r[:, width:] for (h, a), r in zip(chains, right)]
    lane = lax.broadcasted_iota(jnp.int32, (rows, LANES), 1)
    all_logits = jnp.zeros((rows, LANES), F32)
    zeros = jnp.zeros((RIM, width), F32)
    heads_width = grad_ext.shape[1] // 3 // LANES * LANES
    for head in range(group):
        mine = slice(head * chunks, (head + 1) * chunks)
        lanes = slice(head * width, (head + 1) * width)
        d_logit = jnp.concatenate(d_b[mine], axis=0) * keep * sig_b[head] * (1.0 - sig_b[head])
        all_logits = jnp.where(lane == head, d_logit, all_logits)
        g_q, g_k, g_v = (jnp.concatenate(x[mine], axis=0) for x in (d_q, d_k, d_v))
        g_q = root * scale_q[head] * (g_q - q[head] * jnp.sum(g_q * q[head], axis=-1, keepdims=True))
        g_k = scale_k[head] * (g_k - k[head] * jnp.sum(g_k * k[head], axis=-1, keepdims=True))
        for block, grad in enumerate((g_q, g_k, g_v)):
            spot = head * 3 + block
            at = slice(block * heads_width + head * width, block * heads_width + (head + 1) * width)
            pad[spot, pl.ds(0, RIM), :] = zeros
            pad[spot, pl.ds(RIM + rows, RIM), :] = zeros
            mixed = conv_rows(ext, taps, block, lanes, rows, sames)
            sig = silu_parts(mixed)[0]
            d_mixed = grad * sig * (1.0 + mixed * (1.0 - sig))
            total = jnp.zeros((rows + RIM, width), F32)
            for j in range(TAPS):
                masked = d_mixed * sames[j]
                pad[spot, pl.ds(RIM, rows), :] = masked
                total = total + taps[block, j : j + 1, lanes] * pad[spot, pl.ds(j, rows + RIM), :]
                d_taps[block, j : j + 1, lanes] = jnp.sum(
                    masked * ext[RIM - j : RIM - j + rows, at], axis=0, keepdims=True
                )
            grad_ext[:, at] = total.astype(BF16)
            grad_rim[:, at] = total[:RIM]
            grad_tail[:, at] = total[rows:]
    grad_ext[pl.ds(RIM, rows), 3 * heads_width :] = all_logits.astype(BF16)
    grad_ext[pl.ds(0, RIM), 3 * heads_width :] = jnp.zeros((RIM, LANES), BF16)


def back_project_kernel(
    meta, grad_ext, tail, returned, wq, wk, wv, wb, xq, xk, xv, xb, *rest
):
    pieces, grad = rest[:-1], rest[-1]
    count = pieces[0].shape[0]
    chan = wq.shape[1]
    for slot in range(len(pieces)):
        here = pl.ds(slot * count, count)
        start = pl.multiple_of(meta[6 + slot], count)
        grad[here, :] = grad_ext[pl.ds(pl.multiple_of(start + RIM, RIM), count), :]
    last = pl.multiple_of(meta[6 + len(pieces) - 1] + count - RIM, RIM)
    grad[pl.ds(last, RIM), : 3 * chan] = (tail[...] + returned[...]).astype(BF16)
    own, oth = halves(meta, wq.shape[0])
    for side, weights in ((own, (wq, wk, wv, wb)), (oth, (xq, xk, xv, xb))):
        total = dot_nt(grad[:, 3 * chan : 3 * chan + weights[3].shape[1]], weights[3][...])
        for block in range(3):
            total = total + dot_nt(grad[:, block * chan : (block + 1) * chan], weights[block][...])
        total = total.astype(BF16)
        for slot, piece in enumerate(pieces):
            piece[:, side] = total[slot * count : (slot + 1) * count]


def ffn_grad_kernel(meta, low, low_sib, normed, normed_sib, wide, wide_sib, out):
    own = halves(meta, out.shape[0])[0]
    units = wide.shape[1] // 3
    lows = jnp.concatenate([low[:, own], low_sib[...]], axis=0)
    norms = jnp.concatenate([normed[:, own], normed_sib[...]], axis=0)
    for at, left in enumerate((lows, norms, norms)):
        here = slice(at * units, (at + 1) * units)
        out[:, here] = dot_tn(left, jnp.concatenate([wide[:, here], wide_sib[:, here]], axis=0)).astype(BF16)


def proj_grad_kernel(
    meta, normed, grad, normed_sib, grad_sib, grad_att, heads, grad_att_sib, heads_sib, out
):
    half, columns = out.shape[0], grad.shape[1]
    own = halves(meta, half)[0]
    out[:, :columns] = (
        dot_tn(normed[:, own], grad[...]) + dot_tn(normed_sib[...], grad_sib[...])
    ).astype(BF16)
    out[:, columns:] = (
        dot_tn(grad_att[:, own], heads[...]) + dot_tn(grad_att_sib[...], heads_sib[...])
    ).astype(BF16)


def flipped(value, axis, bit):
    return lax.ppermute(value, axis, [(i, i ^ bit) for i in range(lax.axis_size(axis))])


def shifted(value, axis, by, reach=None):
    length = lax.axis_size(axis)
    pairs = [(i, i + by) for i in range(length) if 0 <= i + by < length]
    if reach is not None:
        pairs = [pair for pair in pairs if reach(pair[0])]
    return lax.ppermute(value, axis, pairs)


def exchanged(pieces):
    return [pieces[0]] + [flipped(piece, "tp", slot) for slot, piece in enumerate(pieces) if slot]


def gathered(piece):
    return [piece] + [flipped(piece, "tp", slot) for slot in range(1, lax.axis_size("tp"))]


def summed(value, axis):
    bit = 1
    while bit < lax.axis_size(axis):
        value = value + flipped(value, axis, bit)
        bit *= 2
    return value


def contract_rows(left_side, right_side):
    return lax.dot_general(
        left_side, right_side, (((0,), (0,)), ((), ())), preferred_element_type=F32
    )


def scattered(value):
    return lax.psum_scatter(value, "ctx", scatter_dimension=0, tiled=True)


def line_kernel(meta, value, *rest, step, last):
    rights, lefts = rest[-2:]
    rows = rights.shape[0]
    place = meta[meta.shape[0] - 1]
    for out, due, came in zip((rights, lefts), (last - step + place, place - last + step), rest[:-2] or (None, None)):
        start = pl.multiple_of(jnp.clip(due, 0, last) * rows, rows)
        part = value[pl.ds(start, rows), :]
        if came is not None:
            part = (part.astype(F32) + came[...].astype(F32)).astype(BF16)
        out[...] = part


def line_step(meta, value, step, came, after=()):
    last = lax.axis_size("ctx") - 1
    part = shape(value.shape[0] // (last + 1), value.shape[1], dtype=BF16)
    right, left = call(
        functools.partial(line_kernel, step=step, last=last), [part, part], (meta, value, *came), after=after
    )
    return right, (
        shifted(right, "ctx", 1, lambda i: i <= step),
        shifted(left, "ctx", -1, lambda i: i >= last - step),
    )


def line_total(value, place, came):
    rows = value.shape[0] // lax.axis_size("ctx")
    total = lax.dynamic_slice_in_dim(value, place * rows, rows, 0).astype(F32)
    return total + came[0].astype(F32) + came[1].astype(F32)


def shards(
    tokens, seq_bounds, w_query, w_key, w_value, w_beta, conv_taps, out_gain, w_out,
    attn_gain, ffn_gain, w_gate, w_up, w_down, cotangent,
):
    rows, width = tokens.shape
    half = w_query.shape[0]
    chan = w_query.shape[1]
    heads = w_beta.shape[1]
    dim = out_gain.shape[0]
    units = w_gate.shape[1]
    slots = lax.axis_size("tp")
    count = rows // slots
    core, place, member = lax.axis_index("fsdp"), lax.axis_index("ctx"), lax.axis_index("tp")
    meta = jnp.concatenate(
        [
            seq_bounds[0],
            jnp.stack(
                [place * rows, core * half, (1 - core) * half]
                + [(member ^ slot) * count for slot in range(slots)]
                + [place]
            ).astype(jnp.int32),
        ]
    )
    attn_row, ffn_row, out_row = attn_gain[None, :], ffn_gain[None, :], out_gain[None, :]

    rim = shifted(tokens[rows - RIM :], "ctx", 1)
    x_query, x_key, x_value, x_beta = (flipped(w, "fsdp", 1) for w in (w_query, w_key, w_value, w_beta))
    tok_own = lax.dynamic_slice_in_dim(tokens, member * count, count, 0)
    cot_own = lax.dynamic_slice_in_dim(cotangent, member * count, count, 0)

    normed, proj, logits, normed_oth = call(
        project_kernel,
        [
            shape(rows + RIM, width, dtype=BF16),
            shape(rows + RIM, 3 * chan),
            shape(rows, heads),
            shape(rows + RIM, half, dtype=BF16),
        ],
        (meta, tokens, rim, attn_row, w_query, w_key, w_value, w_beta, x_query, x_key, x_value, x_beta),
        flops=2 * rows * width * 3 * chan,
        vmem=58,
    )
    later = lax.optimization_barrier((w_down, w_gate, w_up, normed_oth))
    x_out = flipped(w_out, "fsdp", 1)
    x_down, x_gate, x_up = (flipped(w, "fsdp", 1) for w in later[:3])
    normed_oth = later[3]
    tall, small = shape(heads, rows, dim), shape(heads, dim, dim, dtype=BF16)
    erase, write, scores, inverse, query_eff, step, prefix, added, query_hat, out_hat, m_total, b_total = call(
        delta_kernel,
        [shape(heads, rows, dim, dtype=BF16)] * 9 + [tall] + [small] * 2,
        (meta, proj, conv_taps, logits),
        flops=heads * 60 * rows * dim * dim,
        vmem=58,
    )

    def hop(matrix, extra, state, flip, after=()):
        return call(
            functools.partial(hop_kernel, flip=flip),
            shape(heads, dim, dim, dtype=BF16),
            (matrix, extra, state),
            flops=2 * heads * dim**3,
            scalars=False,
            after=after,
        )

    state = jnp.zeros((heads, dim, dim), BF16)
    for index in range(lax.axis_size("ctx") - 1):
        sent = b_total if index == 0 else hop(m_total, b_total, state, False)
        state = shifted(sent, "ctx", 1)

    piece_shape = shape(count, width, dtype=BF16)
    normed_sib = flipped(normed_oth, "fsdp", 1)
    heads_slot, heads_out, *pieces = call(
        attend_kernel,
        [shape(rows, chan, dtype=BF16), tall] + [piece_shape] * slots,
        (meta, query_hat, out_hat, state, out_row, w_out, x_out),
        flops=2 * rows * width * chan,
        after=(x_down, x_gate, x_up, normed_sib),
        scratch=[VMEM((rows, chan), BF16)],
    )
    grad_low, grad_act, low_oth = call(
        grad_act_kernel,
        [shape(rows, width, dtype=BF16), shape(rows, units), shape(rows, half, dtype=BF16)],
        (meta, cotangent, w_down, x_down),
        flops=2 * rows * width * units,
        after=(heads_slot,),
    )
    heads_sib, low_sib = flipped(heads_slot, "fsdp", 1), flipped(low_oth, "fsdp", 1)
    hidden, normed_two = call(
        norm_two_kernel,
        [shape(count, width), piece_shape],
        (*exchanged(pieces), tok_own, ffn_row),
        scalars=False,
    )
    maps = None
    if lax.axis_size("ctx") == 4:
        near = shifted(m_total, "ctx", -1)
        chained = call(chain_kernel, small, (m_total, near), scalars=False, after=(normed_two,))
        maps = (near, shifted(chained, "ctx", -1))
    normed_slot, two_oth, wide, *pieces = call(
        ffn_kernel,
        [
            shape(rows, width, dtype=BF16),
            shape(rows, half, dtype=BF16),
            shape(rows, 3 * units, dtype=BF16),
        ]
        + [piece_shape] * slots,
        (meta, *gathered(normed_two), w_gate, x_gate, w_up, x_up, grad_act),
        flops=8 * rows * width * units,
        after=(*(maps or ()), low_sib),
    )
    two_sib, wide_sib = flipped(two_oth, "fsdp", 1), flipped(wide, "fsdp", 1)
    received = exchanged(pieces)
    grad_hidden, grad_att, d_ffn_part = call(
        norm_two_back_kernel,
        [shape(count, width), piece_shape, shape(1, width)],
        (meta, *received, hidden, cot_own, ffn_row),
    )
    ffn_pair = call(
        ffn_grad_kernel,
        shape(half, 3 * units, dtype=BF16),
        (meta, grad_low, low_sib, normed_slot, two_sib, wide, wide_sib),
        flops=4 * rows * half * 3 * units,
    )
    ffn_sum = scattered(ffn_pair)
    down_keep, down_give = call(
        down_kernel,
        [shape(2 * count, width, dtype=BF16)] * 2,
        (meta, wide, w_down, x_down),
        flops=2 * rows * width * units,
        after=(grad_att,),
    )
    grad_o, d_chunk, d_total, d_head_part, grad_att_slot, att_oth = call(
        heads_back_kernel,
        [tall, tall, small, shape(1, dim), shape(rows, width, dtype=BF16), shape(rows, half, dtype=BF16)],
        (meta, *gathered(grad_att), w_out, x_out, heads_out, out_row, query_eff, query_hat),
        flops=2 * rows * width * chan,
        scratch=[VMEM((rows, chan), F32)],
        after=(ffn_pair, down_keep),
    )
    if maps is None:
        grad_state = jnp.zeros((heads, dim, dim), BF16)
        for index in range(lax.axis_size("ctx") - 1):
            sent = d_total if index == 0 else hop(m_total, d_total, grad_state, True)
            grad_state = shifted(sent, "ctx", -1)
        gathered_grads = (grad_state,)
    else:
        sent = d_total
        gathered_grads = tuple(shifted(sent, "ctx", -by) for by in range(1, lax.axis_size("ctx")))
    down_mine, down_other = call(
        add_half_kernel,
        [shape(count, width), piece_shape],
        (down_keep, flipped(down_give, "tp", 1)),
        scalars=False,
        after=(d_total,),
    )
    att_sib = flipped(att_oth, "fsdp", 1)

    grad_ext, grad_rim, grad_tail, d_conv_part = call(
        delta_back_kernel,
        [
            shape(rows + RIM, 3 * chan + LANES, dtype=BF16),
            shape(RIM, 3 * chan),
            shape(RIM, 3 * chan),
            shape(3, TAPS, chan),
        ],
        (
            meta, proj, conv_taps, logits,
            erase, write, scores, inverse, step, prefix, added, state, grad_o, d_chunk,
            *gathered_grads, *(maps or ()),
        ),
        flops=heads * 60 * rows * dim * dim,
        scratch=[VMEM((3 * heads, rows + 2 * RIM, dim), F32)],
        after=(att_sib, down_other),
    )
    returned = shifted(grad_rim, "ctx", -1)
    grad_sib = flipped(grad_ext, "fsdp", 1)
    proj_pair = call(
        proj_grad_kernel,
        shape(half, 4 * chan + LANES, dtype=BF16),
        (meta, normed, grad_ext, normed_sib, grad_sib, grad_att_slot, heads_slot, att_sib, heads_sib),
        flops=4 * rows * half * 4 * chan,
    )
    out_own = call(
        add_kernel,
        piece_shape,
        (down_mine, flipped(down_other, "tp", 2), hidden),
        scalars=False,
        after=(returned, proj_pair),
    )
    pieces = call(
        back_project_kernel,
        [piece_shape] * slots,
        (
            meta, grad_ext, grad_tail, returned,
            w_query, w_key, w_value, w_beta, x_query, x_key, x_value, x_beta,
        ),
        flops=2 * rows * width * 3 * chan,
        scratch=[VMEM((rows, 3 * chan + LANES), BF16)],
        after=(out_own,),
    )
    sent, came = line_step(meta, proj_pair, 0, (), after=(returned,))
    d_tok_own = call(
        norm_one_back_kernel,
        shape(count + RIM, width, dtype=BF16),
        (*exchanged(pieces), tok_own, attn_row, grad_hidden, d_ffn_part, d_head_part),
        scalars=False,
        after=(sent,),
    )
    tok_slots = gathered(d_tok_own)
    sent, came = line_step(meta, proj_pair, 1, came)
    d_tokens, gains = call(
        place_last_kernel,
        [shape(rows, width, dtype=BF16), shape(8, width)],
        (meta, *tok_slots),
        after=(ffn_sum,),
    )
    conv_rows_count = 3 * TAPS * chan // width
    bundle = summed(
        jnp.concatenate([gains, d_conv_part.reshape(conv_rows_count, width)], axis=0), "fsdp"
    )
    if lax.axis_size("ctx") == 4:
        bundle = bundle + sum(flipped(bundle, "ctx", bit) for bit in (1, 2, 3))
    else:
        bundle = summed(bundle, "ctx")
    for step in range(2, lax.axis_size("ctx") - 1):
        sent, came = line_step(meta, proj_pair, step, came, after=(bundle,))
    out_late = call(copy_kernel, piece_shape, (out_own,), scalars=False, after=(bundle,))
    out = call(place_kernel, shape(rows, width, dtype=BF16), (meta, *gathered(out_late)))
    proj_sum, ffn_sum = line_total(proj_pair, place, came), ffn_sum.astype(F32)
    return (
        out,
        d_tokens,
        proj_sum[:, :chan],
        proj_sum[:, chan : 2 * chan],
        proj_sum[:, 2 * chan : 3 * chan],
        proj_sum[:, 3 * chan : 3 * chan + heads],
        bundle[8:].reshape(3, TAPS, chan),
        bundle[2, :dim],
        proj_sum[:, 3 * chan + LANES :],
        bundle[0],
        bundle[1],
        ffn_sum[:, units : 2 * units],
        ffn_sum[:, 2 * units :],
        ffn_sum[:, :units],
    )


def solution(mesh):
    both = P(("fsdp", "ctx"), None)
    weight = P("fsdp", "tp")
    grad = P(("fsdp", "ctx"), "tp")
    in_specs = (
        both, P("fsdp", None), weight, weight, weight, weight, P(None, None, "tp"), P(), weight,
        P(), P(), weight, weight, weight, both,
    )
    out_specs = (
        both, both, grad, grad, grad, grad, P(None, None, "tp"), P(), grad, P(), P(), grad, grad, grad,
    )
    return jax.shard_map(shards, mesh=mesh, in_specs=in_specs, out_specs=out_specs, check_vma=False)
```
